512 devices in a mesh: enc: 16 (over y, core), row: 32 (over x, z).
Axes of the slice: x: 4, y: 8, z: 8, core: 2. Of those that a mesh axis runs over, the one named last changes fastest.
Arguments:
- patches: bfloat16 [131072, 1280], P(('enc', 'row'))
- norm_gain: float32 [1280], replicated, may hold values from 0.1 to 1.9
- merge_gain: float32 [1280], replicated, may hold values from 0.1 to 1.9
- qkv_weight: bfloat16 [1280, 1920], P('row')
- out_weight: bfloat16 [640, 1280], P('row'), may hold values from -0.25 to 0.25
- window_phase: int32 [16], replicated, may hold values from 1 to 63, as said below
- owner_enc: int32 [32768], P(('enc', 'row')), may hold values from 0 to 15, as said below
- owner_slot: int32 [32768], P(('enc', 'row')), may hold values from 0 to 4, as said below
- llm_grads: bfloat16 [40960, 5120], P(('enc', 'row')), may hold values from -6 to 6
Outputs:
- llm_inputs: bfloat16 [40960, 5120], P(('enc', 'row'))
- patch_grads: bfloat16 [131072, 1280], P(('enc', 'row'))
The draws below stay inside these ranges and needn't reach their ends.
Inputs may be any that keep to these rules, and one draw needn't show every extreme that they name: `window_phase`: some region has phase 1 and another has 63. `owner_enc`: the owner of a merged token lies at the same index along row as its source device. A source device sends at most 5 merged tokens to one owner, and in every index along row one owner receives exactly 5 from every source. `owner_slot`: merged tokens of one source that share an owner have distinct slots.
All inputs are finite; a program needn't handle non-finite values.
Results may differ from the reference program's by a relative error of at most 0.012.
Values may be sent and summed in bfloat16 or wider, within the bound.
A program may use at most 64 MiB of HBM per device.

```python
import math
import jax
import jax.numpy as jnp
from jax import lax

D = 1280
HEADS = 8
HEAD_DIM = 80
WIN = 64
MERGED_W = 5120
MERGED_DEV = 64
CAP = 5
SLOTS_DEV = 80
GROUP_TOK = 8192
TOKENS = 131072
N_ENC = 16
N_ROW = 32
DEVICES = 512


def route_table(key):
    column_key = jax.random.fold_in(key, 101)
    favoured = jax.random.randint(column_key, (N_ROW,), 0, N_ENC)
    source_keys = jax.random.split(key, DEVICES)
    chosen_all = favoured[jnp.arange(DEVICES) % N_ROW]

    def one_source(source_key, chosen):
        key_first, key_second, key_third = jax.random.split(source_key, 3)
        others = jax.random.permutation(key_first, (N_ENC - 1) * CAP)[:MERGED_DEV - CAP]
        other_enc = others // CAP
        other_enc = other_enc + (other_enc >= chosen).astype(jnp.int32)
        other_slot = others % CAP
        full_slot = jax.random.permutation(key_second, CAP)
        enc_list = jnp.concatenate([jnp.full((CAP,), chosen, jnp.int32), other_enc.astype(jnp.int32)])
        slot_list = jnp.concatenate([full_slot.astype(jnp.int32), other_slot.astype(jnp.int32)])
        shuffle = jax.random.permutation(key_third, MERGED_DEV)
        return (enc_list[shuffle], slot_list[shuffle])
    enc_all, slot_all = jax.vmap(one_source)(source_keys, chosen_all)
    return (enc_all.reshape(-1).astype(jnp.int32), slot_all.reshape(-1).astype(jnp.int32))


def draw_owner_enc(key, part):
    return route_table(key)[0]


def draw_owner_slot(key, part):
    return route_table(key)[1]


def draw_window_phase(key, part):
    key = jax.random.fold_in(key, 3)
    key_first, key_second = jax.random.split(key)
    values = jax.random.randint(key_first, (N_ENC,), 1, WIN)
    shuffle = jax.random.permutation(key_second, N_ENC)
    values = values.at[shuffle[0]].set(1).at[shuffle[1]].set(WIN - 1)
    return values.astype(jnp.int32)


def draw_patches(key, part):
    key = jax.random.fold_in(key, 11)
    key_base, key_rows, key_cols = jax.random.split(key, 3)
    row_scale = jnp.exp(jax.random.uniform(key_rows, (TOKENS, 1), jnp.float32, math.log(0.3), math.log(3.0)))
    col_scale = jnp.exp(jax.random.uniform(key_cols, (1, D), jnp.float32, math.log(0.3), math.log(3.0)))
    base = jax.random.normal(key_base, (TOKENS, D), jnp.float32)
    return (base * row_scale * col_scale).astype(jnp.bfloat16)


def draw_qkv_weight(key, part):
    key = jax.random.fold_in(key, 13)
    key_base = jax.random.fold_in(key, 0)
    proj_width = HEADS * HEAD_DIM
    base = jax.random.normal(key_base, (D, 3 * proj_width), jnp.float32) / math.sqrt(D)
    return base.astype(jnp.bfloat16)


def block_scale(stream_key, shape, pieces, least, largest):
    factor_of, own = 1.0, jax.random.fold_in(stream_key, 6)
    for dim, shards_of in pieces:
        heights = jnp.exp(jax.random.uniform(jax.random.fold_in(own, dim), (shards_of,), jnp.float32, least / len(pieces), largest / len(pieces)))
        factor_of = factor_of * jnp.repeat(heights, shape[dim] // shards_of).reshape([-1 if axis == dim else 1 for axis in range(len(shape))])
    return factor_of


def scatter_about(stream_key, shape, width, limit, shards=(), held_as=jnp.bfloat16):
    loudness = block_scale(stream_key, shape, shards, -0.22, 0.18) if shards else 1.0
    values = jax.random.normal(stream_key, shape, jnp.float32) * width * loudness
    return jnp.minimum(jnp.maximum(values, -limit), limit).astype(held_as)


def setup_inputs(seed: int = 0) -> dict:
    streams_of = jax.random.split(jax.random.key(seed), 10)
    patches = draw_patches(jax.random.fold_in(streams_of[9], 71), 0)
    norm_gain = jnp.clip(1.0 + 0.18 * jax.random.normal(streams_of[1], (D,), jnp.float32), 0.1, 1.9)
    merge_gain = jnp.clip(1.0 + 0.18 * jax.random.normal(streams_of[2], (D,), jnp.float32), 0.1, 1.9)
    qkv_weight = draw_qkv_weight(jax.random.fold_in(streams_of[9], 71), 0)
    out_weight = scatter_about(streams_of[4], (HEADS * HEAD_DIM, D), (HEADS * HEAD_DIM) ** -0.5, 0.25, ((0, 32),))
    window_phase = draw_window_phase(jax.random.fold_in(streams_of[9], 71), 0)
    owner_enc = draw_owner_enc(jax.random.fold_in(streams_of[9], 71), 0)
    owner_slot = draw_owner_slot(jax.random.fold_in(streams_of[9], 71), 0)
    llm_grads = scatter_about(streams_of[8], (DEVICES * SLOTS_DEV, MERGED_W), 1.0, 6.0, ((0, 512),))
    return {"patches": patches, "norm_gain": norm_gain, "merge_gain": merge_gain, "qkv_weight": qkv_weight, "out_weight": out_weight, "window_phase": window_phase, "owner_enc": owner_enc, "owner_slot": owner_slot, "llm_grads": llm_grads}


EPS = 1e-06

def rms_norm(values, gain_vec):
    wide = values.astype(jnp.float32)
    inv_rms = lax.rsqrt(lax.optimization_barrier(jnp.mean(wide * wide, -1, keepdims=True)) + EPS)
    return (wide * inv_rms * gain_vec).astype(jnp.bfloat16)

def rms_back(values, gain_vec, upstream_in):
    wide = values.astype(jnp.float32)
    inv_rms = lax.rsqrt(lax.optimization_barrier(jnp.mean(wide * wide, -1, keepdims=True)) + EPS)
    upstream = upstream_in.astype(jnp.float32) * gain_vec
    inner = lax.optimization_barrier(jnp.mean(upstream * wide, -1, keepdims=True))
    return inv_rms * upstream - wide * (inv_rms * inv_rms * inv_rms) * inner

def align_rows(values, grid_phase, length):
    padding = jnp.zeros((WIN,) + values.shape[1:], values.dtype)
    padded = jnp.concatenate([padding, values, padding], 0)
    return lax.dynamic_slice_in_dim(padded, grid_phase, length + WIN, 0)

def key_mask(grid_phase, first_pos, group_total, count):
    positions = first_pos + jnp.arange(count, dtype=jnp.int32) + grid_phase - WIN
    valid = jnp.logical_and(positions >= 0, positions < group_total)
    return valid.reshape(count // WIN, WIN)

def window_forward(q_al, k_al, v_al, key_valid):
    windows = q_al.shape[0] // WIN
    shape_four = (windows, WIN, HEADS, HEAD_DIM)
    q_four = q_al.reshape(shape_four).astype(jnp.float32)
    k_four = k_al.reshape(shape_four).astype(jnp.float32)
    v_four = v_al.reshape(shape_four).astype(jnp.float32)
    scores = jnp.einsum('wqhd,wkhd->whqk', q_four, k_four) * HEAD_DIM ** (-0.5)
    scores = jnp.where(key_valid[:, None, None, :], scores, -1e+30)
    highest = lax.optimization_barrier(jnp.max(scores, -1, keepdims=True))
    expo = jnp.exp(scores - highest)
    soft_w = expo / lax.optimization_barrier(jnp.sum(expo, -1, keepdims=True))
    soft_b = soft_w.astype(jnp.bfloat16)
    mixed = jnp.einsum('whqk,wkhd->wqhd', soft_b.astype(jnp.float32), v_four)
    return (mixed.astype(jnp.bfloat16).reshape(windows * WIN, HEADS * HEAD_DIM), soft_w, soft_b)

def window_backward(q_al, k_al, v_al, soft_w, soft_b, grad_al):
    windows = q_al.shape[0] // WIN
    shape_four = (windows, WIN, HEADS, HEAD_DIM)
    q_four = q_al.reshape(shape_four).astype(jnp.float32)
    k_four = k_al.reshape(shape_four).astype(jnp.float32)
    v_four = v_al.reshape(shape_four).astype(jnp.float32)
    grad_four = grad_al.reshape(shape_four).astype(jnp.float32)
    prob_grad = jnp.einsum('wqhd,wkhd->whqk', grad_four, v_four)
    centred = prob_grad - lax.optimization_barrier(jnp.sum(soft_w * prob_grad, -1, keepdims=True))
    score_grad = (soft_w * centred * HEAD_DIM ** (-0.5)).astype(jnp.bfloat16).astype(jnp.float32)
    dq_four = jnp.einsum('whqk,wkhd->wqhd', score_grad, k_four)
    dk_four = jnp.einsum('whqk,wqhd->wkhd', score_grad, q_four)
    dv_four = jnp.einsum('whqk,wqhd->wkhd', soft_b.astype(jnp.float32), grad_four)
    flat = (windows * WIN, HEADS * HEAD_DIM)
    return (dq_four.reshape(flat), dk_four.reshape(flat), dv_four.reshape(flat))

def reference(patches, norm_gain, merge_gain, qkv_weight, out_weight, window_phase, owner_enc, owner_slot, llm_grads):
    proj_width = HEADS * HEAD_DIM
    region_rows = patches.reshape(N_ENC, GROUP_TOK, D)
    phases = window_phase.astype(jnp.int32)

    def attention_parts(region, grid_phase):
        hidden_in = rms_norm(region, norm_gain)
        qkv = jnp.dot(hidden_in, qkv_weight, preferred_element_type=jnp.float32).astype(jnp.bfloat16)
        q_al = align_rows(qkv[:, :proj_width], grid_phase, GROUP_TOK)
        k_al = align_rows(qkv[:, proj_width:2 * proj_width], grid_phase, GROUP_TOK)
        v_al = align_rows(qkv[:, 2 * proj_width:], grid_phase, GROUP_TOK)
        valid = key_mask(grid_phase, jnp.int32(0), GROUP_TOK, GROUP_TOK + WIN)
        return (q_al, k_al, v_al, valid)

    def region_forward(pair):
        region, grid_phase = pair
        q_al, k_al, v_al, valid = attention_parts(region, grid_phase)
        mixed_al, soft_w, soft_b = window_forward(q_al, k_al, v_al, valid)
        attended = lax.dynamic_slice_in_dim(mixed_al, WIN - grid_phase, GROUP_TOK, 0)
        branch = jnp.dot(attended, out_weight, preferred_element_type=jnp.float32)
        return (region.astype(jnp.float32) + branch).astype(jnp.bfloat16)
    resid = lax.map(region_forward, (region_rows, phases))
    normed = rms_norm(resid, merge_gain)
    merged = normed.reshape(TOKENS // 4, MERGED_W)
    source = jnp.arange(TOKENS // 4, dtype=jnp.int32) // MERGED_DEV
    owner = owner_enc.astype(jnp.int32) * N_ROW + source % N_ROW
    places = owner * SLOTS_DEV + source // N_ROW * CAP + owner_slot.astype(jnp.int32)
    llm_inputs = jnp.zeros((DEVICES * SLOTS_DEV, MERGED_W), jnp.bfloat16).at[places].set(merged)
    normed_grad = llm_grads[places].reshape(N_ENC, GROUP_TOK, D)

    def region_backward(group_data):
        region, resid_part, grad_part, grid_phase = group_data
        q_al, k_al, v_al, valid = attention_parts(region, grid_phase)
        mixed_al, soft_w, soft_b = window_forward(q_al, k_al, v_al, valid)
        resid_grad = rms_back(resid_part, merge_gain, grad_part)
        attended_grad = lax.dot_general(resid_grad.astype(jnp.bfloat16), out_weight, (((1,), (1,)), ((), ())), preferred_element_type=jnp.float32).astype(jnp.bfloat16)
        grad_al = align_rows(attended_grad, grid_phase, GROUP_TOK)
        dq_al, dk_al, dv_al = window_backward(q_al, k_al, v_al, soft_w, soft_b, grad_al)
        start = WIN - grid_phase
        qkv_grad = jnp.concatenate([lax.dynamic_slice_in_dim(dq_al, start, GROUP_TOK, 0), lax.dynamic_slice_in_dim(dk_al, start, GROUP_TOK, 0), lax.dynamic_slice_in_dim(dv_al, start, GROUP_TOK, 0)], 1).astype(jnp.bfloat16)
        hidden_grad = lax.dot_general(qkv_grad, qkv_weight, (((1,), (1,)), ((), ())), preferred_element_type=jnp.float32)
        return (resid_grad + rms_back(region, norm_gain, hidden_grad)).astype(jnp.bfloat16)
    patch_grads = lax.map(region_backward, (region_rows, resid, normed_grad, phases))
    return (llm_inputs, patch_grads.reshape(TOKENS, D))
```

```python
import functools
import heapq

import jax
import jax.numpy as jnp
from jax import lax
from jax.experimental import pallas as pl
from jax.experimental.pallas import tpu as pltpu
from jax.sharding import PartitionSpec as P

HEADS = 8
HEAD_DIM = 80
WIN = 64
EPS = 1e-06

ROWS = 256
AL = ROWS + WIN
D = 1280
PROJ = HEADS * HEAD_DIM
CAP = 5
SHARD = 40
OUT_SHARD = 20
FLOWS = (512, 768)
SPLIT = 1024
SLAB = 16
SLAB_W = 1664
PIECES = ((0, 384), (384, 384), (768, 256), (1024, 256))
BLOCKS = ((0, 128, 0), (128, 128, 128), (256, 64, 192))
SLOT = 0.5

F32 = jnp.float32
BF16 = jnp.bfloat16
MESH = pl.DeviceIdType.MESH


def dot(a, b):
    return lax.dot_general(a, b, (((1,), (0,)), ((), ())), preferred_element_type=F32)


def dot_nt(a, b):
    return lax.dot_general(a, b, (((1,), (1,)), ((), ())), preferred_element_type=F32)


def dot_tn(a, b):
    return lax.dot_general(a, b, (((0,), (0,)), ((), ())), preferred_element_type=F32)


def iota(shape, dim):
    return lax.broadcasted_iota(jnp.int32, shape, dim)


def one_hot(cond):
    return jnp.where(cond, 1.0, 0.0).astype(BF16)


def ring_plan(n_x, n_z):
    dims = ((n_x, n_z), (n_z, n_x))
    tile_time = 0.16
    hop_time = 1.0

    def onward(port, da, db):
        size_a, size_b = dims[port]
        out = []
        if db == 0:
            for sign, reach in ((1, size_a // 2), (-1, size_a // 2 - 1)):
                gone = abs(da) if da * sign <= 0 else reach
                if gone < reach:
                    out.append((0, sign, reach - gone + size_b / 2))
        plus = size_b // 2 if da % 2 == 0 else size_b // 2 - 1
        for sign, reach in ((1, plus), (-1, size_b - 1 - plus)):
            gone = abs(db) if db * sign <= 0 else reach
            if gone < reach:
                out.append((1, sign, reach - gone))
        return out

    events = [[] for _ in FLOWS]
    free = {}
    waiting = {}
    count = 100
    agenda = [(0.0, f, f, (0, 0)) for f in range(len(FLOWS))]
    while agenda:
        now, _, flow, what = heapq.heappop(agenda)
        if len(what) == 2:
            port = flow
            if what != (0, 0):
                events[flow].append((now, count, "wait", what, None))
            for axis, sign, left in onward(port, *what):
                link = ("x" if axis == port else "z", sign)
                count += 2
                line = waiting.setdefault(link, [])
                heapq.heappush(line, (-left, count, flow, what, axis, sign, now))
                wake = max(now, free.get(link, 0.0))
                heapq.heappush(agenda, (wake, count + 10**6, flow, (link,)))
            continue
        link = what[0]
        if free.get(link, 0.0) > now + 1e-9 or not waiting[link]:
            continue
        _, _, flow, (da, db), axis, sign, ready = heapq.heappop(waiting[link])
        count += 2
        issue = max(ready, now - 1.0)
        hop = (sign, 0) if axis == 0 else (0, sign)
        events[flow].append((issue, count, "send", (da, db), hop))
        end = now + FLOWS[flow] / 64 * tile_time
        free[link] = end
        there = (da - sign, db) if axis == 0 else (da, db - sign)
        heapq.heappush(agenda, (end + hop_time, count, flow, there))
        heapq.heappush(agenda, (end, count + 10**6, flow, (link,)))
    return [sorted(flow_events) for flow_events in events]


def kernel(
    n_enc,
    n_x,
    n_z,
    phase_ref,
    patches_hbm,
    norm_gain_ref,
    merge_gain_ref,
    qkv_shard_ref,
    out_shard_ref,
    owner_enc_ref,
    owner_slot_ref,
    grads_hbm,
    recv2,
    pg_ref,
    patches_ref,
    grads_ref,
    wg0,
    wg1,
    w_ref,
    wo_ref,
    wo_wide,
    turn_ref,
    own_ref,
    rim_ref,
    pal_ref,
    hid_ref,
    qkv_ref,
    prob_ref,
    mask_ref,
    acc_ref,
    att_ref,
    resid_ref,
    normed_ref,
    ng_ref,
    ng_rim_ref,
    rg_ref,
    rgb_ref,
    ag_ref,
    dqkv_ref,
    dqkvb_ref,
    hg_ref,
    pal_grad_ref,
    grad_rim_ref,
    sel_ref,
    selt_ref,
    target_ref,
    slot_wide,
    slab_wide,
    send1,
    recv1,
    send2,
    relay1,
    relay2,
    w_send,
    w_recv,
    other_recv,
    slab_send,
    slab_recv,
    rim_send,
    rim_recv,
    relay_send,
    relay_recv,
    forward_send,
    own_sem,
    fetch_sem,
):
    n_row = n_x * n_z
    n_y = n_enc // 2
    n_slot = n_enc * CAP
    n_slab_rows = n_enc * SLAB
    enc = lax.axis_index("enc")
    row = lax.axis_index("row")
    core = lax.rem(enc, 2)
    y = enc // 2
    sibling = enc + 1 - 2 * core
    x = row // n_z
    z = lax.rem(row, n_z)
    left = lax.rem(row + n_row - 1, n_row)
    right = lax.rem(row + 1, n_row)
    phase = phase_ref[enc]
    edge = WIN - phase

    xs = [lax.rem(x + d, n_x) * n_z for d in range(n_x)]
    zs = [lax.rem(z + d, n_z) for d in range(n_z)]
    ys = [lax.rem(y + d, n_y) for d in range(n_y)]

    def xz(dx, dz):
        return xs[dx % n_x] + zs[dz % n_z]

    def chip(o):
        return ys[o % n_y]

    def cols(i, width):
        return pl.ds(pl.multiple_of(i * width, width), width)

    fetch_patches = pltpu.make_async_copy(patches_hbm, patches_ref, fetch_sem.at[0])
    fetch_grads = pltpu.make_async_copy(grads_hbm, grads_ref, fetch_sem.at[1])
    fetch_patches.start()
    fetch_grads.start()

    barrier = pltpu.get_barrier_semaphore()
    peers = [(enc, xz(1, 0)), (enc, xz(-1, 0)), (enc, xz(0, 1)), (enc, xz(0, -1))]
    peers += [(enc, left), (enc, right)]
    for peer in peers:
        pl.semaphore_signal(barrier, inc=1, device_id=peer, device_id_type=MESH)

    @pl.loop(1, n_enc)
    def _(d):
        pl.semaphore_signal(
            barrier, inc=1, device_id=(lax.rem(enc + d, n_enc), row), device_id_type=MESH
        )

    q_wide = qkv_shard_ref[...].astype(F32)
    odd_z = lax.rem(z, 2)
    odd = odd_z
    m = iota((SHARD, 1), 0)
    from_left = jnp.where(m < 16, m + 4 * odd, -1)
    from_left = jnp.where((m >= 32) & (m < 36), m - 16 - 64 * odd, from_left)
    from_left = jnp.where(m >= 36, m - 36 - 64 * (1 - odd), from_left)
    from_right = jnp.where((m >= 16) & (m < 32), m - 16 + 4 * odd, -1)
    from_right = jnp.where((m >= 32) & (m < 36), m - 32 - 64 * (1 - odd), from_right)
    from_right = jnp.where(m >= 36, m - 20 - 64 * odd, from_right)
    source = iota((SHARD, OUT_SHARD), 1)
    out40 = dot(one_hot(source == from_left), out_shard_ref[:, :PROJ]) + dot(
        one_hot(source == from_right), out_shard_ref[:, PROJ:]
    )

    def stacked(*parts):
        return jnp.concatenate(parts, 0).astype(BF16)

    wg0[row] = stacked(q_wide[:, :512], q_wide[:, 512:SPLIT])
    wg1[row] = stacked(q_wide[:, SPLIT:1792], jnp.concatenate([q_wide[:, 1792:], out40], 1))

    pl.semaphore_wait(barrier, len(peers) + n_enc - 1)

    plans = ring_plan(n_x, n_z)
    bufs = (wg0, wg1)

    def place(port, da, db):
        return xz(da, db) if port == 0 else xz(db, da)

    def block_wait(port, block):
        buf, r = bufs[port], place(port, *block)
        pltpu.make_async_copy(buf.at[r], buf.at[r], w_recv.at[r]).wait()

    def block_send(port, block, hop):
        buf, r = bufs[port], place(port, *block)
        pltpu.make_async_remote_copy(
            src_ref=buf.at[r],
            dst_ref=buf.at[r],
            send_sem=w_send.at[0],
            recv_sem=w_recv.at[r],
            device_id=(enc, place(port, *hop)),
            device_id_type=MESH,
        ).start()

    def hand_over(ref, send_sem, recv_sem):
        pltpu.make_async_remote_copy(
            src_ref=ref,
            dst_ref=ref,
            send_sem=send_sem,
            recv_sem=recv_sem,
            device_id=(sibling, row),
            device_id_type=MESH,
        ).start()

    def pack_pair(port, j):
        rows = pl.ds(pl.multiple_of(j * 2 * SHARD, 2 * SHARD), 2 * SHARD)
        out_rows = pl.ds(pl.multiple_of(j * 2 * OUT_SHARD, 8), 2 * OUT_SHARD)

        def halves(top):
            return [bufs[port][2 * j + k, top : top + SHARD, :].astype(F32) for k in range(2)]

        if port == 0:
            w_ref[rows, :512] = stacked(*halves(0))
            w_ref[rows, 512:SPLIT] = stacked(*halves(SHARD))
            hand_over(w_ref.at[rows, pl.ds(0, SPLIT)], w_send.at[1], other_recv.at[0])
            return
        w_ref[rows, SPLIT:1792] = stacked(*halves(0))
        even, odd = halves(SHARD)
        w_ref[rows, 1792:] = stacked(even[:, :128], odd[:, :128])
        hand_over(w_ref.at[rows, pl.ds(SPLIT, 3 * PROJ - SPLIT)], w_send.at[1], other_recv.at[0])
        even, odd = even[:, 128:], odd[:, 128:]
        upper = iota((8, 1), 0) < 4
        middle = jnp.where(upper, even[32:], odd[32:])
        wo_wide[out_rows, :PROJ] = jnp.concatenate([even[:16], middle, odd[:16]], 0)
        middle = pltpu.roll(jnp.where(upper, odd[32:], even[32:]), 4, 0)
        wo_wide[out_rows, PROJ:] = jnp.concatenate([even[16:32], middle, odd[16:32]], 0)
        hand_over(wo_wide.at[out_rows], w_send.at[2], other_recv.at[1])

    def rows_wait(ref, sem):
        pltpu.make_async_copy(ref, ref, sem).wait()

    def port_rows(port):
        return w_ref.at[:, pl.ds(0, SPLIT) if port == 0 else pl.ds(SPLIT, 3 * PROJ - SPLIT)]

    def slot_of(event):
        return int(event[0] / SLOT)

    n_slots = max(slot_of(plan[-1]) for plan in plans) + 1

    def pairs_after(port):
        arrival = {(0, 0): 0}
        for event in plans[port]:
            if event[2] == "wait":
                da, db = event[3]
                dx, dz = (da, db) if port == 0 else (db, da)
                arrival[dx % n_x, dz % n_z] = slot_of(event)
        found = []
        for m in range(1, n_z // 2 + 1):
            even, odd = (m - 1, -m) if m % 2 else (-m, m - 1)
            for dx in range(n_x):
                last = max(
                    arrival[dx, (start + k) % n_z] for start in (even, odd) for k in range(2)
                )
                found.append((last, dx, even, odd))
        return found

    def run_slot(port, slot):
        for event in plans[port]:
            if slot_of(event) == slot:
                _, _, kind, block, hop = event
                if kind == "wait":
                    block_wait(port, block)
                else:
                    block_send(port, block, hop)
        for last, dx, even, odd in pairs_after(port):
            if last == slot:
                first = xz(dx, even) + (xz(dx, odd) - xz(dx, even)) * odd_z
                pack_pair(port, first // 2)

    def weights_slot(slot):
        for port in range(2):
            if any(slot_of(event) == slot for event in plans[port]):

                @pl.when(core == port)
                def _():
                    run_slot(port, slot)

    def weights_wait():
        for port in range(2):

            @pl.when(core != port)
            def _():
                rows_wait(port_rows(port), other_recv.at[0])
                if port == 1:
                    rows_wait(wo_wide, other_recv.at[1])

    def weights_drain():
        blocks = pl.ds(0, n_row - 1)
        for port in range(2):

            @pl.when(core == port)
            def _():
                rows_wait(bufs[port].at[blocks], w_send.at[0])
                rows_wait(port_rows(port), w_send.at[1])
                if port == 1:
                    rows_wait(wo_wide, w_send.at[2])

    def rim_copy(index, src, dst, target):
        return pltpu.make_async_remote_copy(
            src_ref=src,
            dst_ref=dst,
            send_sem=rim_send.at[index],
            recv_sem=rim_recv.at[index],
            device_id=(enc, target),
            device_id_type=MESH,
        )

    top = pl.ds(0, WIN)
    rims = (
        rim_copy(0, own_ref.at[top], rim_ref.at[0], right),
        rim_copy(1, own_ref.at[top], rim_ref.at[1], left),
    )
    ng_rim = rim_copy(2, ng_ref.at[top], ng_rim_ref, right)
    grad_rim = rim_copy(3, pal_grad_ref.at[top], grad_rim_ref, left)

    def slab(ref, e):
        return ref.at[pl.ds(pl.multiple_of(SLAB * e, SLAB), SLAB)]

    def exchange_copy(index, send, recv, peer):
        return pltpu.make_async_remote_copy(
            src_ref=slab(send, peer),
            dst_ref=slab(recv, enc),
            send_sem=slab_send.at[index],
            recv_sem=slab_recv.at[index],
            device_id=(peer, row),
            device_id_type=MESH,
        )

    def near_peers():
        for o in range(n_y // 2 - 1, 0, -1):
            ahead, behind = chip(o), chip(-o)
            for side in (0, 1):
                turned = ahead + (behind - ahead) * (core if side == 0 else 1 - core)
                for k in range(2):
                    yield 2 * turned + k
        yield sibling

    next_chip = chip(1) + (chip(-1) - chip(1)) * core
    last_chip = chip(-1) + (chip(1) - chip(-1)) * core
    far_chip = chip(n_y // 2 - 1) + (chip(n_y // 2 + 1) - chip(n_y // 2 - 1)) * core

    def relay_copy(index, send):
        pair = pl.ds(pl.multiple_of(2 * SLAB * chip(n_y // 2), 2 * SLAB), 2 * SLAB)
        return pltpu.make_async_remote_copy(
            src_ref=send.at[pair],
            dst_ref=(relay1, relay2)[index],
            send_sem=relay_send.at[index],
            recv_sem=relay_recv.at[index],
            device_id=(2 * next_chip + core, row),
            device_id_type=MESH,
        )

    def forward_copy(index, recv, k):
        origin = 2 * last_chip + core
        return pltpu.make_async_remote_copy(
            src_ref=(relay1, relay2)[index].at[pl.ds(SLAB * k, SLAB)],
            dst_ref=slab(recv, origin),
            send_sem=forward_send.at[index],
            recv_sem=slab_recv.at[index],
            device_id=(2 * far_chip + k, row),
            device_id_type=MESH,
        )

    def own_copy(index, send, recv):
        return pltpu.make_async_copy(slab(send, enc), slab(recv, enc), own_sem.at[index])

    def exchange_start(index, send, recv):
        relay_copy(index, send).start()
        for peer in near_peers():
            exchange_copy(index, send, recv, peer).start()
        own_copy(index, send, recv).start()

    def exchange_forward(index, recv):
        relay_copy(index, send1).wait_recv()
        for k in range(2):
            forward_copy(index, recv, k).start()

    def exchange_wait(index, send, recv):
        own_copy(index, send, recv).wait()
        rows_wait(recv.at[pl.ds(0, (n_enc - 1) * SLAB)], slab_recv.at[index])

    def exchange_drain(index, send):
        relay_copy(index, send).wait_send()
        rows_wait(send.at[pl.ds(0, (n_enc - 3) * SLAB)], slab_send.at[index])
        rows_wait((relay1, relay2)[index], forward_send.at[index])

    def rotate():
        fetch_patches.wait()
        turn = iota((ROWS, ROWS), 1) == ((iota((ROWS, ROWS), 0) - edge) & (ROWS - 1))
        turn_ref[...] = one_hot(turn)
        for c in range(0, D, 256):
            part = dot(turn_ref[...], patches_ref[:, c : c + 256])
            own_ref[:, c : c + 256] = part.astype(BF16)
        for copy in rims:
            copy.start()

    n_tile = D // 128

    def grads_wide(q0, q1):
        if q0 == 0:
            fetch_grads.wait()
        for t in range(q0 * n_tile, q1 * n_tile):
            slot_wide[t] = grads_ref[:, 128 * t : 128 * t + 128].astype(F32)

    def grads_move(q):
        for t in range(n_tile):
            at = q * n_tile + t
            for slot in range(4):
                part = slot_wide[at, pl.ds(slot, n_enc, stride=CAP), :]
                slab_wide[t, pl.ds(4 * slot + q, n_enc, stride=SLAB), :] = part
        for p, (off, width) in enumerate(PIECES):
            for t in range(3):
                if t < width // 128:
                    at = (q * D + off) // 128 + t
                    part = slot_wide[at, pl.ds(4, n_enc, stride=CAP), :]
                else:
                    part = jnp.zeros((n_enc, 128), F32)
                slab_wide[n_tile + t, pl.ds(4 * q + p, n_enc, stride=SLAB), :] = part

    def grads_pack(first, last):
        for t in range(first, last):
            send1[:, 128 * t : 128 * t + 128] = slab_wide[t].astype(BF16)
        if last == SLAB_W // 128:
            exchange_start(0, send1, recv1)

    n_tok = ROWS // 4

    def targets(code, patch):
        slot, base = code & 7, (code >> 3) * 16
        quarter = patch & 3
        target_a = jnp.where(slot < 4, base + slot * 4 + quarter, -1)
        target_b = jnp.where(slot == 4, base + quarter * 4, -8)
        return target_a, target_b

    def selector_targets():
        code_row = owner_enc_ref[...] * 8 + owner_slot_ref[...]
        square = iota((n_tok, n_tok), 0) == iota((n_tok, n_tok), 1)
        code_col = jnp.sum(jnp.where(square, code_row, 0), 1, keepdims=True)
        patch = (iota((1, ROWS), 1) - edge) & (ROWS - 1)
        tok = iota((n_tok, ROWS), 0) == (patch >> 2)
        code = jnp.sum(jnp.where(tok, code_col, 0), 0, keepdims=True)
        target_ref[0:1, :], target_ref[1:2, :] = targets(code, patch)

    def selector(p):
        bucket = iota((n_slab_rows, ROWS), 0)
        target = target_ref[0:1, :] if p == 0 else target_ref[1:2, :] + (p - 1)
        sel_ref[p] = one_hot(bucket == target)

    def selectors_back():
        code_row = owner_enc_ref[...] * 8 + owner_slot_ref[...]
        patch = (iota((ROWS, 1), 0) - edge) & (ROWS - 1)
        tok = iota((ROWS, n_tok), 1) == (patch >> 2)
        code = jnp.sum(jnp.where(tok, code_row, 0), 1, keepdims=True)
        target_a, target_b = targets(code, patch)
        bucket = iota((ROWS, n_slab_rows), 1)
        selt_ref[0] = one_hot(bucket == target_a)
        for p in range(4):
            selt_ref[1 + p] = one_hot(bucket == target_b + p)

    def piece(body, *args):
        return lambda: body(*args)

    def masks(r0, count, k0):
        i = iota((count, 128), 0) + r0
        j = iota((count, 128), 1) + k0
        first = jnp.where(row == 0, 0, -1)
        last = jnp.where(row == n_row - 1, ROWS // WIN, -1)
        ends = ((i >> 6) == first) | ((i >> 6) == last)
        i_low = jnp.where((i & (WIN - 1)) < edge, 1, 0)
        j_low = jnp.where((j & (WIN - 1)) < edge, 1, 0)
        apart = jnp.where(ends, i_low ^ j_low, 0)
        same = ((i >> 6) == (j >> 6)) & (apart == 0)
        mask_ref[r0 : r0 + count, :] = jnp.where(same, 1.0, 0.0)

    def zeros():
        acc_ref[...] = jnp.zeros_like(acc_ref)

    below = iota((WIN, 1), 0) < edge

    def rims_in():
        for copy in rims:
            copy.wait()
        pal_ref[:WIN, :] = jnp.where(below, rim_ref[0], own_ref[:WIN, :])
        pal_ref[WIN:ROWS, :] = own_ref[WIN:, :]
        pal_ref[ROWS:, :] = jnp.where(below, own_ref[:WIN, :], rim_ref[1])

    def rms_norm(src, dst, gain_ref, rows):
        wide = src[rows, :].astype(F32)
        inv = lax.rsqrt(jnp.mean(wide * wide, -1, keepdims=True) + EPS)
        dst[rows, :] = (wide * inv * gain_ref[...].reshape(1, D)).astype(BF16)

    def rms_back(wide, gain_ref, upstream_in):
        inv = lax.rsqrt(jnp.mean(wide * wide, -1, keepdims=True) + EPS)
        upstream = upstream_in * gain_ref[...].reshape(1, D)
        inner = jnp.mean(upstream * wide, -1, keepdims=True)
        return inv * upstream - wide * (inv * inv * inv) * inner

    def piece(body, *args):
        return lambda: body(*args)

    def project(c0, c1):
        for c in range(c0, c1, 256):
            w = min(256, c1 - c)
            part = dot(hid_ref[...], w_ref[:, c : c + w])
            qkv_ref[:, c : c + w] = part.astype(BF16)

    scale = HEAD_DIM ** (-0.5)
    pairs = range(HEADS // 2)

    def window(t, base=0):
        return slice(base + 128 * t, base + 128 * t + 256)

    def two_heads(t, value):
        lane = iota((1, 256), 1) - 32 * t
        zero = jnp.zeros_like(value)
        first = jnp.where((lane >= 0) & (lane < HEAD_DIM), value, zero)
        second = jnp.where((lane >= HEAD_DIM) & (lane < 2 * HEAD_DIM), value, zero)
        return jnp.concatenate([first, second], 0)

    def attend(t):
        for r0, count, k0 in BLOCKS:
            rows, keys = slice(r0, r0 + count), slice(k0, k0 + 128)
            scores = dot_nt(qkv_ref[rows, window(t)], two_heads(t, qkv_ref[keys, window(t, PROJ)]))
            seen = mask_ref[rows, :] > 0.5
            both = []
            for g in range(2):
                s = jnp.where(seen, scores[:, 128 * g : 128 * g + 128] * scale, -1e30)
                e = jnp.exp(s - jnp.max(s, -1, keepdims=True))
                p = e / jnp.sum(e, -1, keepdims=True)
                if r0 < ROWS:
                    prob_ref[2 * t + g, rows, :] = p
                both.append(p.astype(BF16))
            values = two_heads(t, qkv_ref[keys, window(t, 2 * PROJ)])
            acc_ref[rows, window(t)] += dot(jnp.concatenate(both, 1), values)

    work = [piece(grads_wide, 0, 2), piece(grads_wide, 2, 4)]
    work += [piece(grads_move, q) for q in range(4)]
    work += [piece(grads_pack, 0, SLAB_W // 128)]
    work += [piece(masks, *block) for block in BLOCKS]
    work += [rims_in, selector_targets]
    for k in range(5):
        rows = slice(k * WIN, (k + 1) * WIN)
        work += [piece(selector, k), piece(rms_norm, pal_ref, hid_ref, norm_gain_ref, rows)]
    work += [zeros]
    for slot in range(n_slots):
        weights_slot(slot)
        if slot == 0:
            rotate()
        elif work:
            work.pop(0)()
        if slot == 20:
            exchange_forward(0, recv1)
    assert not work
    weights_wait()
    project(0, 3 * PROJ)
    for t in pairs:
        attend(t)

    att_ref[...] = acc_ref[...].astype(BF16)

    @pl.loop(0, D // 256)
    def _(i):
        c = cols(i, 256)
        wo_ref[:, c] = wo_wide[:, c].astype(BF16)
        branch = dot(att_ref[...], wo_ref[:, c])
        resid_ref[:, c] = (pal_ref[:, c].astype(F32) + branch).astype(BF16)

    @pl.loop(0, AL // WIN)
    def _(i):
        rows = pl.ds(pl.multiple_of(i * WIN, WIN), WIN)
        rms_norm(resid_ref, normed_ref, merge_gain_ref, rows)

    normed_ref[:WIN, :] = jnp.where(below, normed_ref[ROWS:, :], normed_ref[:WIN, :])

    for c in range(0, D, 256):
        send2[:, c : c + 256] = dot(sel_ref[0], normed_ref[:ROWS, c : c + 256]).astype(BF16)
    head_part = jnp.zeros((n_slab_rows, 256), F32)
    tail_part = jnp.zeros((n_slab_rows, 128), F32)
    for p, (off, width) in enumerate(PIECES):
        head_part += dot(sel_ref[1 + p], normed_ref[:ROWS, off : off + 256])
        if width > 256:
            tail_part += dot(sel_ref[1 + p], normed_ref[:ROWS, off + 256 : off + width])
    send2[:, D : D + 256] = head_part.astype(BF16)
    send2[:, D + 256 :] = tail_part.astype(BF16)
    exchange_start(1, send2, recv2)

    selectors_back()
    dqkv_ref[...] = jnp.zeros_like(dqkv_ref)
    exchange_wait(0, send1, recv1)

    def gradients(rows):
        for p, (off, width) in enumerate(PIECES):
            for c in range(0, width, 256):
                w = min(256, width - c)
                part = dot(selt_ref[0, rows], recv1[:, off + c : off + c + w])
                part += dot(selt_ref[1 + p, rows], recv1[:, D + c : D + c + w])
                ng_ref[rows, off + c : off + c + w] = part.astype(BF16)

    gradients(slice(0, WIN))
    ng_rim.start()
    gradients(slice(WIN, ROWS))

    def merge_back(rows, grad_in):
        grad = rms_back(resid_ref[rows, :].astype(F32), merge_gain_ref, grad_in.astype(F32))
        rg_ref[rows, :] = grad
        rgb_ref[rows, :] = grad.astype(BF16)

    @pl.loop(1, ROWS // WIN)
    def _(i):
        rows = pl.ds(pl.multiple_of(i * WIN, WIN), WIN)
        merge_back(rows, ng_ref[rows, :])

    ng_rim.wait()
    merge_back(slice(0, WIN), jnp.where(below, ng_rim_ref[...], ng_ref[:WIN, :]))

    exchange_forward(1, recv2)

    for c0, c1 in ((0, 256), (256, 512), (512, 640)):
        ag_ref[:, c0:c1] = dot_nt(rgb_ref[...], wo_ref[c0:c1, :]).astype(BF16)

    for t in pairs:
        for r0 in (0, 128):
            rows = slice(r0, r0 + 128)
            grad = ag_ref[rows, window(t)]
            values = two_heads(t, qkv_ref[rows, window(t, 2 * PROJ)])
            keys = two_heads(t, qkv_ref[rows, window(t, PROJ)])
            dp = dot_nt(grad, values)
            probs, score_grads = [], []
            for g in range(2):
                p = prob_ref[2 * t + g, rows, :]
                dp_g = dp[:, 128 * g : 128 * g + 128]
                centred = dp_g - jnp.sum(p * dp_g, -1, keepdims=True)
                score_grads.append((p * centred * scale).astype(BF16))
                probs.append(p.astype(BF16))
            dq = dot(jnp.concatenate(score_grads, 1), keys)
            queries = two_heads(t, qkv_ref[rows, window(t)])
            dk = dot_tn(jnp.concatenate(score_grads, 0), queries)
            dv = dot_tn(jnp.concatenate(probs, 0), two_heads(t, grad))
            dqkv_ref[rows, window(t)] += dq
            dqkv_ref[rows, window(t, PROJ)] += dk
            dqkv_ref[rows, window(t, 2 * PROJ)] += dv

    dqkvb_ref[...] = dqkv_ref[...].astype(BF16)

    @pl.loop(0, D // 256)
    def _(i):
        c = cols(i, 256)
        hg_ref[:, c] = dot_nt(dqkvb_ref[...], w_ref[c, :])

    def norm_back(rows):
        grad = rms_back(pal_ref[rows, :].astype(F32), norm_gain_ref, hg_ref[rows, :])
        pal_grad_ref[rows, :] = (rg_ref[rows, :] + grad).astype(BF16)

    norm_back(slice(0, WIN))
    grad_rim.start()

    @pl.loop(1, ROWS // WIN)
    def _(i):
        norm_back(pl.ds(pl.multiple_of(i * WIN, WIN), WIN))

    grad_rim.wait()
    own_ref[:WIN, :] = jnp.where(below, grad_rim_ref[...], pal_grad_ref[:WIN, :])
    own_ref[WIN:, :] = pal_grad_ref[WIN:, :]
    for c in range(0, D, 256):
        part = dot_tn(turn_ref[...], own_ref[:, c : c + 256])
        pg_ref[:, c : c + 256] = part.astype(BF16)

    exchange_drain(0, send1)
    weights_drain()
    exchange_drain(1, send2)
    exchange_wait(1, send2, recv2)


def place_kernel(n_enc, slabs_ref, grads_ref, llm_ref, pg_ref, wide_ref, llm_wide):
    for t in range(SLAB_W // 128):
        wide_ref[t] = slabs_ref[:, 128 * t : 128 * t + 128].astype(F32)
    for q in range(4):
        for t in range(D // 128):
            at = q * (D // 128) + t
            for slot in range(4):
                part = wide_ref[t, pl.ds(4 * slot + q, n_enc, stride=SLAB), :]
                llm_wide[at, pl.ds(slot, n_enc, stride=CAP), :] = part
        for p, (off, width) in enumerate(PIECES):
            for t in range(width // 128):
                at = (q * D + off) // 128 + t
                part = wide_ref[D // 128 + t, pl.ds(4 * q + p, n_enc, stride=SLAB), :]
                llm_wide[at, pl.ds(4, n_enc, stride=CAP), :] = part
    for t in range(4 * D // 128):
        llm_ref[:, 128 * t : 128 * t + 128] = llm_wide[t].astype(BF16)
    pg_ref[...] = grads_ref[...]


def per_device(
    n_enc,
    n_x,
    n_z,
    patches,
    norm_gain,
    merge_gain,
    qkv_weight,
    out_weight,
    window_phase,
    owner_enc,
    owner_slot,
    llm_grads,
):
    n_row = n_x * n_z
    n_slot = n_enc * CAP
    vmem = pl.BlockSpec(memory_space=pltpu.VMEM)
    smem = pl.BlockSpec(memory_space=pltpu.SMEM)
    anywhere = pl.BlockSpec(memory_space=pl.ANY)
    dma = pltpu.SemaphoreType.DMA
    slabs = pltpu.VMEM((n_enc * SLAB, SLAB_W), BF16)
    slabs_in, grads_in = pl.pallas_call(
        functools.partial(kernel, n_enc, n_x, n_z),
        out_shape=(
            jax.ShapeDtypeStruct((n_enc * SLAB, SLAB_W), BF16),
            jax.ShapeDtypeStruct((ROWS, D), BF16),
        ),
        in_specs=[smem, anywhere] + [vmem] * 6 + [anywhere],
        out_specs=(anywhere, vmem),
        scratch_shapes=[
            pltpu.VMEM((ROWS, D), BF16),
            pltpu.VMEM((n_slot, 4 * D), BF16),
            *(pltpu.VMEM((n_row, 2 * SHARD, width), BF16) for width in FLOWS),
            pltpu.VMEM((D, 3 * PROJ), BF16),
            pltpu.VMEM((PROJ, D), BF16),
            pltpu.VMEM((PROJ, D), F32),
            pltpu.VMEM((ROWS, ROWS), BF16),
            pltpu.VMEM((ROWS, D), BF16),
            pltpu.VMEM((2, WIN, D), BF16),
            pltpu.VMEM((AL, D), BF16),
            pltpu.VMEM((AL, D), BF16),
            pltpu.VMEM((AL, 3 * PROJ), BF16),
            pltpu.VMEM((HEADS, ROWS, 128), F32),
            pltpu.VMEM((AL, 128), F32),
            pltpu.VMEM((AL, PROJ), F32),
            pltpu.VMEM((AL, PROJ), BF16),
            pltpu.VMEM((AL, D), BF16),
            pltpu.VMEM((AL, D), BF16),
            pltpu.VMEM((ROWS, D), BF16),
            pltpu.VMEM((WIN, D), BF16),
            pltpu.VMEM((ROWS, D), F32),
            pltpu.VMEM((ROWS, D), BF16),
            pltpu.VMEM((ROWS, PROJ), BF16),
            pltpu.VMEM((ROWS, 3 * PROJ), F32),
            pltpu.VMEM((ROWS, 3 * PROJ), BF16),
            pltpu.VMEM((ROWS, D), F32),
            pltpu.VMEM((ROWS, D), BF16),
            pltpu.VMEM((WIN, D), BF16),
            pltpu.VMEM((5, n_enc * SLAB, ROWS), BF16),
            pltpu.VMEM((5, ROWS, n_enc * SLAB), BF16),
            pltpu.VMEM((8, ROWS), jnp.int32),
            pltpu.VMEM((4 * D // 128, n_slot, 128), F32),
            pltpu.VMEM((SLAB_W // 128, n_enc * SLAB, 128), F32),
            slabs,
            slabs,
            slabs,
            pltpu.VMEM((2 * SLAB, SLAB_W), BF16),
            pltpu.VMEM((2 * SLAB, SLAB_W), BF16),
            dma((3,)),
            dma((n_row,)),
            dma((2,)),
            dma((2,)),
            dma((2,)),
            dma((4,)),
            dma((4,)),
            dma((2,)),
            dma((2,)),
            dma((2,)),
            dma((2,)),
            dma((2,)),
        ],
        compiler_params=pltpu.CompilerParams(
            collective_id=0, has_side_effects=True, vmem_limit_bytes=56 * 1024 * 1024
        ),
        cost_estimate=pl.CostEstimate(flops=8_000_000_000, bytes_accessed=4_000_000, transcendentals=400000),
    )(
        window_phase,
        patches,
        norm_gain,
        merge_gain,
        qkv_weight,
        out_weight,
        owner_enc.reshape(1, -1),
        owner_slot.reshape(1, -1),
        llm_grads,
    )
    return pl.pallas_call(
        functools.partial(place_kernel, n_enc),
        out_shape=(
            jax.ShapeDtypeStruct((n_slot, 4 * D), BF16),
            jax.ShapeDtypeStruct((ROWS, D), BF16),
        ),
        in_specs=[vmem, vmem],
        out_specs=(vmem, vmem),
        scratch_shapes=[
            pltpu.VMEM((SLAB_W // 128, n_enc * SLAB, 128), F32),
            pltpu.VMEM((4 * D // 128, n_slot, 128), F32),
        ],
        compiler_params=pltpu.CompilerParams(vmem_limit_bytes=60 * 1024 * 1024),
        cost_estimate=pl.CostEstimate(
            flops=1_000_000, bytes_accessed=3_200_000, transcendentals=0
        ),
    )(slabs_in, grads_in)


def solution(mesh):
    n_enc, n_row = mesh.shape["enc"], mesh.shape["row"]
    n_x = 4
    in_specs = (
        P(("enc", "row"), None),
        P(),
        P(),
        P("row", None),
        P("row", None),
        P(),
        P(("enc", "row")),
        P(("enc", "row")),
        P(("enc", "row"), None),
    )
    out_specs = (P(("enc", "row"), None), P(("enc", "row"), None))
    return jax.shard_map(
        functools.partial(per_device, n_enc, n_x, n_row // n_x),
        mesh=mesh,
        in_specs=in_specs,
        out_specs=out_specs,
        check_vma=False,
    )
```

```python
import functools
import heapq

import jax
import jax.numpy as jnp
from jax import lax
from jax.experimental import pallas as pl
from jax.experimental.pallas import tpu as pltpu
from jax.sharding import PartitionSpec as P

HEADS = 8
HEAD_DIM = 80
WIN = 64
EPS = 1e-06

ROWS = 256
AL = ROWS + WIN
D = 1280
PROJ = HEADS * HEAD_DIM
CAP = 5
SHARD = 40
OUT_SHARD = 20
FLOWS = (512, 768)
SPLIT = 1024
SLAB = 16
SLAB_W = 1664
PIECES = ((0, 384), (384, 384), (768, 256), (1024, 256))
BLOCKS = ((0, 128, 0), (128, 128, 128), (256, 64, 192))
SLOT = 0.5

F32 = jnp.float32
BF16 = jnp.bfloat16
MESH = pl.DeviceIdType.MESH


def dot(a, b):
    return lax.dot_general(a, b, (((1,), (0,)), ((), ())), preferred_element_type=F32)


def dot_nt(a, b):
    return lax.dot_general(a, b, (((1,), (1,)), ((), ())), preferred_element_type=F32)


def dot_tn(a, b):
    return lax.dot_general(a, b, (((0,), (0,)), ((), ())), preferred_element_type=F32)


def iota(shape, dim):
    return lax.broadcasted_iota(jnp.int32, shape, dim)


def one_hot(cond):
    return jnp.where(cond, 1.0, 0.0).astype(BF16)


def ring_plan(n_x, n_z):
    dims = ((n_x, n_z), (n_z, n_x))
    tile_time = 0.16
    hop_time = 1.0

    def onward(port, da, db):
        size_a, size_b = dims[port]
        out = []
        if db == 0:
            for sign, reach in ((1, size_a // 2), (-1, size_a // 2 - 1)):
                gone = abs(da) if da * sign <= 0 else reach
                if gone < reach:
                    out.append((0, sign, reach - gone + size_b / 2))
        plus = size_b // 2 if da % 2 == 0 else size_b // 2 - 1
        for sign, reach in ((1, plus), (-1, size_b - 1 - plus)):
            gone = abs(db) if db * sign <= 0 else reach
            if gone < reach:
                out.append((1, sign, reach - gone))
        return out

    events = [[] for _ in FLOWS]
    free = {}
    waiting = {}
    count = 100
    agenda = [(0.0, f, f, (0, 0)) for f in range(len(FLOWS))]
    while agenda:
        now, _, flow, what = heapq.heappop(agenda)
        if len(what) == 2:
            port = flow
            if what != (0, 0):
                events[flow].append((now, count, "wait", what, None))
            for axis, sign, left in onward(port, *what):
                link = ("x" if axis == port else "z", sign)
                count += 2
                line = waiting.setdefault(link, [])
                heapq.heappush(line, (-left, count, flow, what, axis, sign, now))
                wake = max(now, free.get(link, 0.0))
                heapq.heappush(agenda, (wake, count + 10**6, flow, (link,)))
            continue
        link = what[0]
        if free.get(link, 0.0) > now + 1e-9 or not waiting[link]:
            continue
        _, _, flow, (da, db), axis, sign, ready = heapq.heappop(waiting[link])
        count += 2
        issue = max(ready, now - 1.0)
        hop = (sign, 0) if axis == 0 else (0, sign)
        events[flow].append((issue, count, "send", (da, db), hop))
        end = now + FLOWS[flow] / 64 * tile_time
        free[link] = end
        there = (da - sign, db) if axis == 0 else (da, db - sign)
        heapq.heappush(agenda, (end + hop_time, count, flow, there))
        heapq.heappush(agenda, (end, count + 10**6, flow, (link,)))
    return [sorted(flow_events) for flow_events in events]


def kernel(
    n_enc,
    n_x,
    n_z,
    phase_ref,
    patches_hbm,
    norm_gain_ref,
    merge_gain_ref,
    qkv_shard_ref,
    out_shard_ref,
    owner_enc_ref,
    owner_slot_ref,
    grads_hbm,
    recv2,
    pg_ref,
    patches_ref,
    grads_ref,
    wg0,
    wg1,
    w_ref,
    wo_ref,
    wo_wide,
    turn_ref,
    own_ref,
    rim_ref,
    pal_ref,
    hid_ref,
    qkv_ref,
    prob_ref,
    mask_ref,
    att_ref,
    resid_ref,
    normed_ref,
    ng_ref,
    ng_rim_ref,
    rg_ref,
    rgb_ref,
    ag_ref,
    dqkvb_ref,
    hg_ref,
    pal_grad_ref,
    grad_rim_ref,
    sel_ref,
    selt_ref,
    target_ref,
    slot_wide,
    slab_wide,
    send1,
    recv1,
    send2,
    relay1,
    relay2,
    w_send,
    w_recv,
    other_recv,
    slab_send,
    slab_recv,
    rim_send,
    rim_recv,
    relay_send,
    relay_recv,
    forward_send,
    own_sem,
    fetch_sem,
):
    n_row = n_x * n_z
    n_y = n_enc // 2
    n_slot = n_enc * CAP
    n_slab_rows = n_enc * SLAB
    enc = lax.axis_index("enc")
    row = lax.axis_index("row")
    core = lax.rem(enc, 2)
    y = enc // 2
    sibling = enc + 1 - 2 * core
    x = row // n_z
    z = lax.rem(row, n_z)
    left = lax.rem(row + n_row - 1, n_row)
    right = lax.rem(row + 1, n_row)
    phase = phase_ref[enc]
    edge = WIN - phase

    xs = [lax.rem(x + d, n_x) * n_z for d in range(n_x)]
    zs = [lax.rem(z + d, n_z) for d in range(n_z)]
    ys = [lax.rem(y + d, n_y) for d in range(n_y)]

    def xz(dx, dz):
        return xs[dx % n_x] + zs[dz % n_z]

    def chip(o):
        return ys[o % n_y]

    def cols(i, width):
        return pl.ds(pl.multiple_of(i * width, width), width)

    fetch_patches = pltpu.make_async_copy(patches_hbm, patches_ref, fetch_sem.at[0])
    fetch_grads = pltpu.make_async_copy(grads_hbm, grads_ref, fetch_sem.at[1])
    fetch_patches.start()
    fetch_grads.start()

    barrier = pltpu.get_barrier_semaphore()
    peers = [(enc, xz(1, 0)), (enc, xz(-1, 0)), (enc, xz(0, 1)), (enc, xz(0, -1))]
    peers += [(enc, left), (enc, right)]
    for peer in peers:
        pl.semaphore_signal(barrier, inc=1, device_id=peer, device_id_type=MESH)

    @pl.loop(1, n_enc)
    def _(d):
        pl.semaphore_signal(
            barrier, inc=1, device_id=(lax.rem(enc + d, n_enc), row), device_id_type=MESH
        )

    q_wide = qkv_shard_ref[...].astype(F32)
    odd_z = lax.rem(z, 2)
    odd = odd_z
    m = iota((SHARD, 1), 0)
    from_left = jnp.where(m < 16, m + 4 * odd, -1)
    from_left = jnp.where((m >= 32) & (m < 36), m - 16 - 64 * odd, from_left)
    from_left = jnp.where(m >= 36, m - 36 - 64 * (1 - odd), from_left)
    from_right = jnp.where((m >= 16) & (m < 32), m - 16 + 4 * odd, -1)
    from_right = jnp.where((m >= 32) & (m < 36), m - 32 - 64 * (1 - odd), from_right)
    from_right = jnp.where(m >= 36, m - 20 - 64 * odd, from_right)
    source = iota((SHARD, OUT_SHARD), 1)
    out40 = dot(one_hot(source == from_left), out_shard_ref[:, :PROJ]) + dot(
        one_hot(source == from_right), out_shard_ref[:, PROJ:]
    )

    def stacked(*parts):
        return jnp.concatenate(parts, 0).astype(BF16)

    wg0[row] = stacked(q_wide[:, :512], q_wide[:, 512:SPLIT])
    wg1[row] = stacked(q_wide[:, SPLIT:1792], jnp.concatenate([q_wide[:, 1792:], out40], 1))

    pl.semaphore_wait(barrier, len(peers) + n_enc - 1)

    plans = ring_plan(n_x, n_z)
    bufs = (wg0, wg1)

    def place(port, da, db):
        return xz(da, db) if port == 0 else xz(db, da)

    def block_wait(port, block):
        buf, r = bufs[port], place(port, *block)
        pltpu.make_async_copy(buf.at[r], buf.at[r], w_recv.at[r]).wait()

    def block_send(port, block, hop):
        buf, r = bufs[port], place(port, *block)
        pltpu.make_async_remote_copy(
            src_ref=buf.at[r],
            dst_ref=buf.at[r],
            send_sem=w_send.at[0],
            recv_sem=w_recv.at[r],
            device_id=(enc, place(port, *hop)),
            device_id_type=MESH,
        ).start()

    def hand_over(ref, send_sem, recv_sem):
        pltpu.make_async_remote_copy(
            src_ref=ref,
            dst_ref=ref,
            send_sem=send_sem,
            recv_sem=recv_sem,
            device_id=(sibling, row),
            device_id_type=MESH,
        ).start()

    def pack_pair(port, j):
        rows = pl.ds(pl.multiple_of(j * 2 * SHARD, 2 * SHARD), 2 * SHARD)
        out_rows = pl.ds(pl.multiple_of(j * 2 * OUT_SHARD, 8), 2 * OUT_SHARD)

        def halves(top):
            return [bufs[port][2 * j + k, top : top + SHARD, :].astype(F32) for k in range(2)]

        if port == 0:
            w_ref[rows, :512] = stacked(*halves(0))
            w_ref[rows, 512:SPLIT] = stacked(*halves(SHARD))
            hand_over(w_ref.at[rows, pl.ds(0, SPLIT)], w_send.at[1], other_recv.at[0])
            return
        w_ref[rows, SPLIT:1792] = stacked(*halves(0))
        even, odd = halves(SHARD)
        w_ref[rows, 1792:] = stacked(even[:, :128], odd[:, :128])
        hand_over(w_ref.at[rows, pl.ds(SPLIT, 3 * PROJ - SPLIT)], w_send.at[1], other_recv.at[0])
        even, odd = even[:, 128:], odd[:, 128:]
        upper = iota((8, 1), 0) < 4
        middle = jnp.where(upper, even[32:], odd[32:])
        wo_wide[out_rows, :PROJ] = jnp.concatenate([even[:16], middle, odd[:16]], 0)
        middle = pltpu.roll(jnp.where(upper, odd[32:], even[32:]), 4, 0)
        wo_wide[out_rows, PROJ:] = jnp.concatenate([even[16:32], middle, odd[16:32]], 0)
        hand_over(wo_wide.at[out_rows], w_send.at[2], other_recv.at[1])

    def rows_wait(ref, sem):
        pltpu.make_async_copy(ref, ref, sem).wait()

    def port_rows(port):
        return w_ref.at[:, pl.ds(0, SPLIT) if port == 0 else pl.ds(SPLIT, 3 * PROJ - SPLIT)]

    def slot_of(event):
        return int(event[0] / SLOT)

    n_slots = max(slot_of(plan[-1]) for plan in plans) + 1

    def pairs_after(port):
        arrival = {(0, 0): 0}
        for event in plans[port]:
            if event[2] == "wait":
                da, db = event[3]
                dx, dz = (da, db) if port == 0 else (db, da)
                arrival[dx % n_x, dz % n_z] = slot_of(event)
        found = []
        for m in range(1, n_z // 2 + 1):
            even, odd = (m - 1, -m) if m % 2 else (-m, m - 1)
            for dx in range(n_x):
                last = max(
                    arrival[dx, (start + k) % n_z] for start in (even, odd) for k in range(2)
                )
                found.append((last, dx, even, odd))
        return found

    def run_slot(port, slot):
        for event in plans[port]:
            if slot_of(event) == slot:
                _, _, kind, block, hop = event
                if kind == "wait":
                    block_wait(port, block)
                else:
                    block_send(port, block, hop)
        for last, dx, even, odd in pairs_after(port):
            if last == slot:
                first = xz(dx, even) + (xz(dx, odd) - xz(dx, even)) * odd_z
                pack_pair(port, first // 2)

    def weights_slot(slot):
        for port in range(2):
            if any(slot_of(event) == slot for event in plans[port]):

                @pl.when(core == port)
                def _():
                    run_slot(port, slot)

    def weights_drain():
        blocks = pl.ds(0, n_row - 1)
        for port in range(2):

            @pl.when(core == port)
            def _():
                rows_wait(bufs[port].at[blocks], w_send.at[0])
                rows_wait(port_rows(port), w_send.at[1])
                if port == 1:
                    rows_wait(wo_wide, w_send.at[2])

    def rim_copy(index, src, dst, target):
        return pltpu.make_async_remote_copy(
            src_ref=src,
            dst_ref=dst,
            send_sem=rim_send.at[index],
            recv_sem=rim_recv.at[index],
            device_id=(enc, target),
            device_id_type=MESH,
        )

    top = pl.ds(0, WIN)
    rims = (
        rim_copy(0, own_ref.at[top], rim_ref.at[0], right),
        rim_copy(1, own_ref.at[top], rim_ref.at[1], left),
    )
    ng_rim = rim_copy(2, ng_ref.at[top], ng_rim_ref, right)
    grad_rim = rim_copy(3, pal_grad_ref.at[top], grad_rim_ref, left)

    def slab(ref, e):
        return ref.at[pl.ds(pl.multiple_of(SLAB * e, SLAB), SLAB)]

    def exchange_copy(index, send, recv, peer):
        return pltpu.make_async_remote_copy(
            src_ref=slab(send, peer),
            dst_ref=slab(recv, enc),
            send_sem=slab_send.at[index],
            recv_sem=slab_recv.at[index],
            device_id=(peer, row),
            device_id_type=MESH,
        )

    def near_peers():
        for o in range(n_y // 2 - 1, 0, -1):
            ahead, behind = chip(o), chip(-o)
            for side in (0, 1):
                turned = ahead + (behind - ahead) * (core if side == 0 else 1 - core)
                for k in range(2):
                    yield 2 * turned + k
        yield sibling

    next_chip = chip(1) + (chip(-1) - chip(1)) * core
    last_chip = chip(-1) + (chip(1) - chip(-1)) * core
    far_chip = chip(n_y // 2 - 1) + (chip(n_y // 2 + 1) - chip(n_y // 2 - 1)) * core

    def relay_copy(index, send):
        pair = pl.ds(pl.multiple_of(2 * SLAB * chip(n_y // 2), 2 * SLAB), 2 * SLAB)
        return pltpu.make_async_remote_copy(
            src_ref=send.at[pair],
            dst_ref=(relay1, relay2)[index],
            send_sem=relay_send.at[index],
            recv_sem=relay_recv.at[index],
            device_id=(2 * next_chip + core, row),
            device_id_type=MESH,
        )

    def forward_copy(index, recv, k):
        origin = 2 * last_chip + core
        return pltpu.make_async_remote_copy(
            src_ref=(relay1, relay2)[index].at[pl.ds(SLAB * k, SLAB)],
            dst_ref=slab(recv, origin),
            send_sem=forward_send.at[index],
            recv_sem=slab_recv.at[index],
            device_id=(2 * far_chip + k, row),
            device_id_type=MESH,
        )

    def own_copy(index, send, recv):
        return pltpu.make_async_copy(slab(send, enc), slab(recv, enc), own_sem.at[index])

    def exchange_start(index, send, recv):
        relay_copy(index, send).start()
        for peer in near_peers():
            exchange_copy(index, send, recv, peer).start()
        own_copy(index, send, recv).start()

    def exchange_forward(index, recv):
        relay_copy(index, send1).wait_recv()
        for k in range(2):
            forward_copy(index, recv, k).start()

    def exchange_wait(index, send, recv):
        own_copy(index, send, recv).wait()
        rows_wait(recv.at[pl.ds(0, (n_enc - 1) * SLAB)], slab_recv.at[index])

    def exchange_drain(index, send):
        relay_copy(index, send).wait_send()
        rows_wait(send.at[pl.ds(0, (n_enc - 3) * SLAB)], slab_send.at[index])
        rows_wait((relay1, relay2)[index], forward_send.at[index])

    def rotate():
        fetch_patches.wait()
        turn = iota((ROWS, ROWS), 1) == ((iota((ROWS, ROWS), 0) - edge) & (ROWS - 1))
        turn_ref[...] = one_hot(turn)
        for c in range(0, D, 256):
            part = dot(turn_ref[...], patches_ref[:, c : c + 256])
            own_ref[:, c : c + 256] = part.astype(BF16)
        for copy in rims:
            copy.start()

    n_tile = D // 128

    def grads_wide(q0, q1):
        if q0 == 0:
            fetch_grads.wait()
        for t in range(q0 * n_tile, q1 * n_tile):
            slot_wide[t] = grads_ref[:, 128 * t : 128 * t + 128].astype(F32)

    def grads_move(q):
        for t in range(n_tile):
            at = q * n_tile + t
            for slot in range(4):
                part = slot_wide[at, pl.ds(slot, n_enc, stride=CAP), :]
                slab_wide[t, pl.ds(4 * slot + q, n_enc, stride=SLAB), :] = part
        for p, (off, width) in enumerate(PIECES):
            for t in range(3):
                if t < width // 128:
                    at = (q * D + off) // 128 + t
                    part = slot_wide[at, pl.ds(4, n_enc, stride=CAP), :]
                else:
                    part = jnp.zeros((n_enc, 128), F32)
                slab_wide[n_tile + t, pl.ds(4 * q + p, n_enc, stride=SLAB), :] = part

    def grads_pack(first, last):
        for t in range(first, last):
            send1[:, 128 * t : 128 * t + 128] = slab_wide[t].astype(BF16)
        if last == SLAB_W // 128:
            exchange_start(0, send1, recv1)

    n_tok = ROWS // 4

    def targets(code, patch):
        slot, base = code & 7, (code >> 3) * 16
        quarter = patch & 3
        target_a = jnp.where(slot < 4, base + slot * 4 + quarter, -1)
        target_b = jnp.where(slot == 4, base + quarter * 4, -8)
        return target_a, target_b

    def selector_targets():
        code_row = owner_enc_ref[...] * 8 + owner_slot_ref[...]
        square = iota((n_tok, n_tok), 0) == iota((n_tok, n_tok), 1)
        code_col = jnp.sum(jnp.where(square, code_row, 0), 1, keepdims=True)
        patch = (iota((1, ROWS), 1) - edge) & (ROWS - 1)
        tok = iota((n_tok, ROWS), 0) == (patch >> 2)
        code = jnp.sum(jnp.where(tok, code_col, 0), 0, keepdims=True)
        target_ref[0:1, :], target_ref[1:2, :] = targets(code, patch)

    def selector(p):
        bucket = iota((n_slab_rows, ROWS), 0)
        target = target_ref[0:1, :] if p == 0 else target_ref[1:2, :] + (p - 1)
        sel_ref[p] = one_hot(bucket == target)

    def selectors_back():
        code_row = owner_enc_ref[...] * 8 + owner_slot_ref[...]
        patch = (iota((ROWS, 1), 0) - edge) & (ROWS - 1)
        tok = iota((ROWS, n_tok), 1) == (patch >> 2)
        code = jnp.sum(jnp.where(tok, code_row, 0), 1, keepdims=True)
        target_a, target_b = targets(code, patch)
        bucket = iota((ROWS, n_slab_rows), 1)
        selt_ref[0] = one_hot(bucket == target_a)
        for p in range(4):
            selt_ref[1 + p] = one_hot(bucket == target_b + p)

    def piece(body, *args):
        return lambda: body(*args)

    def masks(r0, count, k0):
        i = iota((count, 128), 0) + r0
        j = iota((count, 128), 1) + k0
        first = jnp.where(row == 0, 0, -1)
        last = jnp.where(row == n_row - 1, ROWS // WIN, -1)
        ends = ((i >> 6) == first) | ((i >> 6) == last)
        i_low = jnp.where((i & (WIN - 1)) < edge, 1, 0)
        j_low = jnp.where((j & (WIN - 1)) < edge, 1, 0)
        apart = jnp.where(ends, i_low ^ j_low, 0)
        same = ((i >> 6) == (j >> 6)) & (apart == 0)
        mask_ref[r0 : r0 + count, :] = jnp.where(same, 1.0, 0.0)

    below = iota((WIN, 1), 0) < edge

    def rims_in():
        for copy in rims:
            copy.wait()
        pal_ref[:WIN, :] = jnp.where(below, rim_ref[0], own_ref[:WIN, :])
        pal_ref[WIN:ROWS, :] = own_ref[WIN:, :]
        pal_ref[ROWS:, :] = jnp.where(below, own_ref[:WIN, :], rim_ref[1])

    def rms_norm(src, dst, gain_ref, rows):
        wide = src[rows, :].astype(F32)
        inv = lax.rsqrt(jnp.mean(wide * wide, -1, keepdims=True) + EPS)
        dst[rows, :] = (wide * inv * gain_ref[...].reshape(1, D)).astype(BF16)

    def rms_back(wide, gain_ref, upstream_in):
        inv = lax.rsqrt(jnp.mean(wide * wide, -1, keepdims=True) + EPS)
        upstream = upstream_in * gain_ref[...].reshape(1, D)
        inner = jnp.mean(upstream * wide, -1, keepdims=True)
        return inv * upstream - wide * (inv * inv * inv) * inner

    def piece(body, *args):
        return lambda: body(*args)

    def project(c0, c1):
        for c in range(c0, c1, 256):
            w = min(256, c1 - c)
            part = dot(hid_ref[...], w_ref[:, c : c + w])
            qkv_ref[:, c : c + w] = part.astype(BF16)

    scale = HEAD_DIM ** (-0.5)
    pairs = range(HEADS // 2)

    def window(t, base=0):
        return slice(base + 128 * t, base + 128 * t + 256)

    def two_heads(t, value):
        lane = iota((1, 256), 1) - 32 * t
        zero = jnp.zeros_like(value)
        first = jnp.where((lane >= 0) & (lane < HEAD_DIM), value, zero)
        second = jnp.where((lane >= HEAD_DIM) & (lane < 2 * HEAD_DIM), value, zero)
        return jnp.concatenate([first, second], 0)

    def join(ref, rows, base, t, value, carry):
        low = value[:, :128] if carry is None else value[:, :128] + carry
        ref[rows, base + 128 * t : base + 128 * t + 128] = low.astype(BF16)
        high = value[:, 128:]
        if t == pairs[-1]:
            ref[rows, base + 128 * t + 128 : base + 128 * t + 256] = high.astype(BF16)
        return high

    def attend(r0, count, k0):
        rows, keys = slice(r0, r0 + count), slice(k0, k0 + 128)
        carry = None
        for t in pairs:
            scores = dot_nt(qkv_ref[rows, window(t)], two_heads(t, qkv_ref[keys, window(t, PROJ)]))
            seen = mask_ref[rows, :] > 0.5
            both = []
            for g in range(2):
                s = jnp.where(seen, scores[:, 128 * g : 128 * g + 128] * scale, -1e30)
                e = jnp.exp(s - jnp.max(s, -1, keepdims=True))
                p = e / jnp.sum(e, -1, keepdims=True)
                if r0 < ROWS:
                    prob_ref[2 * t + g, rows, :] = p
                both.append(p.astype(BF16))
            values = two_heads(t, qkv_ref[keys, window(t, 2 * PROJ)])
            carry = join(att_ref, rows, 0, t, dot(jnp.concatenate(both, 1), values), carry)

    work = [piece(grads_wide, 0, 2), piece(grads_wide, 2, 4)]
    work += [piece(grads_move, q) for q in range(4)]
    work += [piece(grads_pack, 0, SLAB_W // 128)]
    work += [piece(masks, *block) for block in BLOCKS]
    work += [rims_in, selector_targets]
    for k in range(5):
        rows = slice(k * WIN, (k + 1) * WIN)
        work += [piece(selector, k), piece(rms_norm, pal_ref, hid_ref, norm_gain_ref, rows)]
    work += [selectors_back]
    for slot in range(n_slots):
        weights_slot(slot)
        if slot == 0:
            rotate()
        elif work:
            work.pop(0)()
        if slot == 20:
            exchange_forward(0, recv1)
    assert not work
    for port in range(2):

        @pl.when(core == port)
        def _():
            spans = ((0, SPLIT), (SPLIT, 3 * PROJ))
            project(*spans[port])
            rows_wait(port_rows(1 - port), other_recv.at[0])
            project(*spans[1 - port])
            if port == 0:
                rows_wait(wo_wide, other_recv.at[1])

    for block in BLOCKS:
        attend(*block)

    @pl.loop(0, D // 256)
    def _(i):
        c = cols(i, 256)
        wo_ref[:, c] = wo_wide[:, c].astype(BF16)
        branch = dot(att_ref[...], wo_ref[:, c])
        resid_ref[:, c] = (pal_ref[:, c].astype(F32) + branch).astype(BF16)

    @pl.loop(0, AL // WIN)
    def _(i):
        rows = pl.ds(pl.multiple_of(i * WIN, WIN), WIN)
        rms_norm(resid_ref, normed_ref, merge_gain_ref, rows)

    normed_ref[:WIN, :] = jnp.where(below, normed_ref[ROWS:, :], normed_ref[:WIN, :])

    for c in range(0, D, 256):
        send2[:, c : c + 256] = dot(sel_ref[0], normed_ref[:ROWS, c : c + 256]).astype(BF16)
    head_part = jnp.zeros((n_slab_rows, 256), F32)
    tail_part = jnp.zeros((n_slab_rows, 128), F32)
    for p, (off, width) in enumerate(PIECES):
        head_part += dot(sel_ref[1 + p], normed_ref[:ROWS, off : off + 256])
        if width > 256:
            tail_part += dot(sel_ref[1 + p], normed_ref[:ROWS, off + 256 : off + width])
    send2[:, D : D + 256] = head_part.astype(BF16)
    send2[:, D + 256 :] = tail_part.astype(BF16)
    exchange_start(1, send2, recv2)

    exchange_wait(0, send1, recv1)

    def gradients(rows):
        for p, (off, width) in enumerate(PIECES):
            for c in range(0, width, 256):
                w = min(256, width - c)
                part = dot(selt_ref[0, rows], recv1[:, off + c : off + c + w])
                part += dot(selt_ref[1 + p, rows], recv1[:, D + c : D + c + w])
                ng_ref[rows, off + c : off + c + w] = part.astype(BF16)

    gradients(slice(0, WIN))
    ng_rim.start()
    gradients(slice(WIN, ROWS))

    def merge_back(rows, grad_in):
        grad = rms_back(resid_ref[rows, :].astype(F32), merge_gain_ref, grad_in.astype(F32))
        rg_ref[rows, :] = grad
        rgb_ref[rows, :] = grad.astype(BF16)

    @pl.loop(1, ROWS // WIN)
    def _(i):
        rows = pl.ds(pl.multiple_of(i * WIN, WIN), WIN)
        merge_back(rows, ng_ref[rows, :])

    ng_rim.wait()
    merge_back(slice(0, WIN), jnp.where(below, ng_rim_ref[...], ng_ref[:WIN, :]))

    exchange_forward(1, recv2)

    for c0, c1 in ((0, 256), (256, 512), (512, 640)):
        ag_ref[:, c0:c1] = dot_nt(rgb_ref[...], wo_ref[c0:c1, :]).astype(BF16)

    for r0 in (0, 128):
        rows = slice(r0, r0 + 128)
        carries = [None] * 3
        for t in pairs:
            grad = ag_ref[rows, window(t)]
            values = two_heads(t, qkv_ref[rows, window(t, 2 * PROJ)])
            keys = two_heads(t, qkv_ref[rows, window(t, PROJ)])
            dp = dot_nt(grad, values)
            probs, score_grads = [], []
            for g in range(2):
                p = prob_ref[2 * t + g, rows, :]
                dp_g = dp[:, 128 * g : 128 * g + 128]
                centred = dp_g - jnp.sum(p * dp_g, -1, keepdims=True)
                score_grads.append((p * centred * scale).astype(BF16))
                probs.append(p.astype(BF16))
            dq = dot(jnp.concatenate(score_grads, 1), keys)
            queries = two_heads(t, qkv_ref[rows, window(t)])
            dk = dot_tn(jnp.concatenate(score_grads, 0), queries)
            dv = dot_tn(jnp.concatenate(probs, 0), two_heads(t, grad))
            for k, value in enumerate((dq, dk, dv)):
                carries[k] = join(dqkvb_ref, rows, k * PROJ, t, value, carries[k])

    @pl.loop(0, D // 256)
    def _(i):
        c = cols(i, 256)
        hg_ref[:, c] = dot_nt(dqkvb_ref[...], w_ref[c, :])

    def norm_back(rows):
        grad = rms_back(pal_ref[rows, :].astype(F32), norm_gain_ref, hg_ref[rows, :])
        pal_grad_ref[rows, :] = (rg_ref[rows, :] + grad).astype(BF16)

    norm_back(slice(0, WIN))
    grad_rim.start()

    @pl.loop(1, ROWS // WIN)
    def _(i):
        norm_back(pl.ds(pl.multiple_of(i * WIN, WIN), WIN))

    grad_rim.wait()
    own_ref[:WIN, :] = jnp.where(below, grad_rim_ref[...], pal_grad_ref[:WIN, :])
    own_ref[WIN:, :] = pal_grad_ref[WIN:, :]
    for c in range(0, D, 256):
        part = dot_tn(turn_ref[...], own_ref[:, c : c + 256])
        pg_ref[:, c : c + 256] = part.astype(BF16)

    exchange_drain(0, send1)
    weights_drain()
    exchange_drain(1, send2)
    exchange_wait(1, send2, recv2)


def place_kernel(n_enc, slabs_ref, grads_ref, llm_ref, pg_ref, wide_ref, llm_wide):
    q = pl.program_id(0)

    @pl.when(q == 0)
    def _():
        for t in range(SLAB_W // 128):
            wide_ref[t] = slabs_ref[:, 128 * t : 128 * t + 128].astype(F32)

    n_tile = D // 128
    for t in range(n_tile):
        for slot in range(4):
            part = wide_ref[t, pl.ds(4 * slot + q, n_enc, stride=SLAB), :]
            llm_wide[t, pl.ds(slot, n_enc, stride=CAP), :] = part
    for p, (off, width) in enumerate(PIECES):
        for t in range(width // 128):
            part = wide_ref[n_tile + t, pl.ds(4 * q + p, n_enc, stride=SLAB), :]
            llm_wide[off // 128 + t, pl.ds(4, n_enc, stride=CAP), :] = part
    for t in range(n_tile):
        llm_ref[:, 128 * t : 128 * t + 128] = llm_wide[t].astype(BF16)
    pg_ref[...] = grads_ref[...]


def per_device(
    n_enc,
    n_x,
    n_z,
    patches,
    norm_gain,
    merge_gain,
    qkv_weight,
    out_weight,
    window_phase,
    owner_enc,
    owner_slot,
    llm_grads,
):
    n_row = n_x * n_z
    n_slot = n_enc * CAP
    vmem = pl.BlockSpec(memory_space=pltpu.VMEM)
    smem = pl.BlockSpec(memory_space=pltpu.SMEM)
    anywhere = pl.BlockSpec(memory_space=pl.ANY)
    dma = pltpu.SemaphoreType.DMA
    slabs = pltpu.VMEM((n_enc * SLAB, SLAB_W), BF16)
    slabs_in, grads_in = pl.pallas_call(
        functools.partial(kernel, n_enc, n_x, n_z),
        out_shape=(
            jax.ShapeDtypeStruct((n_enc * SLAB, SLAB_W), BF16),
            jax.ShapeDtypeStruct((ROWS, D), BF16),
        ),
        in_specs=[smem, anywhere] + [vmem] * 6 + [anywhere],
        out_specs=(anywhere, vmem),
        scratch_shapes=[
            pltpu.VMEM((ROWS, D), BF16),
            pltpu.VMEM((n_slot, 4 * D), BF16),
            *(pltpu.VMEM((n_row, 2 * SHARD, width), BF16) for width in FLOWS),
            pltpu.VMEM((D, 3 * PROJ), BF16),
            pltpu.VMEM((PROJ, D), BF16),
            pltpu.VMEM((PROJ, D), F32),
            pltpu.VMEM((ROWS, ROWS), BF16),
            pltpu.VMEM((ROWS, D), BF16),
            pltpu.VMEM((2, WIN, D), BF16),
            pltpu.VMEM((AL, D), BF16),
            pltpu.VMEM((AL, D), BF16),
            pltpu.VMEM((AL, 3 * PROJ), BF16),
            pltpu.VMEM((HEADS, ROWS, 128), F32),
            pltpu.VMEM((AL, 128), F32),
            pltpu.VMEM((AL, PROJ), BF16),
            pltpu.VMEM((AL, D), BF16),
            pltpu.VMEM((AL, D), BF16),
            pltpu.VMEM((ROWS, D), BF16),
            pltpu.VMEM((WIN, D), BF16),
            pltpu.VMEM((ROWS, D), F32),
            pltpu.VMEM((ROWS, D), BF16),
            pltpu.VMEM((ROWS, PROJ), BF16),
            pltpu.VMEM((ROWS, 3 * PROJ), BF16),
            pltpu.VMEM((ROWS, D), F32),
            pltpu.VMEM((ROWS, D), BF16),
            pltpu.VMEM((WIN, D), BF16),
            pltpu.VMEM((5, n_enc * SLAB, ROWS), BF16),
            pltpu.VMEM((5, ROWS, n_enc * SLAB), BF16),
            pltpu.VMEM((8, ROWS), jnp.int32),
            pltpu.VMEM((4 * D // 128, n_slot, 128), F32),
            pltpu.VMEM((SLAB_W // 128, n_enc * SLAB, 128), F32),
            slabs,
            slabs,
            slabs,
            pltpu.VMEM((2 * SLAB, SLAB_W), BF16),
            pltpu.VMEM((2 * SLAB, SLAB_W), BF16),
            dma((3,)),
            dma((n_row,)),
            dma((2,)),
            dma((2,)),
            dma((2,)),
            dma((4,)),
            dma((4,)),
            dma((2,)),
            dma((2,)),
            dma((2,)),
            dma((2,)),
            dma((2,)),
        ],
        compiler_params=pltpu.CompilerParams(
            collective_id=0, has_side_effects=True, vmem_limit_bytes=56 * 1024 * 1024
        ),
        cost_estimate=pl.CostEstimate(flops=8_000_000_000, bytes_accessed=4_000_000, transcendentals=400000),
    )(
        window_phase,
        patches,
        norm_gain,
        merge_gain,
        qkv_weight,
        out_weight,
        owner_enc.reshape(1, -1),
        owner_slot.reshape(1, -1),
        llm_grads,
    )
    return pl.pallas_call(
        functools.partial(place_kernel, n_enc),
        out_shape=(
            jax.ShapeDtypeStruct((n_slot, 4 * D), BF16),
            jax.ShapeDtypeStruct((ROWS, D), BF16),
        ),
        grid=(4,),
        in_specs=[
            pl.BlockSpec((n_enc * SLAB, SLAB_W), lambda q: (0, 0)),
            pl.BlockSpec((WIN, D), lambda q: (q, 0)),
        ],
        out_specs=(
            pl.BlockSpec((n_slot, D), lambda q: (0, q)),
            pl.BlockSpec((WIN, D), lambda q: (q, 0)),
        ),
        scratch_shapes=[
            pltpu.VMEM((SLAB_W // 128, n_enc * SLAB, 128), F32),
            pltpu.VMEM((D // 128, n_slot, 128), F32),
        ],
        compiler_params=pltpu.CompilerParams(vmem_limit_bytes=60 * 1024 * 1024),
        cost_estimate=pl.CostEstimate(
            flops=1_000_000, bytes_accessed=3_200_000, transcendentals=0
        ),
    )(slabs_in, grads_in)


def solution(mesh):
    n_enc, n_row = mesh.shape["enc"], mesh.shape["row"]
    n_x = 4
    in_specs = (
        P(("enc", "row"), None),
        P(),
        P(),
        P("row", None),
        P("row", None),
        P(),
        P(("enc", "row")),
        P(("enc", "row")),
        P(("enc", "row"), None),
    )
    out_specs = (P(("enc", "row"), None), P(("enc", "row"), None))
    return jax.shard_map(
        functools.partial(per_device, n_enc, n_x, n_row // n_x),
        mesh=mesh,
        in_specs=in_specs,
        out_specs=out_specs,
        check_vma=False,
    )
```

```python
import functools
import heapq

import jax
import jax.numpy as jnp
from jax import lax
from jax.experimental import pallas as pl
from jax.experimental.pallas import tpu as pltpu
from jax.sharding import PartitionSpec as P

HEADS = 8
HEAD_DIM = 80
WIN = 64
EPS = 1e-06

ROWS = 256
AL = ROWS + WIN
D = 1280
PROJ = HEADS * HEAD_DIM
CAP = 5
SHARD = 40
OUT_SHARD = 20
FLOWS = (512, 768)
SPLIT = 1024
SLAB = 16
SLAB_W = 1664
PIECES = ((0, 384), (384, 384), (768, 256), (1024, 256))
BLOCKS = ((0, 128, 0), (128, 128, 128), (256, 64, 192))
SLOT = 0.5

F32 = jnp.float32
BF16 = jnp.bfloat16
MESH = pl.DeviceIdType.MESH


def dot(a, b):
    return lax.dot_general(a, b, (((1,), (0,)), ((), ())), preferred_element_type=F32)


def dot_nt(a, b):
    return lax.dot_general(a, b, (((1,), (1,)), ((), ())), preferred_element_type=F32)


def dot_tn(a, b):
    return lax.dot_general(a, b, (((0,), (0,)), ((), ())), preferred_element_type=F32)


def iota(shape, dim):
    return lax.broadcasted_iota(jnp.int32, shape, dim)


def one_hot(cond):
    return jnp.where(cond, 1.0, 0.0).astype(BF16)


def ring_plan(n_x, n_z):
    dims = ((n_x, n_z), (n_z, n_x))
    tile_time = 0.16
    hop_time = 1.0

    def onward(port, da, db):
        size_a, size_b = dims[port]
        out = []
        if db == 0:
            for sign, reach in ((1, size_a // 2), (-1, size_a // 2 - 1)):
                gone = abs(da) if da * sign <= 0 else reach
                if gone < reach:
                    out.append((0, sign, reach - gone + size_b / 2))
        plus = size_b // 2 if da % 2 == 0 else size_b // 2 - 1
        for sign, reach in ((1, plus), (-1, size_b - 1 - plus)):
            gone = abs(db) if db * sign <= 0 else reach
            if gone < reach:
                out.append((1, sign, reach - gone))
        return out

    events = [[] for _ in FLOWS]
    free = {}
    waiting = {}
    count = 100
    agenda = [(0.0, f, f, (0, 0)) for f in range(len(FLOWS))]
    while agenda:
        now, _, flow, what = heapq.heappop(agenda)
        if len(what) == 2:
            port = flow
            if what != (0, 0):
                events[flow].append((now, count, "wait", what, None))
            for axis, sign, left in onward(port, *what):
                link = ("x" if axis == port else "z", sign)
                count += 2
                line = waiting.setdefault(link, [])
                heapq.heappush(line, (-left, count, flow, what, axis, sign, now))
                wake = max(now, free.get(link, 0.0))
                heapq.heappush(agenda, (wake, count + 10**6, flow, (link,)))
            continue
        link = what[0]
        if free.get(link, 0.0) > now + 1e-9 or not waiting[link]:
            continue
        _, _, flow, (da, db), axis, sign, ready = heapq.heappop(waiting[link])
        count += 2
        issue = max(ready, now - 1.0)
        hop = (sign, 0) if axis == 0 else (0, sign)
        events[flow].append((issue, count, "send", (da, db), hop))
        end = now + FLOWS[flow] / 64 * tile_time
        free[link] = end
        there = (da - sign, db) if axis == 0 else (da, db - sign)
        heapq.heappush(agenda, (end + hop_time, count, flow, there))
        heapq.heappush(agenda, (end, count + 10**6, flow, (link,)))
    return [sorted(flow_events) for flow_events in events]


def kernel(
    n_enc,
    n_x,
    n_z,
    phase_ref,
    patches_hbm,
    norm_gain_ref,
    merge_gain_ref,
    qkv_shard_ref,
    out_shard_ref,
    owner_enc_ref,
    owner_slot_ref,
    grads_hbm,
    recv2,
    pg_ref,
    patches_ref,
    grads_ref,
    wg0,
    wg1,
    w_ref,
    wo_ref,
    wo_wide,
    turn_ref,
    own_ref,
    rim_ref,
    pal_ref,
    hid_ref,
    qkv_ref,
    prob_ref,
    mask_ref,
    att_ref,
    resid_ref,
    normed_ref,
    ng_ref,
    ng_rim_ref,
    rg_ref,
    rgb_ref,
    ag_ref,
    dqkvb_ref,
    hg_ref,
    pal_grad_ref,
    grad_rim_ref,
    sel_ref,
    selt_ref,
    target_ref,
    slot_wide,
    slab_wide,
    send1,
    recv1,
    send2,
    relay1,
    relay2,
    w_send,
    w_recv,
    other_recv,
    slab_send,
    slab_recv,
    rim_send,
    rim_recv,
    relay_send,
    relay_recv,
    forward_send,
    own_sem,
    fetch_sem,
    ready_sem,
):
    n_row = n_x * n_z
    n_y = n_enc // 2
    n_slot = n_enc * CAP
    n_slab_rows = n_enc * SLAB
    enc = lax.axis_index("enc")
    row = lax.axis_index("row")
    core = lax.rem(enc, 2)
    y = enc // 2
    sibling = enc + 1 - 2 * core
    x = row // n_z
    z = lax.rem(row, n_z)
    left = lax.rem(row + n_row - 1, n_row)
    right = lax.rem(row + 1, n_row)
    phase = phase_ref[enc]
    edge = WIN - phase

    xs = [lax.rem(x + d, n_x) * n_z for d in range(n_x)]
    zs = [lax.rem(z + d, n_z) for d in range(n_z)]
    ys = [lax.rem(y + d, n_y) for d in range(n_y)]

    def xz(dx, dz):
        return xs[dx % n_x] + zs[dz % n_z]

    def chip(o):
        return ys[o % n_y]

    def cols(i, width):
        return pl.ds(pl.multiple_of(i * width, width), width)

    fetch_patches = pltpu.make_async_copy(patches_hbm, patches_ref, fetch_sem.at[0])
    fetch_grads = pltpu.make_async_copy(grads_hbm, grads_ref, fetch_sem.at[1])
    fetch_patches.start()
    fetch_grads.start()

    barrier = pltpu.get_barrier_semaphore()
    above = [xz(0, 1), right]
    below_z = [xz(0, -1), left]

    def tell(sem, target):
        pl.semaphore_signal(sem, inc=1, device_id=(enc, target), device_id_type=MESH)

    for target in (xz(1, 0), xz(-1, 0)):
        tell(barrier, target)

    @pl.loop(1, n_enc)
    def _(d):
        pl.semaphore_signal(
            barrier, inc=1, device_id=(lax.rem(enc + d, n_enc), row), device_id_type=MESH
        )

    def tell_neighbours(sem, higher):
        @pl.when((z < n_z - 1) if higher else (z == n_z - 1))
        def _():
            for target in above:
                tell(sem, target)

        @pl.when((z == 0) if higher else (z > 0))
        def _():
            for target in below_z:
                tell(sem, target)

    tell_neighbours(barrier, True)
    n_lower = jnp.where(z == 0, 0, jnp.where(z == n_z - 1, 4, 2))

    q_wide = qkv_shard_ref[...].astype(F32)
    odd_z = lax.rem(z, 2)
    odd = odd_z
    m = iota((SHARD, 1), 0)
    from_left = jnp.where(m < 16, m + 4 * odd, -1)
    from_left = jnp.where((m >= 32) & (m < 36), m - 16 - 64 * odd, from_left)
    from_left = jnp.where(m >= 36, m - 36 - 64 * (1 - odd), from_left)
    from_right = jnp.where((m >= 16) & (m < 32), m - 16 + 4 * odd, -1)
    from_right = jnp.where((m >= 32) & (m < 36), m - 32 - 64 * (1 - odd), from_right)
    from_right = jnp.where(m >= 36, m - 20 - 64 * odd, from_right)
    source = iota((SHARD, OUT_SHARD), 1)
    out40 = dot(one_hot(source == from_left), out_shard_ref[:, :PROJ]) + dot(
        one_hot(source == from_right), out_shard_ref[:, PROJ:]
    )

    def stacked(*parts):
        return jnp.concatenate(parts, 0).astype(BF16)

    wg0[row] = stacked(q_wide[:, :512], q_wide[:, 512:SPLIT])
    wg1[row] = stacked(q_wide[:, SPLIT:1792], jnp.concatenate([q_wide[:, 1792:], out40], 1))


    plans = ring_plan(n_x, n_z)
    bufs = (wg0, wg1)

    def place(port, da, db):
        return xz(da, db) if port == 0 else xz(db, da)

    def block_wait(port, block):
        buf, r = bufs[port], place(port, *block)
        pltpu.make_async_copy(buf.at[r], buf.at[r], w_recv.at[r]).wait()

    def block_send(port, block, hop):
        buf, r = bufs[port], place(port, *block)
        pltpu.make_async_remote_copy(
            src_ref=buf.at[r],
            dst_ref=buf.at[r],
            send_sem=w_send.at[0],
            recv_sem=w_recv.at[r],
            device_id=(enc, place(port, *hop)),
            device_id_type=MESH,
        ).start()

    def hand_over(ref, send_sem, recv_sem):
        pltpu.make_async_remote_copy(
            src_ref=ref,
            dst_ref=ref,
            send_sem=send_sem,
            recv_sem=recv_sem,
            device_id=(sibling, row),
            device_id_type=MESH,
        ).start()

    def pack_pair(port, j):
        rows = pl.ds(pl.multiple_of(j * 2 * SHARD, 2 * SHARD), 2 * SHARD)
        out_rows = pl.ds(pl.multiple_of(j * 2 * OUT_SHARD, 8), 2 * OUT_SHARD)

        def halves(top):
            return [bufs[port][2 * j + k, top : top + SHARD, :].astype(F32) for k in range(2)]

        if port == 0:
            w_ref[rows, :512] = stacked(*halves(0))
            w_ref[rows, 512:SPLIT] = stacked(*halves(SHARD))
            hand_over(w_ref.at[rows, pl.ds(0, SPLIT)], w_send.at[1], other_recv.at[0])
            return
        w_ref[rows, SPLIT:1792] = stacked(*halves(0))
        even, odd = halves(SHARD)
        w_ref[rows, 1792:] = stacked(even[:, :128], odd[:, :128])
        hand_over(w_ref.at[rows, pl.ds(SPLIT, 3 * PROJ - SPLIT)], w_send.at[1], other_recv.at[0])
        even, odd = even[:, 128:], odd[:, 128:]
        upper = iota((8, 1), 0) < 4
        middle = jnp.where(upper, even[32:], odd[32:])
        wo_wide[out_rows, :PROJ] = jnp.concatenate([even[:16], middle, odd[:16]], 0)
        middle = pltpu.roll(jnp.where(upper, odd[32:], even[32:]), 4, 0)
        wo_wide[out_rows, PROJ:] = jnp.concatenate([even[16:32], middle, odd[16:32]], 0)
        hand_over(wo_wide.at[out_rows], w_send.at[2], other_recv.at[1])

    def rows_wait(ref, sem):
        pltpu.make_async_copy(ref, ref, sem).wait()

    def port_rows(port):
        return w_ref.at[:, pl.ds(0, SPLIT) if port == 0 else pl.ds(SPLIT, 3 * PROJ - SPLIT)]

    def slot_of(event):
        return int(event[0] / SLOT)

    n_slots = max(slot_of(plan[-1]) for plan in plans) + 1

    def pairs_after(port):
        arrival = {(0, 0): 0}
        for event in plans[port]:
            if event[2] == "wait":
                da, db = event[3]
                dx, dz = (da, db) if port == 0 else (db, da)
                arrival[dx % n_x, dz % n_z] = slot_of(event)
        found = []
        for m in range(1, n_z // 2 + 1):
            even, odd = (m - 1, -m) if m % 2 else (-m, m - 1)
            for dx in range(n_x):
                last = max(
                    arrival[dx, (start + k) % n_z] for start in (even, odd) for k in range(2)
                )
                found.append((last, dx, even, odd))
        return found

    def run_slot(port, slot):
        for event in plans[port]:
            if slot_of(event) == slot:
                _, _, kind, block, hop = event
                if kind == "wait":
                    block_wait(port, block)
                else:
                    block_send(port, block, hop)
        for last, dx, even, odd in pairs_after(port):
            if last == slot:
                first = xz(dx, even) + (xz(dx, odd) - xz(dx, even)) * odd_z
                pack_pair(port, first // 2)

    def weights_slot(slot):
        for port in range(2):
            if any(slot_of(event) == slot for event in plans[port]):

                @pl.when(core == port)
                def _():
                    run_slot(port, slot)

    def weights_drain():
        blocks = pl.ds(0, n_row - 1)
        for port in range(2):

            @pl.when(core == port)
            def _():
                rows_wait(bufs[port].at[blocks], w_send.at[0])
                rows_wait(port_rows(port), w_send.at[1])
                if port == 1:
                    rows_wait(wo_wide, w_send.at[2])

    def rim_copy(index, src, dst, target):
        return pltpu.make_async_remote_copy(
            src_ref=src,
            dst_ref=dst,
            send_sem=rim_send.at[index],
            recv_sem=rim_recv.at[index],
            device_id=(enc, target),
            device_id_type=MESH,
        )

    top = pl.ds(0, WIN)
    rims = (
        rim_copy(0, own_ref.at[top], rim_ref.at[0], right),
        rim_copy(1, own_ref.at[top], rim_ref.at[1], left),
    )
    ng_rim = rim_copy(2, ng_ref.at[top], ng_rim_ref, right)
    grad_rim = rim_copy(3, pal_grad_ref.at[top], grad_rim_ref, left)

    def slab(ref, e):
        return ref.at[pl.ds(pl.multiple_of(SLAB * e, SLAB), SLAB)]

    def exchange_copy(index, send, recv, peer):
        return pltpu.make_async_remote_copy(
            src_ref=slab(send, peer),
            dst_ref=slab(recv, enc),
            send_sem=slab_send.at[index],
            recv_sem=slab_recv.at[index],
            device_id=(peer, row),
            device_id_type=MESH,
        )

    def near_peers():
        for o in range(n_y // 2 - 1, 0, -1):
            ahead, behind = chip(o), chip(-o)
            for side in (0, 1):
                turned = ahead + (behind - ahead) * (core if side == 0 else 1 - core)
                for k in range(2):
                    yield 2 * turned + k
        yield sibling

    next_chip = chip(1) + (chip(-1) - chip(1)) * core
    last_chip = chip(-1) + (chip(1) - chip(-1)) * core
    far_chip = chip(n_y // 2 - 1) + (chip(n_y // 2 + 1) - chip(n_y // 2 - 1)) * core

    def relay_copy(index, send):
        pair = pl.ds(pl.multiple_of(2 * SLAB * chip(n_y // 2), 2 * SLAB), 2 * SLAB)
        return pltpu.make_async_remote_copy(
            src_ref=send.at[pair],
            dst_ref=(relay1, relay2)[index],
            send_sem=relay_send.at[index],
            recv_sem=relay_recv.at[index],
            device_id=(2 * next_chip + core, row),
            device_id_type=MESH,
        )

    def forward_copy(index, recv, k):
        origin = 2 * last_chip + core
        return pltpu.make_async_remote_copy(
            src_ref=(relay1, relay2)[index].at[pl.ds(SLAB * k, SLAB)],
            dst_ref=slab(recv, origin),
            send_sem=forward_send.at[index],
            recv_sem=slab_recv.at[index],
            device_id=(2 * far_chip + k, row),
            device_id_type=MESH,
        )

    def own_copy(index, send, recv):
        return pltpu.make_async_copy(slab(send, enc), slab(recv, enc), own_sem.at[index])

    def exchange_start(index, send, recv):
        relay_copy(index, send).start()
        for peer in near_peers():
            exchange_copy(index, send, recv, peer).start()
        own_copy(index, send, recv).start()

    def exchange_forward(index, recv):
        relay_copy(index, send1).wait_recv()
        for k in range(2):
            forward_copy(index, recv, k).start()

    def exchange_wait(index, send, recv):
        own_copy(index, send, recv).wait()
        rows_wait(recv.at[pl.ds(0, (n_enc - 1) * SLAB)], slab_recv.at[index])

    def exchange_drain(index, send):
        relay_copy(index, send).wait_send()
        rows_wait(send.at[pl.ds(0, (n_enc - 3) * SLAB)], slab_send.at[index])
        rows_wait((relay1, relay2)[index], forward_send.at[index])

    def rotate():
        fetch_patches.wait()
        turn = iota((ROWS, ROWS), 1) == ((iota((ROWS, ROWS), 0) - edge) & (ROWS - 1))
        turn_ref[...] = one_hot(turn)
        for c in range(0, D, 256):
            part = dot(turn_ref[...], patches_ref[:, c : c + 256])
            own_ref[:, c : c + 256] = part.astype(BF16)
        for copy in rims:
            copy.start()

    n_tile = D // 128

    def grads_wide(q0, q1):
        if q0 == 0:
            fetch_grads.wait()
        for t in range(q0 * n_tile, q1 * n_tile):
            slot_wide[t] = grads_ref[:, 128 * t : 128 * t + 128].astype(F32)

    def grads_move(q):
        for t in range(n_tile):
            at = q * n_tile + t
            for slot in range(4):
                part = slot_wide[at, pl.ds(slot, n_enc, stride=CAP), :]
                slab_wide[t, pl.ds(4 * slot + q, n_enc, stride=SLAB), :] = part
        for p, (off, width) in enumerate(PIECES):
            for t in range(3):
                if t < width // 128:
                    at = (q * D + off) // 128 + t
                    part = slot_wide[at, pl.ds(4, n_enc, stride=CAP), :]
                else:
                    part = jnp.zeros((n_enc, 128), F32)
                slab_wide[n_tile + t, pl.ds(4 * q + p, n_enc, stride=SLAB), :] = part

    def grads_pack():
        for t in range(SLAB_W // 128):
            send1[:, 128 * t : 128 * t + 128] = slab_wide[t].astype(BF16)

    n_tok = ROWS // 4

    def targets(code, patch):
        slot, base = code & 7, (code >> 3) * 16
        quarter = patch & 3
        target_a = jnp.where(slot < 4, base + slot * 4 + quarter, -1)
        target_b = jnp.where(slot == 4, base + quarter * 4, -8)
        return target_a, target_b

    def selector_targets():
        code_row = owner_enc_ref[...] * 8 + owner_slot_ref[...]
        square = iota((n_tok, n_tok), 0) == iota((n_tok, n_tok), 1)
        code_col = jnp.sum(jnp.where(square, code_row, 0), 1, keepdims=True)
        patch = (iota((1, ROWS), 1) - edge) & (ROWS - 1)
        tok = iota((n_tok, ROWS), 0) == (patch >> 2)
        code = jnp.sum(jnp.where(tok, code_col, 0), 0, keepdims=True)
        target_ref[0:1, :], target_ref[1:2, :] = targets(code, patch)

    def selector(p):
        bucket = iota((n_slab_rows, ROWS), 0)
        target = target_ref[0:1, :] if p == 0 else target_ref[1:2, :] + (p - 1)
        sel_ref[p] = one_hot(bucket == target)

    def selectors_back():
        code_row = owner_enc_ref[...] * 8 + owner_slot_ref[...]
        patch = (iota((ROWS, 1), 0) - edge) & (ROWS - 1)
        tok = iota((ROWS, n_tok), 1) == (patch >> 2)
        code = jnp.sum(jnp.where(tok, code_row, 0), 1, keepdims=True)
        target_a, target_b = targets(code, patch)
        bucket = iota((ROWS, n_slab_rows), 1)
        selt_ref[0] = one_hot(bucket == target_a)
        for p in range(4):
            selt_ref[1 + p] = one_hot(bucket == target_b + p)

    def piece(body, *args):
        return lambda: body(*args)

    def masks(r0, count, k0):
        i = iota((count, 128), 0) + r0
        j = iota((count, 128), 1) + k0
        first = jnp.where(row == 0, 0, -1)
        last = jnp.where(row == n_row - 1, ROWS // WIN, -1)
        ends = ((i >> 6) == first) | ((i >> 6) == last)
        i_low = jnp.where((i & (WIN - 1)) < edge, 1, 0)
        j_low = jnp.where((j & (WIN - 1)) < edge, 1, 0)
        apart = jnp.where(ends, i_low ^ j_low, 0)
        same = ((i >> 6) == (j >> 6)) & (apart == 0)
        mask_ref[r0 : r0 + count, :] = jnp.where(same, 1.0, 0.0)

    below = iota((WIN, 1), 0) < edge

    def rims_in():
        for copy in rims:
            copy.wait()
        pal_ref[:WIN, :] = jnp.where(below, rim_ref[0], own_ref[:WIN, :])
        pal_ref[WIN:ROWS, :] = own_ref[WIN:, :]
        pal_ref[ROWS:, :] = jnp.where(below, own_ref[:WIN, :], rim_ref[1])

    def rms_norm(src, dst, gain_ref, rows):
        wide = src[rows, :].astype(F32)
        inv = lax.rsqrt(jnp.mean(wide * wide, -1, keepdims=True) + EPS)
        dst[rows, :] = (wide * inv * gain_ref[...].reshape(1, D)).astype(BF16)

    def rms_back(wide, gain_ref, upstream_in):
        inv = lax.rsqrt(jnp.mean(wide * wide, -1, keepdims=True) + EPS)
        upstream = upstream_in * gain_ref[...].reshape(1, D)
        inner = jnp.mean(upstream * wide, -1, keepdims=True)
        return inv * upstream - wide * (inv * inv * inv) * inner

    def piece(body, *args):
        return lambda: body(*args)

    def project(c0, c1):
        for c in range(c0, c1, 256):
            w = min(256, c1 - c)
            part = dot(hid_ref[...], w_ref[:, c : c + w])
            qkv_ref[:, c : c + w] = part.astype(BF16)

    scale = HEAD_DIM ** (-0.5)
    pairs = range(HEADS // 2)

    def window(t, base=0):
        return slice(base + 128 * t, base + 128 * t + 256)

    def two_heads(t, value):
        lane = iota((1, 256), 1) - 32 * t
        zero = jnp.zeros_like(value)
        first = jnp.where((lane >= 0) & (lane < HEAD_DIM), value, zero)
        second = jnp.where((lane >= HEAD_DIM) & (lane < 2 * HEAD_DIM), value, zero)
        return jnp.concatenate([first, second], 0)

    def join(ref, rows, base, t, value, carry):
        low = value[:, :128] if carry is None else value[:, :128] + carry
        ref[rows, base + 128 * t : base + 128 * t + 128] = low.astype(BF16)
        high = value[:, 128:]
        if t == pairs[-1]:
            ref[rows, base + 128 * t + 128 : base + 128 * t + 256] = high.astype(BF16)
        return high

    def attend(r0, count, k0):
        rows, keys = slice(r0, r0 + count), slice(k0, k0 + 128)
        carry = None
        for t in pairs:
            scores = dot_nt(qkv_ref[rows, window(t)], two_heads(t, qkv_ref[keys, window(t, PROJ)]))
            seen = mask_ref[rows, :] > 0.5
            both = []
            for g in range(2):
                s = jnp.where(seen, scores[:, 128 * g : 128 * g + 128] * scale, -1e30)
                e = jnp.exp(s - jnp.max(s, -1, keepdims=True))
                p = e / jnp.sum(e, -1, keepdims=True)
                if r0 < ROWS:
                    prob_ref[2 * t + g, rows, :] = p
                both.append(p.astype(BF16))
            values = two_heads(t, qkv_ref[keys, window(t, 2 * PROJ)])
            carry = join(att_ref, rows, 0, t, dot(jnp.concatenate(both, 1), values), carry)

    grads_wide(0, 4)
    for q in range(4):
        grads_move(q)
    grads_pack()
    pl.semaphore_wait(barrier, n_enc + 1 + n_lower)
    tell_neighbours(ready_sem, False)
    exchange_start(0, send1, recv1)

    @pl.when(z < n_z - 1)
    def _():
        pl.semaphore_wait(ready_sem, 4 - n_lower)


    work = [piece(masks, *block) for block in BLOCKS]
    work += [rims_in, selector_targets]
    for k in range(5):
        rows = slice(k * WIN, (k + 1) * WIN)
        work += [piece(selector, k), piece(rms_norm, pal_ref, hid_ref, norm_gain_ref, rows)]
    work += [selectors_back]
    for slot in range(n_slots):
        weights_slot(slot)
        if slot == 0:
            rotate()
        elif work:
            work.pop(0)()
        if slot == 20:
            exchange_forward(0, recv1)
    assert not work
    for port in range(2):

        @pl.when(core == port)
        def _():
            spans = ((0, SPLIT), (SPLIT, 3 * PROJ))
            project(*spans[port])
            rows_wait(port_rows(1 - port), other_recv.at[0])
            project(*spans[1 - port])
            if port == 0:
                rows_wait(wo_wide, other_recv.at[1])

    for block in BLOCKS:
        attend(*block)

    @pl.loop(0, D // 256)
    def _(i):
        c = cols(i, 256)
        wo_ref[:, c] = wo_wide[:, c].astype(BF16)
        branch = dot(att_ref[...], wo_ref[:, c])
        resid_ref[:, c] = (pal_ref[:, c].astype(F32) + branch).astype(BF16)

    @pl.loop(0, AL // WIN)
    def _(i):
        rows = pl.ds(pl.multiple_of(i * WIN, WIN), WIN)
        rms_norm(resid_ref, normed_ref, merge_gain_ref, rows)

    normed_ref[:WIN, :] = jnp.where(below, normed_ref[ROWS:, :], normed_ref[:WIN, :])

    for c in range(0, D, 256):
        send2[:, c : c + 256] = dot(sel_ref[0], normed_ref[:ROWS, c : c + 256]).astype(BF16)
    head_part = jnp.zeros((n_slab_rows, 256), F32)
    tail_part = jnp.zeros((n_slab_rows, 128), F32)
    for p, (off, width) in enumerate(PIECES):
        head_part += dot(sel_ref[1 + p], normed_ref[:ROWS, off : off + 256])
        if width > 256:
            tail_part += dot(sel_ref[1 + p], normed_ref[:ROWS, off + 256 : off + width])
    send2[:, D : D + 256] = head_part.astype(BF16)
    send2[:, D + 256 :] = tail_part.astype(BF16)
    exchange_start(1, send2, recv2)

    exchange_wait(0, send1, recv1)

    def gradients(rows):
        for p, (off, width) in enumerate(PIECES):
            for c in range(0, width, 256):
                w = min(256, width - c)
                part = dot(selt_ref[0, rows], recv1[:, off + c : off + c + w])
                part += dot(selt_ref[1 + p, rows], recv1[:, D + c : D + c + w])
                ng_ref[rows, off + c : off + c + w] = part.astype(BF16)

    gradients(slice(0, WIN))
    ng_rim.start()
    gradients(slice(WIN, ROWS))

    def merge_back(rows, grad_in):
        grad = rms_back(resid_ref[rows, :].astype(F32), merge_gain_ref, grad_in.astype(F32))
        rg_ref[rows, :] = grad
        rgb_ref[rows, :] = grad.astype(BF16)

    @pl.loop(1, ROWS // WIN)
    def _(i):
        rows = pl.ds(pl.multiple_of(i * WIN, WIN), WIN)
        merge_back(rows, ng_ref[rows, :])

    ng_rim.wait()
    merge_back(slice(0, WIN), jnp.where(below, ng_rim_ref[...], ng_ref[:WIN, :]))

    exchange_forward(1, recv2)

    for c0, c1 in ((0, 256), (256, 512), (512, 640)):
        ag_ref[:, c0:c1] = dot_nt(rgb_ref[...], wo_ref[c0:c1, :]).astype(BF16)

    for r0 in (0, 128):
        rows = slice(r0, r0 + 128)
        carries = [None] * 3
        for t in pairs:
            grad = ag_ref[rows, window(t)]
            values = two_heads(t, qkv_ref[rows, window(t, 2 * PROJ)])
            keys = two_heads(t, qkv_ref[rows, window(t, PROJ)])
            dp = dot_nt(grad, values)
            probs, score_grads = [], []
            for g in range(2):
                p = prob_ref[2 * t + g, rows, :]
                dp_g = dp[:, 128 * g : 128 * g + 128]
                centred = dp_g - jnp.sum(p * dp_g, -1, keepdims=True)
                score_grads.append((p * centred * scale).astype(BF16))
                probs.append(p.astype(BF16))
            dq = dot(jnp.concatenate(score_grads, 1), keys)
            queries = two_heads(t, qkv_ref[rows, window(t)])
            dk = dot_tn(jnp.concatenate(score_grads, 0), queries)
            dv = dot_tn(jnp.concatenate(probs, 0), two_heads(t, grad))
            for k, value in enumerate((dq, dk, dv)):
                carries[k] = join(dqkvb_ref, rows, k * PROJ, t, value, carries[k])

    @pl.loop(0, D // 256)
    def _(i):
        c = cols(i, 256)
        hg_ref[:, c] = dot_nt(dqkvb_ref[...], w_ref[c, :])

    def norm_back(rows):
        grad = rms_back(pal_ref[rows, :].astype(F32), norm_gain_ref, hg_ref[rows, :])
        pal_grad_ref[rows, :] = (rg_ref[rows, :] + grad).astype(BF16)

    norm_back(slice(0, WIN))
    grad_rim.start()

    @pl.loop(1, ROWS // WIN)
    def _(i):
        norm_back(pl.ds(pl.multiple_of(i * WIN, WIN), WIN))

    grad_rim.wait()
    own_ref[:WIN, :] = jnp.where(below, grad_rim_ref[...], pal_grad_ref[:WIN, :])
    own_ref[WIN:, :] = pal_grad_ref[WIN:, :]
    for c in range(0, D, 256):
        part = dot_tn(turn_ref[...], own_ref[:, c : c + 256])
        pg_ref[:, c : c + 256] = part.astype(BF16)

    exchange_drain(0, send1)
    weights_drain()
    exchange_drain(1, send2)
    exchange_wait(1, send2, recv2)


def place_kernel(n_enc, slabs_ref, grads_ref, llm_ref, pg_ref, wide_ref, llm_wide):
    for t in range(SLAB_W // 128):
        wide_ref[t] = slabs_ref[:, 128 * t : 128 * t + 128].astype(F32)
    for q in range(4):
        for t in range(D // 128):
            at = q * (D // 128) + t
            for slot in range(4):
                part = wide_ref[t, pl.ds(4 * slot + q, n_enc, stride=SLAB), :]
                llm_wide[at, pl.ds(slot, n_enc, stride=CAP), :] = part
        for p, (off, width) in enumerate(PIECES):
            for t in range(width // 128):
                at = (q * D + off) // 128 + t
                part = wide_ref[D // 128 + t, pl.ds(4 * q + p, n_enc, stride=SLAB), :]
                llm_wide[at, pl.ds(4, n_enc, stride=CAP), :] = part
    for t in range(4 * D // 128):
        llm_ref[:, 128 * t : 128 * t + 128] = llm_wide[t].astype(BF16)
    pg_ref[...] = grads_ref[...]


def per_device(
    n_enc,
    n_x,
    n_z,
    patches,
    norm_gain,
    merge_gain,
    qkv_weight,
    out_weight,
    window_phase,
    owner_enc,
    owner_slot,
    llm_grads,
):
    n_row = n_x * n_z
    n_slot = n_enc * CAP
    vmem = pl.BlockSpec(memory_space=pltpu.VMEM)
    smem = pl.BlockSpec(memory_space=pltpu.SMEM)
    anywhere = pl.BlockSpec(memory_space=pl.ANY)
    dma = pltpu.SemaphoreType.DMA
    slabs = pltpu.VMEM((n_enc * SLAB, SLAB_W), BF16)
    slabs_in, grads_in = pl.pallas_call(
        functools.partial(kernel, n_enc, n_x, n_z),
        out_shape=(
            jax.ShapeDtypeStruct((n_enc * SLAB, SLAB_W), BF16),
            jax.ShapeDtypeStruct((ROWS, D), BF16),
        ),
        in_specs=[smem, anywhere] + [vmem] * 6 + [anywhere],
        out_specs=(anywhere, vmem),
        scratch_shapes=[
            pltpu.VMEM((ROWS, D), BF16),
            pltpu.VMEM((n_slot, 4 * D), BF16),
            *(pltpu.VMEM((n_row, 2 * SHARD, width), BF16) for width in FLOWS),
            pltpu.VMEM((D, 3 * PROJ), BF16),
            pltpu.VMEM((PROJ, D), BF16),
            pltpu.VMEM((PROJ, D), F32),
            pltpu.VMEM((ROWS, ROWS), BF16),
            pltpu.VMEM((ROWS, D), BF16),
            pltpu.VMEM((2, WIN, D), BF16),
            pltpu.VMEM((AL, D), BF16),
            pltpu.VMEM((AL, D), BF16),
            pltpu.VMEM((AL, 3 * PROJ), BF16),
            pltpu.VMEM((HEADS, ROWS, 128), F32),
            pltpu.VMEM((AL, 128), F32),
            pltpu.VMEM((AL, PROJ), BF16),
            pltpu.VMEM((AL, D), BF16),
            pltpu.VMEM((AL, D), BF16),
            pltpu.VMEM((ROWS, D), BF16),
            pltpu.VMEM((WIN, D), BF16),
            pltpu.VMEM((ROWS, D), F32),
            pltpu.VMEM((ROWS, D), BF16),
            pltpu.VMEM((ROWS, PROJ), BF16),
            pltpu.VMEM((ROWS, 3 * PROJ), BF16),
            pltpu.VMEM((ROWS, D), F32),
            pltpu.VMEM((ROWS, D), BF16),
            pltpu.VMEM((WIN, D), BF16),
            pltpu.VMEM((5, n_enc * SLAB, ROWS), BF16),
            pltpu.VMEM((5, ROWS, n_enc * SLAB), BF16),
            pltpu.VMEM((8, ROWS), jnp.int32),
            pltpu.VMEM((4 * D // 128, n_slot, 128), F32),
            pltpu.VMEM((SLAB_W // 128, n_enc * SLAB, 128), F32),
            slabs,
            slabs,
            slabs,
            pltpu.VMEM((2 * SLAB, SLAB_W), BF16),
            pltpu.VMEM((2 * SLAB, SLAB_W), BF16),
            dma((3,)),
            dma((n_row,)),
            dma((2,)),
            dma((2,)),
            dma((2,)),
            dma((4,)),
            dma((4,)),
            dma((2,)),
            dma((2,)),
            dma((2,)),
            dma((2,)),
            dma((2,)),
            pltpu.SemaphoreType.REGULAR,
        ],
        compiler_params=pltpu.CompilerParams(
            collective_id=0, has_side_effects=True, vmem_limit_bytes=56 * 1024 * 1024
        ),
        cost_estimate=pl.CostEstimate(flops=8_000_000_000, bytes_accessed=4_000_000, transcendentals=400000),
    )(
        window_phase,
        patches,
        norm_gain,
        merge_gain,
        qkv_weight,
        out_weight,
        owner_enc.reshape(1, -1),
        owner_slot.reshape(1, -1),
        llm_grads,
    )
    return pl.pallas_call(
        functools.partial(place_kernel, n_enc),
        out_shape=(
            jax.ShapeDtypeStruct((n_slot, 4 * D), BF16),
            jax.ShapeDtypeStruct((ROWS, D), BF16),
        ),
        in_specs=[vmem, vmem],
        out_specs=(vmem, vmem),
        scratch_shapes=[
            pltpu.VMEM((SLAB_W // 128, n_enc * SLAB, 128), F32),
            pltpu.VMEM((4 * D // 128, n_slot, 128), F32),
        ],
        compiler_params=pltpu.CompilerParams(vmem_limit_bytes=60 * 1024 * 1024),
        cost_estimate=pl.CostEstimate(
            flops=1_000_000, bytes_accessed=3_200_000, transcendentals=0
        ),
    )(slabs_in, grads_in)


def solution(mesh):
    n_enc, n_row = mesh.shape["enc"], mesh.shape["row"]
    n_x = 4
    in_specs = (
        P(("enc", "row"), None),
        P(),
        P(),
        P("row", None),
        P("row", None),
        P(),
        P(("enc", "row")),
        P(("enc", "row")),
        P(("enc", "row"), None),
    )
    out_specs = (P(("enc", "row"), None), P(("enc", "row"), None))
    return jax.shard_map(
        functools.partial(per_device, n_enc, n_x, n_row // n_x),
        mesh=mesh,
        in_specs=in_specs,
        out_specs=out_specs,
        check_vma=False,
    )
```

```python
import functools
import heapq

import jax
import jax.numpy as jnp
from jax import lax
from jax.experimental import pallas as pl
from jax.experimental.pallas import tpu as pltpu
from jax.sharding import PartitionSpec as P

HEADS = 8
HEAD_DIM = 80
WIN = 64
EPS = 1e-06

ROWS = 256
AL = ROWS + WIN
D = 1280
PROJ = HEADS * HEAD_DIM
CAP = 5
SHARD = 40
OUT_SHARD = 20
FLOWS = (512, 768)
SPLIT = 1024
SLAB = 16
SLAB_W = 1664
PIECES = ((0, 384), (384, 384), (768, 256), (1024, 256))
BLOCKS = ((0, 128, 0), (128, 128, 128), (256, 64, 192))
SLOT = 0.5

F32 = jnp.float32
BF16 = jnp.bfloat16
MESH = pl.DeviceIdType.MESH


def dot(a, b):
    return lax.dot_general(a, b, (((1,), (0,)), ((), ())), preferred_element_type=F32)


def dot_nt(a, b):
    return lax.dot_general(a, b, (((1,), (1,)), ((), ())), preferred_element_type=F32)


def dot_tn(a, b):
    return lax.dot_general(a, b, (((0,), (0,)), ((), ())), preferred_element_type=F32)


def iota(shape, dim):
    return lax.broadcasted_iota(jnp.int32, shape, dim)


def one_hot(cond):
    return jnp.where(cond, 1.0, 0.0).astype(BF16)


def ring_plan(n_x, n_z):
    dims = ((n_x, n_z), (n_z, n_x))
    tile_time = 0.16
    hop_time = 1.0

    def onward(port, da, db):
        size_a, size_b = dims[port]
        out = []
        if db == 0:
            for sign, reach in ((1, size_a // 2), (-1, size_a // 2 - 1)):
                gone = abs(da) if da * sign <= 0 else reach
                if gone < reach:
                    out.append((0, sign, reach - gone + size_b / 2))
        plus = size_b // 2 if da % 2 == 0 else size_b // 2 - 1
        for sign, reach in ((1, plus), (-1, size_b - 1 - plus)):
            gone = abs(db) if db * sign <= 0 else reach
            if gone < reach:
                out.append((1, sign, reach - gone))
        return out

    events = [[] for _ in FLOWS]
    free = {}
    waiting = {}
    count = 100
    agenda = [(0.0, f, f, (0, 0)) for f in range(len(FLOWS))]
    while agenda:
        now, _, flow, what = heapq.heappop(agenda)
        if len(what) == 2:
            port = flow
            if what != (0, 0):
                events[flow].append((now, count, "wait", what, None))
            for axis, sign, left in onward(port, *what):
                link = ("x" if axis == port else "z", sign)
                count += 2
                line = waiting.setdefault(link, [])
                heapq.heappush(line, (-left, count, flow, what, axis, sign, now))
                wake = max(now, free.get(link, 0.0))
                heapq.heappush(agenda, (wake, count + 10**6, flow, (link,)))
            continue
        link = what[0]
        if free.get(link, 0.0) > now + 1e-9 or not waiting[link]:
            continue
        _, _, flow, (da, db), axis, sign, ready = heapq.heappop(waiting[link])
        count += 2
        issue = max(ready, now - 1.0)
        hop = (sign, 0) if axis == 0 else (0, sign)
        events[flow].append((issue, count, "send", (da, db), hop))
        end = now + FLOWS[flow] / 64 * tile_time
        free[link] = end
        there = (da - sign, db) if axis == 0 else (da, db - sign)
        heapq.heappush(agenda, (end + hop_time, count, flow, there))
        heapq.heappush(agenda, (end, count + 10**6, flow, (link,)))
    return [sorted(flow_events) for flow_events in events]


def kernel(
    n_enc,
    n_x,
    n_z,
    phase_ref,
    patches_hbm,
    norm_gain_ref,
    merge_gain_ref,
    qkv_shard_ref,
    out_shard_ref,
    owner_enc_ref,
    owner_slot_ref,
    grads_hbm,
    recv2,
    pg_ref,
    patches_ref,
    grads_ref,
    wg0,
    wg1,
    w_ref,
    wo_ref,
    wo_wide,
    turn_ref,
    own_ref,
    rim_ref,
    pal_ref,
    hid_ref,
    qkv_ref,
    prob_ref,
    mask_ref,
    att_ref,
    resid_ref,
    normed_ref,
    ng_ref,
    ng_rim_ref,
    rg_ref,
    rgb_ref,
    ag_ref,
    dqkvb_ref,
    hg_ref,
    pal_grad_ref,
    grad_rim_ref,
    sel_ref,
    selt_ref,
    target_ref,
    slot_wide,
    slab_wide,
    send1,
    recv1,
    send2,
    relay1,
    relay2,
    stage,
    w_send,
    w_recv,
    other_recv,
    slab_send,
    slab_recv,
    rim_send,
    rim_recv,
    relay_send,
    relay_recv,
    forward_send,
    own_sem,
    fetch_sem,
    bundle_send,
    bundle_recv,
):
    n_row = n_x * n_z
    n_y = n_enc // 2
    n_slot = n_enc * CAP
    n_slab_rows = n_enc * SLAB
    enc = lax.axis_index("enc")
    row = lax.axis_index("row")
    core = lax.rem(enc, 2)
    y = enc // 2
    sibling = enc + 1 - 2 * core
    x = row // n_z
    z = lax.rem(row, n_z)
    left = lax.rem(row + n_row - 1, n_row)
    right = lax.rem(row + 1, n_row)
    phase = phase_ref[enc]
    edge = WIN - phase

    xs = [lax.rem(x + d, n_x) * n_z for d in range(n_x)]
    zs = [lax.rem(z + d, n_z) for d in range(n_z)]
    ys = [lax.rem(y + d, n_y) for d in range(n_y)]

    def xz(dx, dz):
        return xs[dx % n_x] + zs[dz % n_z]

    def chip(o):
        return ys[o % n_y]

    def cols(i, width):
        return pl.ds(pl.multiple_of(i * width, width), width)

    fetch_patches = pltpu.make_async_copy(patches_hbm, patches_ref, fetch_sem.at[0])
    fetch_grads = pltpu.make_async_copy(grads_hbm, grads_ref, fetch_sem.at[1])
    fetch_patches.start()
    fetch_grads.start()

    barrier = pltpu.get_barrier_semaphore()
    peers = [(enc, xz(1, 0)), (enc, xz(-1, 0)), (enc, xz(0, 1)), (enc, xz(0, -1))]
    peers += [(enc, left), (enc, right)]
    for peer in peers:
        pl.semaphore_signal(barrier, inc=1, device_id=peer, device_id_type=MESH)

    @pl.loop(1, n_enc)
    def _(d):
        pl.semaphore_signal(
            barrier, inc=1, device_id=(lax.rem(enc + d, n_enc), row), device_id_type=MESH
        )

    q_wide = qkv_shard_ref[...].astype(F32)
    odd_z = lax.rem(z, 2)
    odd = odd_z
    m = iota((SHARD, 1), 0)
    from_left = jnp.where(m < 16, m + 4 * odd, -1)
    from_left = jnp.where((m >= 32) & (m < 36), m - 16 - 64 * odd, from_left)
    from_left = jnp.where(m >= 36, m - 36 - 64 * (1 - odd), from_left)
    from_right = jnp.where((m >= 16) & (m < 32), m - 16 + 4 * odd, -1)
    from_right = jnp.where((m >= 32) & (m < 36), m - 32 - 64 * (1 - odd), from_right)
    from_right = jnp.where(m >= 36, m - 20 - 64 * odd, from_right)
    source = iota((SHARD, OUT_SHARD), 1)
    out40 = dot(one_hot(source == from_left), out_shard_ref[:, :PROJ]) + dot(
        one_hot(source == from_right), out_shard_ref[:, PROJ:]
    )

    def stacked(*parts):
        return jnp.concatenate(parts, 0).astype(BF16)

    wg0[row] = stacked(q_wide[:, :512], q_wide[:, 512:SPLIT])
    wg1[row] = stacked(q_wide[:, SPLIT:1792], jnp.concatenate([q_wide[:, 1792:], out40], 1))

    pl.semaphore_wait(barrier, len(peers) + n_enc - 1)

    plans = ring_plan(n_x, n_z)
    bufs = (wg0, wg1)

    def place(port, da, db):
        return xz(da, db) if port == 0 else xz(db, da)

    def block_wait(port, block):
        buf, r = bufs[port], place(port, *block)
        pltpu.make_async_copy(buf.at[r], buf.at[r], w_recv.at[r]).wait()

    def block_send(port, block, hop):
        buf, r = bufs[port], place(port, *block)
        pltpu.make_async_remote_copy(
            src_ref=buf.at[r],
            dst_ref=buf.at[r],
            send_sem=w_send.at[0],
            recv_sem=w_recv.at[r],
            device_id=(enc, place(port, *hop)),
            device_id_type=MESH,
        ).start()

    def hand_over(ref, send_sem, recv_sem):
        pltpu.make_async_remote_copy(
            src_ref=ref,
            dst_ref=ref,
            send_sem=send_sem,
            recv_sem=recv_sem,
            device_id=(sibling, row),
            device_id_type=MESH,
        ).start()

    def pack_pair(port, j):
        rows = pl.ds(pl.multiple_of(j * 2 * SHARD, 2 * SHARD), 2 * SHARD)
        out_rows = pl.ds(pl.multiple_of(j * 2 * OUT_SHARD, 8), 2 * OUT_SHARD)

        def halves(top):
            return [bufs[port][2 * j + k, top : top + SHARD, :].astype(F32) for k in range(2)]

        if port == 0:
            w_ref[rows, :512] = stacked(*halves(0))
            w_ref[rows, 512:SPLIT] = stacked(*halves(SHARD))
            hand_over(w_ref.at[rows, pl.ds(0, SPLIT)], w_send.at[1], other_recv.at[0])
            return
        w_ref[rows, SPLIT:1792] = stacked(*halves(0))
        even, odd = halves(SHARD)
        w_ref[rows, 1792:] = stacked(even[:, :128], odd[:, :128])
        hand_over(w_ref.at[rows, pl.ds(SPLIT, 3 * PROJ - SPLIT)], w_send.at[1], other_recv.at[0])
        even, odd = even[:, 128:], odd[:, 128:]
        upper = iota((8, 1), 0) < 4
        middle = jnp.where(upper, even[32:], odd[32:])
        wo_wide[out_rows, :PROJ] = jnp.concatenate([even[:16], middle, odd[:16]], 0)
        middle = pltpu.roll(jnp.where(upper, odd[32:], even[32:]), 4, 0)
        wo_wide[out_rows, PROJ:] = jnp.concatenate([even[16:32], middle, odd[16:32]], 0)
        hand_over(wo_wide.at[out_rows], w_send.at[2], other_recv.at[1])

    def rows_wait(ref, sem):
        pltpu.make_async_copy(ref, ref, sem).wait()

    def port_rows(port):
        return w_ref.at[:, pl.ds(0, SPLIT) if port == 0 else pl.ds(SPLIT, 3 * PROJ - SPLIT)]

    def slot_of(event):
        return int(event[0] / SLOT)

    n_slots = max(slot_of(plan[-1]) for plan in plans) + 1

    def pairs_after(port):
        arrival = {(0, 0): 0}
        for event in plans[port]:
            if event[2] == "wait":
                da, db = event[3]
                dx, dz = (da, db) if port == 0 else (db, da)
                arrival[dx % n_x, dz % n_z] = slot_of(event)
        found = []
        for m in range(1, n_z // 2 + 1):
            even, odd = (m - 1, -m) if m % 2 else (-m, m - 1)
            for dx in range(n_x):
                last = max(
                    arrival[dx, (start + k) % n_z] for start in (even, odd) for k in range(2)
                )
                found.append((last, dx, even, odd))
        return found

    def run_slot(port, slot):
        for event in plans[port]:
            if slot_of(event) == slot:
                _, _, kind, block, hop = event
                if kind == "wait":
                    block_wait(port, block)
                else:
                    block_send(port, block, hop)
        for last, dx, even, odd in pairs_after(port):
            if last == slot:
                first = xz(dx, even) + (xz(dx, odd) - xz(dx, even)) * odd_z
                pack_pair(port, first // 2)

    def weights_slot(slot):
        for port in range(2):
            if any(slot_of(event) == slot for event in plans[port]):

                @pl.when(core == port)
                def _():
                    run_slot(port, slot)

    def weights_drain():
        blocks = pl.ds(0, n_row - 1)
        for port in range(2):

            @pl.when(core == port)
            def _():
                rows_wait(bufs[port].at[blocks], w_send.at[0])
                rows_wait(port_rows(port), w_send.at[1])
                if port == 1:
                    rows_wait(wo_wide, w_send.at[2])

    def rim_copy(index, src, dst, target):
        return pltpu.make_async_remote_copy(
            src_ref=src,
            dst_ref=dst,
            send_sem=rim_send.at[index],
            recv_sem=rim_recv.at[index],
            device_id=(enc, target),
            device_id_type=MESH,
        )

    top = pl.ds(0, WIN)
    rims = (
        rim_copy(0, own_ref.at[top], rim_ref.at[0], right),
        rim_copy(1, own_ref.at[top], rim_ref.at[1], left),
    )
    ng_rim = rim_copy(2, ng_ref.at[top], ng_rim_ref, right)
    grad_rim = rim_copy(3, pal_grad_ref.at[top], grad_rim_ref, left)

    def slab(ref, e):
        return ref.at[pl.ds(pl.multiple_of(SLAB * e, SLAB), SLAB)]

    def exchange_copy(index, send, recv, peer):
        return pltpu.make_async_remote_copy(
            src_ref=slab(send, peer),
            dst_ref=slab(recv, enc),
            send_sem=slab_send.at[index],
            recv_sem=slab_recv.at[index],
            device_id=(peer, row),
            device_id_type=MESH,
        )

    half = n_y // 2

    def bundle(ref, c):
        return ref.at[pl.ds(pl.multiple_of(2 * SLAB * c, 2 * SLAB), 2 * SLAB)]

    def bundle_copies(index, send):
        for d in range(half - 1, 0, -1):
            up, down = chip(d), chip(-d)
            for side in range(2):
                turned = core if side == 0 else 1 - core
                target = up + (down - up) * turned
                yield pltpu.make_async_remote_copy(
                    src_ref=bundle(send, target),
                    dst_ref=stage.at[index, 2 * (half - 1 - d) + turned],
                    send_sem=bundle_send.at[index],
                    recv_sem=bundle_recv.at[index, 0 if d > 1 else 1],
                    device_id=(2 * target + core, row),
                    device_id_type=MESH,
                )

    n_stage = 2 * half - 1
    groups = (range(0, n_stage - 3), range(n_stage - 3, n_stage))

    def origin_of(b):
        if b == n_stage - 1:
            return chip(half)
        d = half - 1 - b // 2
        return chip(-d if b % 2 == 0 else d)

    next_chip = chip(1) + (chip(-1) - chip(1)) * core
    far_chip = chip(n_y // 2 - 1) + (chip(n_y // 2 + 1) - chip(n_y // 2 - 1)) * core

    def relay_copy(index, send):
        pair = pl.ds(pl.multiple_of(2 * SLAB * chip(n_y // 2), 2 * SLAB), 2 * SLAB)
        return pltpu.make_async_remote_copy(
            src_ref=send.at[pair],
            dst_ref=(relay1, relay2)[index],
            send_sem=relay_send.at[index],
            recv_sem=relay_recv.at[index],
            device_id=(2 * next_chip + core, row),
            device_id_type=MESH,
        )

    def forward_copy(index):
        return pltpu.make_async_remote_copy(
            src_ref=(relay1, relay2)[index],
            dst_ref=stage.at[index, n_stage - 1],
            send_sem=forward_send.at[index],
            recv_sem=bundle_recv.at[index, 1],
            device_id=(2 * far_chip + core, row),
            device_id_type=MESH,
        )

    def own_copy(index, send, recv):
        return pltpu.make_async_copy(slab(send, enc), slab(recv, enc), own_sem.at[index])

    def exchange_start(index, send, recv):
        relay_copy(index, send).start()
        for copy in bundle_copies(index, send):
            copy.start()
        exchange_copy(index, send, recv, sibling).start()
        own_copy(index, send, recv).start()

    def exchange_forward(index):
        relay_copy(index, send1).wait_recv()
        forward_copy(index).start()

    def exchange_collect(index, recv, group):
        first = groups[group].start
        here = stage.at[index, pl.ds(first, len(groups[group]))]
        rows_wait(here, bundle_recv.at[index, group])
        for b in groups[group]:
            origin = 2 * origin_of(b) + core

            def part(c):
                return stage.at[index, b, pl.ds(pl.multiple_of(SLAB * c, SLAB), SLAB)]

            pltpu.make_async_remote_copy(
                src_ref=part(1 - core),
                dst_ref=slab(recv, origin),
                send_sem=slab_send.at[index],
                recv_sem=slab_recv.at[index],
                device_id=(sibling, row),
                device_id_type=MESH,
            ).start()
            pltpu.make_async_copy(part(core), slab(recv, origin), own_sem.at[index]).start()

    half_rows = pl.ds(0, n_y * SLAB)

    def exchange_wait(index, recv):
        rows_wait(recv.at[half_rows], own_sem.at[index])
        rows_wait(recv.at[half_rows], slab_recv.at[index])

    def exchange_drain(index, send):
        relay_copy(index, send).wait_send()
        rows_wait(send.at[pl.ds(0, 2 * SLAB * (n_stage - 1))], bundle_send.at[index])
        rows_wait(send.at[half_rows], slab_send.at[index])
        rows_wait((relay1, relay2)[index], forward_send.at[index])

    def rotate():
        fetch_patches.wait()
        turn = iota((ROWS, ROWS), 1) == ((iota((ROWS, ROWS), 0) - edge) & (ROWS - 1))
        turn_ref[...] = one_hot(turn)
        for c in range(0, D, 256):
            part = dot(turn_ref[...], patches_ref[:, c : c + 256])
            own_ref[:, c : c + 256] = part.astype(BF16)
        for copy in rims:
            copy.start()

    n_tile = D // 128

    def grads_wide(q0, q1):
        if q0 == 0:
            fetch_grads.wait()
        for t in range(q0 * n_tile, q1 * n_tile):
            slot_wide[t] = grads_ref[:, 128 * t : 128 * t + 128].astype(F32)

    def grads_move(q):
        for t in range(n_tile):
            at = q * n_tile + t
            for slot in range(4):
                part = slot_wide[at, pl.ds(slot, n_enc, stride=CAP), :]
                slab_wide[t, pl.ds(4 * slot + q, n_enc, stride=SLAB), :] = part
        for p, (off, width) in enumerate(PIECES):
            for t in range(3):
                if t < width // 128:
                    at = (q * D + off) // 128 + t
                    part = slot_wide[at, pl.ds(4, n_enc, stride=CAP), :]
                else:
                    part = jnp.zeros((n_enc, 128), F32)
                slab_wide[n_tile + t, pl.ds(4 * q + p, n_enc, stride=SLAB), :] = part

    def grads_pack(first, last):
        for t in range(first, last):
            send1[:, 128 * t : 128 * t + 128] = slab_wide[t].astype(BF16)
        if last == SLAB_W // 128:
            exchange_start(0, send1, recv1)

    n_tok = ROWS // 4

    def targets(code, patch):
        slot, base = code & 7, (code >> 3) * 16
        quarter = patch & 3
        target_a = jnp.where(slot < 4, base + slot * 4 + quarter, -1)
        target_b = jnp.where(slot == 4, base + quarter * 4, -8)
        return target_a, target_b

    def selector_targets():
        code_row = owner_enc_ref[...] * 8 + owner_slot_ref[...]
        square = iota((n_tok, n_tok), 0) == iota((n_tok, n_tok), 1)
        code_col = jnp.sum(jnp.where(square, code_row, 0), 1, keepdims=True)
        patch = (iota((1, ROWS), 1) - edge) & (ROWS - 1)
        tok = iota((n_tok, ROWS), 0) == (patch >> 2)
        code = jnp.sum(jnp.where(tok, code_col, 0), 0, keepdims=True)
        target_ref[0:1, :], target_ref[1:2, :] = targets(code, patch)

    def selector(p):
        bucket = iota((n_slab_rows, ROWS), 0)
        target = target_ref[0:1, :] if p == 0 else target_ref[1:2, :] + (p - 1)
        sel_ref[p] = one_hot(bucket == target)

    def selectors_back():
        code_row = owner_enc_ref[...] * 8 + owner_slot_ref[...]
        patch = (iota((ROWS, 1), 0) - edge) & (ROWS - 1)
        tok = iota((ROWS, n_tok), 1) == (patch >> 2)
        code = jnp.sum(jnp.where(tok, code_row, 0), 1, keepdims=True)
        target_a, target_b = targets(code, patch)
        bucket = iota((ROWS, n_slab_rows), 1)
        selt_ref[0] = one_hot(bucket == target_a)
        for p in range(4):
            selt_ref[1 + p] = one_hot(bucket == target_b + p)

    def piece(body, *args):
        return lambda: body(*args)

    def masks(r0, count, k0):
        i = iota((count, 128), 0) + r0
        j = iota((count, 128), 1) + k0
        first = jnp.where(row == 0, 0, -1)
        last = jnp.where(row == n_row - 1, ROWS // WIN, -1)
        ends = ((i >> 6) == first) | ((i >> 6) == last)
        i_low = jnp.where((i & (WIN - 1)) < edge, 1, 0)
        j_low = jnp.where((j & (WIN - 1)) < edge, 1, 0)
        apart = jnp.where(ends, i_low ^ j_low, 0)
        same = ((i >> 6) == (j >> 6)) & (apart == 0)
        mask_ref[r0 : r0 + count, :] = jnp.where(same, 1.0, 0.0)

    below = iota((WIN, 1), 0) < edge

    def rims_in():
        for copy in rims:
            copy.wait()
        pal_ref[:WIN, :] = jnp.where(below, rim_ref[0], own_ref[:WIN, :])
        pal_ref[WIN:ROWS, :] = own_ref[WIN:, :]
        pal_ref[ROWS:, :] = jnp.where(below, own_ref[:WIN, :], rim_ref[1])

    def rms_norm(src, dst, gain_ref, rows):
        wide = src[rows, :].astype(F32)
        inv = lax.rsqrt(jnp.mean(wide * wide, -1, keepdims=True) + EPS)
        dst[rows, :] = (wide * inv * gain_ref[...].reshape(1, D)).astype(BF16)

    def rms_back(wide, gain_ref, upstream_in):
        inv = lax.rsqrt(jnp.mean(wide * wide, -1, keepdims=True) + EPS)
        upstream = upstream_in * gain_ref[...].reshape(1, D)
        inner = jnp.mean(upstream * wide, -1, keepdims=True)
        return inv * upstream - wide * (inv * inv * inv) * inner

    def piece(body, *args):
        return lambda: body(*args)

    def project(c0, c1):
        for c in range(c0, c1, 256):
            w = min(256, c1 - c)
            part = dot(hid_ref[...], w_ref[:, c : c + w])
            qkv_ref[:, c : c + w] = part.astype(BF16)

    scale = HEAD_DIM ** (-0.5)
    pairs = range(HEADS // 2)

    def window(t, base=0):
        return slice(base + 128 * t, base + 128 * t + 256)

    def two_heads(t, value):
        lane = iota((1, 256), 1) - 32 * t
        zero = jnp.zeros_like(value)
        first = jnp.where((lane >= 0) & (lane < HEAD_DIM), value, zero)
        second = jnp.where((lane >= HEAD_DIM) & (lane < 2 * HEAD_DIM), value, zero)
        return jnp.concatenate([first, second], 0)

    def join(ref, rows, base, t, value, carry):
        low = value[:, :128] if carry is None else value[:, :128] + carry
        ref[rows, base + 128 * t : base + 128 * t + 128] = low.astype(BF16)
        high = value[:, 128:]
        if t == pairs[-1]:
            ref[rows, base + 128 * t + 128 : base + 128 * t + 256] = high.astype(BF16)
        return high

    def attend(r0, count, k0):
        rows, keys = slice(r0, r0 + count), slice(k0, k0 + 128)
        carry = None
        for t in pairs:
            scores = dot_nt(qkv_ref[rows, window(t)], two_heads(t, qkv_ref[keys, window(t, PROJ)]))
            seen = mask_ref[rows, :] > 0.5
            both = []
            for g in range(2):
                s = jnp.where(seen, scores[:, 128 * g : 128 * g + 128] * scale, -1e30)
                e = jnp.exp(s - jnp.max(s, -1, keepdims=True))
                p = e / jnp.sum(e, -1, keepdims=True)
                if r0 < ROWS:
                    prob_ref[2 * t + g, rows, :] = p
                both.append(p.astype(BF16))
            values = two_heads(t, qkv_ref[keys, window(t, 2 * PROJ)])
            carry = join(att_ref, rows, 0, t, dot(jnp.concatenate(both, 1), values), carry)

    work = [piece(grads_wide, 0, 2), piece(grads_wide, 2, 4)]
    work += [piece(grads_move, q) for q in range(4)]
    work += [piece(grads_pack, 0, SLAB_W // 128)]
    work += [piece(masks, *block) for block in BLOCKS]
    work += [rims_in, selector_targets]
    for k in range(5):
        rows = slice(k * WIN, (k + 1) * WIN)
        work += [piece(selector, k), piece(rms_norm, pal_ref, hid_ref, norm_gain_ref, rows)]
    work += [selectors_back]
    for slot in range(n_slots):
        weights_slot(slot)
        if slot == 0:
            rotate()
        elif work:
            work.pop(0)()
        if slot == 20:
            exchange_forward(0)
    assert not work
    for port in range(2):

        @pl.when(core == port)
        def _():
            spans = ((0, SPLIT), (SPLIT, 3 * PROJ))
            project(*spans[port])
            rows_wait(port_rows(1 - port), other_recv.at[0])
            project(*spans[1 - port])
            if port == 0:
                rows_wait(wo_wide, other_recv.at[1])

    for block in BLOCKS:
        attend(*block)

    @pl.loop(0, D // 256)
    def _(i):
        c = cols(i, 256)
        wo_ref[:, c] = wo_wide[:, c].astype(BF16)
        branch = dot(att_ref[...], wo_ref[:, c])
        resid_ref[:, c] = (pal_ref[:, c].astype(F32) + branch).astype(BF16)

    @pl.loop(0, AL // WIN)
    def _(i):
        rows = pl.ds(pl.multiple_of(i * WIN, WIN), WIN)
        rms_norm(resid_ref, normed_ref, merge_gain_ref, rows)

    normed_ref[:WIN, :] = jnp.where(below, normed_ref[ROWS:, :], normed_ref[:WIN, :])

    for c in range(0, D, 256):
        send2[:, c : c + 256] = dot(sel_ref[0], normed_ref[:ROWS, c : c + 256]).astype(BF16)
    head_part = jnp.zeros((n_slab_rows, 256), F32)
    tail_part = jnp.zeros((n_slab_rows, 128), F32)
    for p, (off, width) in enumerate(PIECES):
        head_part += dot(sel_ref[1 + p], normed_ref[:ROWS, off : off + 256])
        if width > 256:
            tail_part += dot(sel_ref[1 + p], normed_ref[:ROWS, off + 256 : off + width])
    send2[:, D : D + 256] = head_part.astype(BF16)
    send2[:, D + 256 :] = tail_part.astype(BF16)
    exchange_start(1, send2, recv2)

    exchange_collect(0, recv1, 0)
    exchange_collect(0, recv1, 1)
    exchange_wait(0, recv1)

    def gradients(rows):
        for p, (off, width) in enumerate(PIECES):
            for c in range(0, width, 256):
                w = min(256, width - c)
                part = dot(selt_ref[0, rows], recv1[:, off + c : off + c + w])
                part += dot(selt_ref[1 + p, rows], recv1[:, D + c : D + c + w])
                ng_ref[rows, off + c : off + c + w] = part.astype(BF16)

    gradients(slice(0, WIN))
    ng_rim.start()
    gradients(slice(WIN, ROWS))

    def merge_back(rows, grad_in):
        grad = rms_back(resid_ref[rows, :].astype(F32), merge_gain_ref, grad_in.astype(F32))
        rg_ref[rows, :] = grad
        rgb_ref[rows, :] = grad.astype(BF16)

    @pl.loop(1, ROWS // WIN)
    def _(i):
        rows = pl.ds(pl.multiple_of(i * WIN, WIN), WIN)
        merge_back(rows, ng_ref[rows, :])

    ng_rim.wait()
    merge_back(slice(0, WIN), jnp.where(below, ng_rim_ref[...], ng_ref[:WIN, :]))

    exchange_forward(1)

    for c0, c1 in ((0, 256), (256, 512), (512, 640)):
        ag_ref[:, c0:c1] = dot_nt(rgb_ref[...], wo_ref[c0:c1, :]).astype(BF16)

    for r0 in (0, 128):
        rows = slice(r0, r0 + 128)
        carries = [None] * 3
        for t in pairs:
            grad = ag_ref[rows, window(t)]
            values = two_heads(t, qkv_ref[rows, window(t, 2 * PROJ)])
            keys = two_heads(t, qkv_ref[rows, window(t, PROJ)])
            dp = dot_nt(grad, values)
            probs, score_grads = [], []
            for g in range(2):
                p = prob_ref[2 * t + g, rows, :]
                dp_g = dp[:, 128 * g : 128 * g + 128]
                centred = dp_g - jnp.sum(p * dp_g, -1, keepdims=True)
                score_grads.append((p * centred * scale).astype(BF16))
                probs.append(p.astype(BF16))
            dq = dot(jnp.concatenate(score_grads, 1), keys)
            queries = two_heads(t, qkv_ref[rows, window(t)])
            dk = dot_tn(jnp.concatenate(score_grads, 0), queries)
            dv = dot_tn(jnp.concatenate(probs, 0), two_heads(t, grad))
            for k, value in enumerate((dq, dk, dv)):
                carries[k] = join(dqkvb_ref, rows, k * PROJ, t, value, carries[k])

    @pl.loop(0, D // 256)
    def _(i):
        c = cols(i, 256)
        hg_ref[:, c] = dot_nt(dqkvb_ref[...], w_ref[c, :])

    def norm_back(rows):
        grad = rms_back(pal_ref[rows, :].astype(F32), norm_gain_ref, hg_ref[rows, :])
        pal_grad_ref[rows, :] = (rg_ref[rows, :] + grad).astype(BF16)

    norm_back(slice(0, WIN))
    grad_rim.start()

    @pl.loop(1, ROWS // WIN)
    def _(i):
        norm_back(pl.ds(pl.multiple_of(i * WIN, WIN), WIN))

    exchange_collect(1, recv2, 0)
    grad_rim.wait()
    own_ref[:WIN, :] = jnp.where(below, grad_rim_ref[...], pal_grad_ref[:WIN, :])
    own_ref[WIN:, :] = pal_grad_ref[WIN:, :]
    for c in range(0, D, 256):
        part = dot_tn(turn_ref[...], own_ref[:, c : c + 256])
        pg_ref[:, c : c + 256] = part.astype(BF16)

    exchange_drain(0, send1)
    weights_drain()
    exchange_collect(1, recv2, 1)
    exchange_drain(1, send2)
    exchange_wait(1, recv2)


def place_kernel(n_enc, slabs_ref, grads_ref, llm_ref, pg_ref, wide_ref, llm_wide):
    for t in range(SLAB_W // 128):
        wide_ref[t] = slabs_ref[:, 128 * t : 128 * t + 128].astype(F32)
    for q in range(4):
        for t in range(D // 128):
            at = q * (D // 128) + t
            for slot in range(4):
                part = wide_ref[t, pl.ds(4 * slot + q, n_enc, stride=SLAB), :]
                llm_wide[at, pl.ds(slot, n_enc, stride=CAP), :] = part
        for p, (off, width) in enumerate(PIECES):
            for t in range(width // 128):
                at = (q * D + off) // 128 + t
                part = wide_ref[D // 128 + t, pl.ds(4 * q + p, n_enc, stride=SLAB), :]
                llm_wide[at, pl.ds(4, n_enc, stride=CAP), :] = part
    for t in range(4 * D // 128):
        llm_ref[:, 128 * t : 128 * t + 128] = llm_wide[t].astype(BF16)
    pg_ref[...] = grads_ref[...]


def per_device(
    n_enc,
    n_x,
    n_z,
    patches,
    norm_gain,
    merge_gain,
    qkv_weight,
    out_weight,
    window_phase,
    owner_enc,
    owner_slot,
    llm_grads,
):
    n_row = n_x * n_z
    n_slot = n_enc * CAP
    vmem = pl.BlockSpec(memory_space=pltpu.VMEM)
    smem = pl.BlockSpec(memory_space=pltpu.SMEM)
    anywhere = pl.BlockSpec(memory_space=pl.ANY)
    dma = pltpu.SemaphoreType.DMA
    slabs = pltpu.VMEM((n_enc * SLAB, SLAB_W), BF16)
    slabs_in, grads_in = pl.pallas_call(
        functools.partial(kernel, n_enc, n_x, n_z),
        out_shape=(
            jax.ShapeDtypeStruct((n_enc * SLAB, SLAB_W), BF16),
            jax.ShapeDtypeStruct((ROWS, D), BF16),
        ),
        in_specs=[smem, anywhere] + [vmem] * 6 + [anywhere],
        out_specs=(anywhere, vmem),
        scratch_shapes=[
            pltpu.VMEM((ROWS, D), BF16),
            pltpu.VMEM((n_slot, 4 * D), BF16),
            *(pltpu.VMEM((n_row, 2 * SHARD, width), BF16) for width in FLOWS),
            pltpu.VMEM((D, 3 * PROJ), BF16),
            pltpu.VMEM((PROJ, D), BF16),
            pltpu.VMEM((PROJ, D), F32),
            pltpu.VMEM((ROWS, ROWS), BF16),
            pltpu.VMEM((ROWS, D), BF16),
            pltpu.VMEM((2, WIN, D), BF16),
            pltpu.VMEM((AL, D), BF16),
            pltpu.VMEM((AL, D), BF16),
            pltpu.VMEM((AL, 3 * PROJ), BF16),
            pltpu.VMEM((HEADS, ROWS, 128), F32),
            pltpu.VMEM((AL, 128), F32),
            pltpu.VMEM((AL, PROJ), BF16),
            pltpu.VMEM((AL, D), BF16),
            pltpu.VMEM((AL, D), BF16),
            pltpu.VMEM((ROWS, D), BF16),
            pltpu.VMEM((WIN, D), BF16),
            pltpu.VMEM((ROWS, D), F32),
            pltpu.VMEM((ROWS, D), BF16),
            pltpu.VMEM((ROWS, PROJ), BF16),
            pltpu.VMEM((ROWS, 3 * PROJ), BF16),
            pltpu.VMEM((ROWS, D), F32),
            pltpu.VMEM((ROWS, D), BF16),
            pltpu.VMEM((WIN, D), BF16),
            pltpu.VMEM((5, n_enc * SLAB, ROWS), BF16),
            pltpu.VMEM((5, ROWS, n_enc * SLAB), BF16),
            pltpu.VMEM((8, ROWS), jnp.int32),
            pltpu.VMEM((4 * D // 128, n_slot, 128), F32),
            pltpu.VMEM((SLAB_W // 128, n_enc * SLAB, 128), F32),
            slabs,
            slabs,
            slabs,
            pltpu.VMEM((2 * SLAB, SLAB_W), BF16),
            pltpu.VMEM((2 * SLAB, SLAB_W), BF16),
            pltpu.VMEM((2, 2 * (n_enc // 4) - 1, 2 * SLAB, SLAB_W), BF16),
            dma((3,)),
            dma((n_row,)),
            dma((2,)),
            dma((2,)),
            dma((2,)),
            dma((4,)),
            dma((4,)),
            dma((2,)),
            dma((2,)),
            dma((2,)),
            dma((2,)),
            dma((2,)),
            dma((2,)),
            dma((2, 2)),
        ],
        compiler_params=pltpu.CompilerParams(
            collective_id=0, has_side_effects=True, vmem_limit_bytes=56 * 1024 * 1024
        ),
        cost_estimate=pl.CostEstimate(flops=8_000_000_000, bytes_accessed=4_000_000, transcendentals=400000),
    )(
        window_phase,
        patches,
        norm_gain,
        merge_gain,
        qkv_weight,
        out_weight,
        owner_enc.reshape(1, -1),
        owner_slot.reshape(1, -1),
        llm_grads,
    )
    return pl.pallas_call(
        functools.partial(place_kernel, n_enc),
        out_shape=(
            jax.ShapeDtypeStruct((n_slot, 4 * D), BF16),
            jax.ShapeDtypeStruct((ROWS, D), BF16),
        ),
        in_specs=[vmem, vmem],
        out_specs=(vmem, vmem),
        scratch_shapes=[
            pltpu.VMEM((SLAB_W // 128, n_enc * SLAB, 128), F32),
            pltpu.VMEM((4 * D // 128, n_slot, 128), F32),
        ],
        compiler_params=pltpu.CompilerParams(vmem_limit_bytes=60 * 1024 * 1024),
        cost_estimate=pl.CostEstimate(
            flops=1_000_000, bytes_accessed=3_200_000, transcendentals=0
        ),
    )(slabs_in, grads_in)


def solution(mesh):
    n_enc, n_row = mesh.shape["enc"], mesh.shape["row"]
    n_x = 4
    in_specs = (
        P(("enc", "row"), None),
        P(),
        P(),
        P("row", None),
        P("row", None),
        P(),
        P(("enc", "row")),
        P(("enc", "row")),
        P(("enc", "row"), None),
    )
    out_specs = (P(("enc", "row"), None), P(("enc", "row"), None))
    return jax.shard_map(
        functools.partial(per_device, n_enc, n_x, n_row // n_x),
        mesh=mesh,
        in_specs=in_specs,
        out_specs=out_specs,
        check_vma=False,
    )
```

```python
import functools
import heapq

import jax
import jax.numpy as jnp
from jax import lax
from jax.experimental import pallas as pl
from jax.experimental.pallas import tpu as pltpu
from jax.sharding import PartitionSpec as P

HEADS = 8
HEAD_DIM = 80
WIN = 64
EPS = 1e-06

ROWS = 256
AL = ROWS + WIN
D = 1280
PROJ = HEADS * HEAD_DIM
CAP = 5
SHARD = 40
OUT_SHARD = 20
FLOWS = (512, 768)
SPLIT = 1024
SLAB = 16
SLAB_W = 1664
PIECES = ((0, 384), (384, 384), (768, 256), (1024, 256))
BLOCKS = ((0, 128, 0), (128, 128, 128), (256, 64, 192))
PART = 16
SLOT = 0.5

F32 = jnp.float32
BF16 = jnp.bfloat16
MESH = pl.DeviceIdType.MESH


def dot(a, b):
    return lax.dot_general(a, b, (((1,), (0,)), ((), ())), preferred_element_type=F32)


def dot_nt(a, b):
    return lax.dot_general(a, b, (((1,), (1,)), ((), ())), preferred_element_type=F32)


def dot_tn(a, b):
    return lax.dot_general(a, b, (((0,), (0,)), ((), ())), preferred_element_type=F32)


def iota(shape, dim):
    return lax.broadcasted_iota(jnp.int32, shape, dim)


def one_hot(cond):
    return jnp.where(cond, 1.0, 0.0).astype(BF16)


def ring_plan(n_x, n_z):
    dims = ((n_x, n_z), (n_z, n_x))
    tile_time = 0.16
    hop_time = 1.0

    def onward(port, da, db):
        size_a, size_b = dims[port]
        out = []
        if db == 0:
            for sign, reach in ((1, size_a // 2), (-1, size_a // 2 - 1)):
                gone = abs(da) if da * sign <= 0 else reach
                if gone < reach:
                    out.append((0, sign, reach - gone + size_b / 2))
        plus = size_b // 2 if da % 2 == 0 else size_b // 2 - 1
        for sign, reach in ((1, plus), (-1, size_b - 1 - plus)):
            gone = abs(db) if db * sign <= 0 else reach
            if gone < reach:
                out.append((1, sign, reach - gone))
        return out

    events = [[] for _ in FLOWS]
    free = {}
    waiting = {}
    count = 100
    agenda = [(0.0, f, f, (0, 0)) for f in range(len(FLOWS))]
    while agenda:
        now, _, flow, what = heapq.heappop(agenda)
        if len(what) == 2:
            port = flow
            if what != (0, 0):
                events[flow].append((now, count, "wait", what, None))
            for axis, sign, left in onward(port, *what):
                link = ("x" if axis == port else "z", sign)
                count += 2
                line = waiting.setdefault(link, [])
                heapq.heappush(line, (-left, count, flow, what, axis, sign, now))
                wake = max(now, free.get(link, 0.0))
                heapq.heappush(agenda, (wake, count + 10**6, flow, (link,)))
            continue
        link = what[0]
        if free.get(link, 0.0) > now + 1e-9 or not waiting[link]:
            continue
        _, _, flow, (da, db), axis, sign, ready = heapq.heappop(waiting[link])
        count += 2
        issue = max(ready, now - 1.0)
        hop = (sign, 0) if axis == 0 else (0, sign)
        events[flow].append((issue, count, "send", (da, db), hop))
        end = now + FLOWS[flow] / 64 * tile_time
        free[link] = end
        there = (da - sign, db) if axis == 0 else (da, db - sign)
        heapq.heappush(agenda, (end + hop_time, count, flow, there))
        heapq.heappush(agenda, (end, count + 10**6, flow, (link,)))
    return [sorted(flow_events) for flow_events in events]


def kernel(
    n_enc,
    n_x,
    n_z,
    phase_ref,
    patches_hbm,
    norm_gain_ref,
    merge_gain_ref,
    qkv_shard_ref,
    out_shard_ref,
    owner_enc_ref,
    owner_slot_ref,
    grads_hbm,
    recv2,
    pg_ref,
    patches_ref,
    grads_ref,
    wg0,
    wg1,
    w_ref,
    wo_ref,
    wo_wide,
    turn_ref,
    own_ref,
    rim_ref,
    pal_ref,
    hid_ref,
    qkv_ref,
    prob_ref,
    mask_ref,
    acc_ref,
    att_ref,
    resid_ref,
    normed_ref,
    ng_ref,
    ng_rim_ref,
    rg_ref,
    rgb_ref,
    ag_ref,
    dqkv_ref,
    dqkvb_ref,
    hg_ref,
    pal_grad_ref,
    grad_rim_ref,
    sel_ref,
    selt_ref,
    target_ref,
    slot_wide,
    slab_wide,
    send1,
    recv1,
    send2,
    relay1,
    relay2,
    w_send,
    w_recv,
    other_recv,
    slab_send,
    slab_recv,
    rim_send,
    rim_recv,
    relay_send,
    relay_recv,
    forward_send,
    own_sem,
    fetch_sem,
):
    n_row = n_x * n_z
    n_y = n_enc // 2
    n_slot = n_enc * CAP
    n_slab_rows = n_enc * SLAB
    enc = lax.axis_index("enc")
    row = lax.axis_index("row")
    core = lax.rem(enc, 2)
    y = enc // 2
    sibling = enc + 1 - 2 * core
    x = row // n_z
    z = lax.rem(row, n_z)
    left = lax.rem(row + n_row - 1, n_row)
    right = lax.rem(row + 1, n_row)
    phase = phase_ref[enc]
    edge = WIN - phase

    xs = [lax.rem(x + d, n_x) * n_z for d in range(n_x)]
    zs = [lax.rem(z + d, n_z) for d in range(n_z)]
    ys = [lax.rem(y + d, n_y) for d in range(n_y)]

    def xz(dx, dz):
        return xs[dx % n_x] + zs[dz % n_z]

    def chip(o):
        return ys[o % n_y]

    def cols(i, width):
        return pl.ds(pl.multiple_of(i * width, width), width)

    fetch_patches = pltpu.make_async_copy(patches_hbm, patches_ref, fetch_sem.at[0])
    fetch_grads = pltpu.make_async_copy(grads_hbm, grads_ref, fetch_sem.at[1])
    fetch_patches.start()
    fetch_grads.start()

    barrier = pltpu.get_barrier_semaphore()
    peers = [(enc, xz(1, 0)), (enc, xz(-1, 0)), (enc, xz(0, 1)), (enc, xz(0, -1))]
    peers += [(enc, left), (enc, right)]
    for peer in peers:
        pl.semaphore_signal(barrier, inc=1, device_id=peer, device_id_type=MESH)

    @pl.loop(1, n_enc)
    def _(d):
        pl.semaphore_signal(
            barrier, inc=1, device_id=(lax.rem(enc + d, n_enc), row), device_id_type=MESH
        )

    q_wide = qkv_shard_ref[...].astype(F32)
    odd_z = lax.rem(z, 2)
    odd = odd_z
    m = iota((SHARD, 1), 0)
    from_left = jnp.where(m < 16, m + 4 * odd, -1)
    from_left = jnp.where((m >= 32) & (m < 36), m - 16 - 64 * odd, from_left)
    from_left = jnp.where(m >= 36, m - 36 - 64 * (1 - odd), from_left)
    from_right = jnp.where((m >= 16) & (m < 32), m - 16 + 4 * odd, -1)
    from_right = jnp.where((m >= 32) & (m < 36), m - 32 - 64 * (1 - odd), from_right)
    from_right = jnp.where(m >= 36, m - 20 - 64 * odd, from_right)
    source = iota((SHARD, OUT_SHARD), 1)
    out40 = dot(one_hot(source == from_left), out_shard_ref[:, :PROJ]) + dot(
        one_hot(source == from_right), out_shard_ref[:, PROJ:]
    )

    def stacked(*parts):
        return jnp.concatenate(parts, 0).astype(BF16)

    wg0[row] = stacked(q_wide[:, :512], q_wide[:, 512:SPLIT])
    wg1[row] = stacked(q_wide[:, SPLIT:1792], jnp.concatenate([q_wide[:, 1792:], out40], 1))

    pl.semaphore_wait(barrier, len(peers) + n_enc - 1)

    plans = ring_plan(n_x, n_z)
    bufs = (wg0, wg1)

    def place(port, da, db):
        return xz(da, db) if port == 0 else xz(db, da)

    def block_wait(port, block):
        buf, r = bufs[port], place(port, *block)
        pltpu.make_async_copy(buf.at[r], buf.at[r], w_recv.at[r]).wait()

    def block_send(port, block, hop):
        buf, r = bufs[port], place(port, *block)
        pltpu.make_async_remote_copy(
            src_ref=buf.at[r],
            dst_ref=buf.at[r],
            send_sem=w_send.at[0],
            recv_sem=w_recv.at[r],
            device_id=(enc, place(port, *hop)),
            device_id_type=MESH,
        ).start()

    def hand_over(ref, send_sem, recv_sem):
        pltpu.make_async_remote_copy(
            src_ref=ref,
            dst_ref=ref,
            send_sem=send_sem,
            recv_sem=recv_sem,
            device_id=(sibling, row),
            device_id_type=MESH,
        ).start()

    def pack_pair(port, j):
        rows = pl.ds(pl.multiple_of(j * 2 * SHARD, 2 * SHARD), 2 * SHARD)
        out_rows = pl.ds(pl.multiple_of(j * 2 * OUT_SHARD, 8), 2 * OUT_SHARD)

        def halves(top):
            return [bufs[port][2 * j + k, top : top + SHARD, :].astype(F32) for k in range(2)]

        if port == 0:
            w_ref[rows, :512] = stacked(*halves(0))
            w_ref[rows, 512:SPLIT] = stacked(*halves(SHARD))
            hand_over(w_ref.at[rows, pl.ds(0, SPLIT)], w_send.at[1], other_recv.at[0])
            return
        w_ref[rows, SPLIT:1792] = stacked(*halves(0))
        even, odd = halves(SHARD)
        w_ref[rows, 1792:] = stacked(even[:, :128], odd[:, :128])
        hand_over(w_ref.at[rows, pl.ds(SPLIT, 3 * PROJ - SPLIT)], w_send.at[1], other_recv.at[0])
        even, odd = even[:, 128:], odd[:, 128:]
        upper = iota((8, 1), 0) < 4
        middle = jnp.where(upper, even[32:], odd[32:])
        wo_wide[out_rows, :PROJ] = jnp.concatenate([even[:16], middle, odd[:16]], 0)
        middle = pltpu.roll(jnp.where(upper, odd[32:], even[32:]), 4, 0)
        wo_wide[out_rows, PROJ:] = jnp.concatenate([even[16:32], middle, odd[16:32]], 0)
        hand_over(wo_wide.at[out_rows], w_send.at[2], other_recv.at[1])

    def rows_wait(ref, sem):
        pltpu.make_async_copy(ref, ref, sem).wait()

    def port_rows(port):
        return w_ref.at[:, pl.ds(0, SPLIT) if port == 0 else pl.ds(SPLIT, 3 * PROJ - SPLIT)]

    def slot_of(event):
        return int(event[0] / SLOT)

    n_slots = max(slot_of(plan[-1]) for plan in plans) + 1

    def pairs_after(port):
        arrival = {(0, 0): 0}
        for event in plans[port]:
            if event[2] == "wait":
                da, db = event[3]
                dx, dz = (da, db) if port == 0 else (db, da)
                arrival[dx % n_x, dz % n_z] = slot_of(event)
        found = []
        for m in range(1, n_z // 2 + 1):
            even, odd = (m - 1, -m) if m % 2 else (-m, m - 1)
            for dx in range(n_x):
                last = max(
                    arrival[dx, (start + k) % n_z] for start in (even, odd) for k in range(2)
                )
                found.append((last, dx, even, odd))
        return found

    def run_slot(port, slot):
        for event in plans[port]:
            if slot_of(event) == slot:
                _, _, kind, block, hop = event
                if kind == "wait":
                    block_wait(port, block)
                else:
                    block_send(port, block, hop)
        for last, dx, even, odd in pairs_after(port):
            if last == slot:
                first = xz(dx, even) + (xz(dx, odd) - xz(dx, even)) * odd_z
                pack_pair(port, first // 2)

    def weights_slot(slot):
        for port in range(2):
            if any(slot_of(event) == slot for event in plans[port]):

                @pl.when(core == port)
                def _():
                    run_slot(port, slot)

    def weights_wait():
        for port in range(2):

            @pl.when(core != port)
            def _():
                rows_wait(port_rows(port), other_recv.at[0])
                if port == 1:
                    rows_wait(wo_wide, other_recv.at[1])

    def weights_drain():
        blocks = pl.ds(0, n_row - 1)
        for port in range(2):

            @pl.when(core == port)
            def _():
                rows_wait(bufs[port].at[blocks], w_send.at[0])
                rows_wait(port_rows(port), w_send.at[1])
                if port == 1:
                    rows_wait(wo_wide, w_send.at[2])

    def rim_copy(index, src, dst, target):
        return pltpu.make_async_remote_copy(
            src_ref=src,
            dst_ref=dst,
            send_sem=rim_send.at[index],
            recv_sem=rim_recv.at[index],
            device_id=(enc, target),
            device_id_type=MESH,
        )

    top = pl.ds(0, WIN)
    rims = (
        rim_copy(0, own_ref.at[top], rim_ref.at[0], right),
        rim_copy(1, own_ref.at[top], rim_ref.at[1], left),
    )
    ng_rim = rim_copy(2, ng_ref.at[top], ng_rim_ref, right)
    grad_rim = rim_copy(3, pal_grad_ref.at[top], grad_rim_ref, left)

    def slab(ref, e):
        return ref.at[pl.ds(pl.multiple_of(SLAB * e, SLAB), SLAB)]

    def exchange_copy(index, send, recv, peer):
        return pltpu.make_async_remote_copy(
            src_ref=slab(send, peer),
            dst_ref=slab(recv, enc),
            send_sem=slab_send.at[index],
            recv_sem=slab_recv.at[index],
            device_id=(peer, row),
            device_id_type=MESH,
        )

    def near_peers():
        for o in range(n_y // 2 - 1, 0, -1):
            ahead, behind = chip(o), chip(-o)
            for side in (0, 1):
                turned = ahead + (behind - ahead) * (core if side == 0 else 1 - core)
                for k in range(2):
                    yield 2 * turned + k
        yield sibling

    next_chip = chip(1) + (chip(-1) - chip(1)) * core
    last_chip = chip(-1) + (chip(1) - chip(-1)) * core
    far_chip = chip(n_y // 2 - 1) + (chip(n_y // 2 + 1) - chip(n_y // 2 - 1)) * core

    def relay_copy(index, send):
        pair = pl.ds(pl.multiple_of(2 * SLAB * chip(n_y // 2), 2 * SLAB), 2 * SLAB)
        return pltpu.make_async_remote_copy(
            src_ref=send.at[pair],
            dst_ref=(relay1, relay2)[index],
            send_sem=relay_send.at[index],
            recv_sem=relay_recv.at[index],
            device_id=(2 * next_chip + core, row),
            device_id_type=MESH,
        )

    def forward_copy(index, recv, k):
        origin = 2 * last_chip + core
        return pltpu.make_async_remote_copy(
            src_ref=(relay1, relay2)[index].at[pl.ds(SLAB * k, SLAB)],
            dst_ref=slab(recv, origin),
            send_sem=forward_send.at[index],
            recv_sem=slab_recv.at[index],
            device_id=(2 * far_chip + k, row),
            device_id_type=MESH,
        )

    def own_copy(index, send, recv):
        return pltpu.make_async_copy(slab(send, enc), slab(recv, enc), own_sem.at[index])

    def exchange_start(index, send, recv):
        relay_copy(index, send).start()
        for peer in near_peers():
            exchange_copy(index, send, recv, peer).start()
        own_copy(index, send, recv).start()

    def exchange_forward(index, recv):
        relay_copy(index, send1).wait_recv()
        for k in range(2):
            forward_copy(index, recv, k).start()

    def exchange_wait(index, send, recv):
        own_copy(index, send, recv).wait()
        rows_wait(recv.at[pl.ds(0, (n_enc - 1) * SLAB)], slab_recv.at[index])

    def exchange_drain(index, send):
        relay_copy(index, send).wait_send()
        rows_wait(send.at[pl.ds(0, (n_enc - 3) * SLAB)], slab_send.at[index])
        rows_wait((relay1, relay2)[index], forward_send.at[index])

    def rotate():
        fetch_patches.wait()
        turn = iota((ROWS, ROWS), 1) == ((iota((ROWS, ROWS), 0) - edge) & (ROWS - 1))
        turn_ref[...] = one_hot(turn)
        for c in range(0, D, 256):
            part = dot(turn_ref[...], patches_ref[:, c : c + 256])
            own_ref[:, c : c + 256] = part.astype(BF16)
        for copy in rims:
            copy.start()

    n_tile = D // 128

    def grads_wide(q0, q1):
        if q0 == 0:
            fetch_grads.wait()
        for t in range(q0 * n_tile, q1 * n_tile):
            slot_wide[t] = grads_ref[:, 128 * t : 128 * t + 128].astype(F32)

    def grads_move(q):
        for t in range(n_tile):
            at = q * n_tile + t
            for slot in range(4):
                part = slot_wide[at, pl.ds(slot, n_enc, stride=CAP), :]
                slab_wide[t, pl.ds(4 * slot + q, n_enc, stride=SLAB), :] = part
        for p, (off, width) in enumerate(PIECES):
            for t in range(3):
                if t < width // 128:
                    at = (q * D + off) // 128 + t
                    part = slot_wide[at, pl.ds(4, n_enc, stride=CAP), :]
                else:
                    part = jnp.zeros((n_enc, 128), F32)
                slab_wide[n_tile + t, pl.ds(4 * q + p, n_enc, stride=SLAB), :] = part

    def grads_pack(first, last):
        for t in range(first, last):
            send1[:, 128 * t : 128 * t + 128] = slab_wide[t].astype(BF16)
        if last == SLAB_W // 128:
            exchange_start(0, send1, recv1)

    n_tok = ROWS // 4

    def targets(code, patch):
        slot, base = code & 7, (code >> 3) * 16
        quarter = patch & 3
        target_a = jnp.where(slot < 4, base + slot * 4 + quarter, -1)
        target_b = jnp.where(slot == 4, base + quarter * 4, -8)
        return target_a, target_b

    def selector_targets():
        code_row = owner_enc_ref[...] * 8 + owner_slot_ref[...]
        square = iota((n_tok, n_tok), 0) == iota((n_tok, n_tok), 1)
        code_col = jnp.sum(jnp.where(square, code_row, 0), 1, keepdims=True)
        patch = (iota((1, ROWS), 1) - edge) & (ROWS - 1)
        tok = iota((n_tok, ROWS), 0) == (patch >> 2)
        code = jnp.sum(jnp.where(tok, code_col, 0), 0, keepdims=True)
        target_ref[0:1, :], target_ref[1:2, :] = targets(code, patch)

    def selector(p):
        bucket = iota((n_slab_rows, ROWS), 0)
        target = target_ref[0:1, :] if p == 0 else target_ref[1:2, :] + (p - 1)
        sel_ref[p] = one_hot(bucket == target)

    def selectors_back():
        code_row = owner_enc_ref[...] * 8 + owner_slot_ref[...]
        patch = (iota((ROWS, 1), 0) - edge) & (ROWS - 1)
        tok = iota((ROWS, n_tok), 1) == (patch >> 2)
        code = jnp.sum(jnp.where(tok, code_row, 0), 1, keepdims=True)
        target_a, target_b = targets(code, patch)
        bucket = iota((ROWS, n_slab_rows), 1)
        selt_ref[0] = one_hot(bucket == target_a)
        for p in range(4):
            selt_ref[1 + p] = one_hot(bucket == target_b + p)

    def piece(body, *args):
        return lambda: body(*args)

    def masks(r0, count, k0):
        i = iota((count, 128), 0) + r0
        j = iota((count, 128), 1) + k0
        first = jnp.where(row == 0, 0, -1)
        last = jnp.where(row == n_row - 1, ROWS // WIN, -1)
        ends = ((i >> 6) == first) | ((i >> 6) == last)
        i_low = jnp.where((i & (WIN - 1)) < edge, 1, 0)
        j_low = jnp.where((j & (WIN - 1)) < edge, 1, 0)
        apart = jnp.where(ends, i_low ^ j_low, 0)
        same = ((i >> 6) == (j >> 6)) & (apart == 0)
        mask_ref[r0 : r0 + count, :] = jnp.where(same, 1.0, 0.0)

    def zeros():
        acc_ref[...] = jnp.zeros_like(acc_ref)
        dqkv_ref[...] = jnp.zeros_like(dqkv_ref)

    below = iota((WIN, 1), 0) < edge

    def rims_in():
        for copy in rims:
            copy.wait()
        pal_ref[:WIN, :] = jnp.where(below, rim_ref[0], own_ref[:WIN, :])
        pal_ref[WIN:ROWS, :] = own_ref[WIN:, :]
        pal_ref[ROWS:, :] = jnp.where(below, own_ref[:WIN, :], rim_ref[1])

    def in_parts(first, body):
        for k in range(WIN // PART):
            body(pl.ds(pl.multiple_of(first + PART * k, PART), PART))

    def rms_norm(src, dst, gain_ref, first):
        def body(rows):
            wide = src[rows, :].astype(F32)
            inv = lax.rsqrt(jnp.mean(wide * wide, -1, keepdims=True) + EPS)
            dst[rows, :] = (wide * inv * gain_ref[...].reshape(1, D)).astype(BF16)

        in_parts(first, body)

    def rms_back(wide, gain_ref, upstream_in):
        inv = lax.rsqrt(jnp.mean(wide * wide, -1, keepdims=True) + EPS)
        upstream = upstream_in * gain_ref[...].reshape(1, D)
        inner = jnp.mean(upstream * wide, -1, keepdims=True)
        return inv * upstream - wide * (inv * inv * inv) * inner

    def piece(body, *args):
        return lambda: body(*args)

    def project(c0, c1):
        for c in range(c0, c1, 256):
            w = min(256, c1 - c)
            part = dot(hid_ref[...], w_ref[:, c : c + w])
            qkv_ref[:, c : c + w] = part.astype(BF16)

    scale = HEAD_DIM ** (-0.5)
    pairs = range(HEADS // 2)

    def window(t, base=0):
        return slice(base + 128 * t, base + 128 * t + 256)

    def two_heads(t, value):
        lane = iota((1, 256), 1) - 32 * t
        zero = jnp.zeros_like(value)
        first = jnp.where((lane >= 0) & (lane < HEAD_DIM), value, zero)
        second = jnp.where((lane >= HEAD_DIM) & (lane < 2 * HEAD_DIM), value, zero)
        return jnp.concatenate([first, second], 0)

    def attend(t):
        for r0, count, k0 in BLOCKS:
            rows, keys = slice(r0, r0 + count), slice(k0, k0 + 128)
            scores = dot_nt(qkv_ref[rows, window(t)], two_heads(t, qkv_ref[keys, window(t, PROJ)]))
            seen = mask_ref[rows, :] > 0.5
            both = []
            for g in range(2):
                s = jnp.where(seen, scores[:, 128 * g : 128 * g + 128] * scale, -1e30)
                e = jnp.exp(s - jnp.max(s, -1, keepdims=True))
                p = e / jnp.sum(e, -1, keepdims=True)
                if r0 < ROWS:
                    prob_ref[2 * t + g, rows, :] = p
                both.append(p.astype(BF16))
            values = two_heads(t, qkv_ref[keys, window(t, 2 * PROJ)])
            acc_ref[rows, window(t)] += dot(jnp.concatenate(both, 1), values)

    work = [piece(grads_wide, 0, 2), piece(grads_wide, 2, 4)]
    work += [piece(grads_move, q) for q in range(4)]
    work += [piece(grads_pack, 0, SLAB_W // 128)]
    work += [piece(masks, *block) for block in BLOCKS]
    work += [rims_in, selector_targets]
    for k in range(5):
        work += [piece(selector, k), piece(rms_norm, pal_ref, hid_ref, norm_gain_ref, k * WIN)]
    work += [zeros, selectors_back]
    for slot in range(n_slots):
        weights_slot(slot)
        if slot == 0:
            rotate()
        elif work:
            work.pop(0)()
        if slot == 20:
            exchange_forward(0, recv1)
    assert not work
    weights_wait()
    project(0, 3 * PROJ)
    for t in pairs:
        attend(t)

    att_ref[...] = acc_ref[...].astype(BF16)

    @pl.loop(0, D // 256)
    def _(i):
        c = cols(i, 256)
        wo_ref[:, c] = wo_wide[:, c].astype(BF16)
        branch = dot(att_ref[...], wo_ref[:, c])
        resid_ref[:, c] = (pal_ref[:, c].astype(F32) + branch).astype(BF16)

    @pl.loop(0, AL // WIN)
    def _(i):
        rms_norm(resid_ref, normed_ref, merge_gain_ref, i * WIN)

    normed_ref[:WIN, :] = jnp.where(below, normed_ref[ROWS:, :], normed_ref[:WIN, :])

    for c in range(0, D, 256):
        send2[:, c : c + 256] = dot(sel_ref[0], normed_ref[:ROWS, c : c + 256]).astype(BF16)
    head_part = jnp.zeros((n_slab_rows, 256), F32)
    tail_part = jnp.zeros((n_slab_rows, 128), F32)
    for p, (off, width) in enumerate(PIECES):
        head_part += dot(sel_ref[1 + p], normed_ref[:ROWS, off : off + 256])
        if width > 256:
            tail_part += dot(sel_ref[1 + p], normed_ref[:ROWS, off + 256 : off + width])
    send2[:, D : D + 256] = head_part.astype(BF16)
    send2[:, D + 256 :] = tail_part.astype(BF16)
    exchange_start(1, send2, recv2)

    exchange_wait(0, send1, recv1)

    def gradients(rows):
        for p, (off, width) in enumerate(PIECES):
            for c in range(0, width, 256):
                w = min(256, width - c)
                part = dot(selt_ref[0, rows], recv1[:, off + c : off + c + w])
                part += dot(selt_ref[1 + p, rows], recv1[:, D + c : D + c + w])
                ng_ref[rows, off + c : off + c + w] = part.astype(BF16)

    gradients(slice(0, WIN))
    ng_rim.start()
    gradients(slice(WIN, ROWS))

    def merge_back(rows):
        upstream = ng_ref[rows, :].astype(F32)
        grad = rms_back(resid_ref[rows, :].astype(F32), merge_gain_ref, upstream)
        rg_ref[rows, :] = grad
        rgb_ref[rows, :] = grad.astype(BF16)

    @pl.loop(1, ROWS // WIN)
    def _(i):
        in_parts(i * WIN, merge_back)

    ng_rim.wait()
    ng_ref[:WIN, :] = jnp.where(below, ng_rim_ref[...], ng_ref[:WIN, :])
    in_parts(0, merge_back)

    exchange_forward(1, recv2)

    for c0, c1 in ((0, 256), (256, 512), (512, 640)):
        ag_ref[:, c0:c1] = dot_nt(rgb_ref[...], wo_ref[c0:c1, :]).astype(BF16)

    for t in pairs:
        for r0 in (0, 128):
            rows = slice(r0, r0 + 128)
            grad = ag_ref[rows, window(t)]
            values = two_heads(t, qkv_ref[rows, window(t, 2 * PROJ)])
            keys = two_heads(t, qkv_ref[rows, window(t, PROJ)])
            dp = dot_nt(grad, values)
            probs, score_grads = [], []
            for g in range(2):
                p = prob_ref[2 * t + g, rows, :]
                dp_g = dp[:, 128 * g : 128 * g + 128]
                centred = dp_g - jnp.sum(p * dp_g, -1, keepdims=True)
                score_grads.append((p * centred * scale).astype(BF16))
                probs.append(p.astype(BF16))
            dq = dot(jnp.concatenate(score_grads, 1), keys)
            queries = two_heads(t, qkv_ref[rows, window(t)])
            dk = dot_tn(jnp.concatenate(score_grads, 0), queries)
            dv = dot_tn(jnp.concatenate(probs, 0), two_heads(t, grad))
            dqkv_ref[rows, window(t)] += dq
            dqkv_ref[rows, window(t, PROJ)] += dk
            dqkv_ref[rows, window(t, 2 * PROJ)] += dv

    dqkvb_ref[...] = dqkv_ref[...].astype(BF16)

    @pl.loop(0, D // 256)
    def _(i):
        c = cols(i, 256)
        hg_ref[:, c] = dot_nt(dqkvb_ref[...], w_ref[c, :])

    def norm_back(rows):
        grad = rms_back(pal_ref[rows, :].astype(F32), norm_gain_ref, hg_ref[rows, :])
        pal_grad_ref[rows, :] = (rg_ref[rows, :] + grad).astype(BF16)

    in_parts(0, norm_back)
    grad_rim.start()

    @pl.loop(1, ROWS // WIN)
    def _(i):
        in_parts(i * WIN, norm_back)

    exchange_drain(0, send1)
    weights_drain()

    grad_rim.wait()
    own_ref[:WIN, :] = jnp.where(below, grad_rim_ref[...], pal_grad_ref[:WIN, :])
    own_ref[WIN:, :] = pal_grad_ref[WIN:, :]
    for c in range(0, D, 256):
        part = dot_tn(turn_ref[...], own_ref[:, c : c + 256])
        pg_ref[:, c : c + 256] = part.astype(BF16)

    exchange_drain(1, send2)
    exchange_wait(1, send2, recv2)


def place_kernel(n_enc, slabs_ref, grads_ref, llm_ref, pg_ref, wide_ref, llm_wide):
    for t in range(SLAB_W // 128):
        wide_ref[t] = slabs_ref[:, 128 * t : 128 * t + 128].astype(F32)
    for q in range(4):
        for t in range(D // 128):
            at = q * (D // 128) + t
            for slot in range(4):
                part = wide_ref[t, pl.ds(4 * slot + q, n_enc, stride=SLAB), :]
                llm_wide[at, pl.ds(slot, n_enc, stride=CAP), :] = part
        for p, (off, width) in enumerate(PIECES):
            for t in range(width // 128):
                at = (q * D + off) // 128 + t
                part = wide_ref[D // 128 + t, pl.ds(4 * q + p, n_enc, stride=SLAB), :]
                llm_wide[at, pl.ds(4, n_enc, stride=CAP), :] = part
    for t in range(4 * D // 128):
        llm_ref[:, 128 * t : 128 * t + 128] = llm_wide[t].astype(BF16)
    pg_ref[...] = grads_ref[...]


def per_device(
    n_enc,
    n_x,
    n_z,
    patches,
    norm_gain,
    merge_gain,
    qkv_weight,
    out_weight,
    window_phase,
    owner_enc,
    owner_slot,
    llm_grads,
):
    n_row = n_x * n_z
    n_slot = n_enc * CAP
    vmem = pl.BlockSpec(memory_space=pltpu.VMEM)
    smem = pl.BlockSpec(memory_space=pltpu.SMEM)
    anywhere = pl.BlockSpec(memory_space=pl.ANY)
    dma = pltpu.SemaphoreType.DMA
    slabs = pltpu.VMEM((n_enc * SLAB, SLAB_W), BF16)
    slabs_in, grads_in = pl.pallas_call(
        functools.partial(kernel, n_enc, n_x, n_z),
        out_shape=(
            jax.ShapeDtypeStruct((n_enc * SLAB, SLAB_W), BF16),
            jax.ShapeDtypeStruct((ROWS, D), BF16),
        ),
        in_specs=[smem, anywhere] + [vmem] * 6 + [anywhere],
        out_specs=(anywhere, vmem),
        scratch_shapes=[
            pltpu.VMEM((ROWS, D), BF16),
            pltpu.VMEM((n_slot, 4 * D), BF16),
            *(pltpu.VMEM((n_row, 2 * SHARD, width), BF16) for width in FLOWS),
            pltpu.VMEM((D, 3 * PROJ), BF16),
            pltpu.VMEM((PROJ, D), BF16),
            pltpu.VMEM((PROJ, D), F32),
            pltpu.VMEM((ROWS, ROWS), BF16),
            pltpu.VMEM((ROWS, D), BF16),
            pltpu.VMEM((2, WIN, D), BF16),
            pltpu.VMEM((AL, D), BF16),
            pltpu.VMEM((AL, D), BF16),
            pltpu.VMEM((AL, 3 * PROJ), BF16),
            pltpu.VMEM((HEADS, ROWS, 128), F32),
            pltpu.VMEM((AL, 128), F32),
            pltpu.VMEM((AL, PROJ), F32),
            pltpu.VMEM((AL, PROJ), BF16),
            pltpu.VMEM((AL, D), BF16),
            pltpu.VMEM((AL, D), BF16),
            pltpu.VMEM((ROWS, D), BF16),
            pltpu.VMEM((WIN, D), BF16),
            pltpu.VMEM((ROWS, D), F32),
            pltpu.VMEM((ROWS, D), BF16),
            pltpu.VMEM((ROWS, PROJ), BF16),
            pltpu.VMEM((ROWS, 3 * PROJ), F32),
            pltpu.VMEM((ROWS, 3 * PROJ), BF16),
            pltpu.VMEM((ROWS, D), F32),
            pltpu.VMEM((ROWS, D), BF16),
            pltpu.VMEM((WIN, D), BF16),
            pltpu.VMEM((5, n_enc * SLAB, ROWS), BF16),
            pltpu.VMEM((5, ROWS, n_enc * SLAB), BF16),
            pltpu.VMEM((8, ROWS), jnp.int32),
            pltpu.VMEM((4 * D // 128, n_slot, 128), F32),
            pltpu.VMEM((SLAB_W // 128, n_enc * SLAB, 128), F32),
            slabs,
            slabs,
            slabs,
            pltpu.VMEM((2 * SLAB, SLAB_W), BF16),
            pltpu.VMEM((2 * SLAB, SLAB_W), BF16),
            dma((3,)),
            dma((n_row,)),
            dma((2,)),
            dma((2,)),
            dma((2,)),
            dma((4,)),
            dma((4,)),
            dma((2,)),
            dma((2,)),
            dma((2,)),
            dma((2,)),
            dma((2,)),
        ],
        compiler_params=pltpu.CompilerParams(
            collective_id=0, has_side_effects=True, vmem_limit_bytes=56 * 1024 * 1024
        ),
        cost_estimate=pl.CostEstimate(flops=8_000_000_000, bytes_accessed=4_000_000, transcendentals=400000),
    )(
        window_phase,
        patches,
        norm_gain,
        merge_gain,
        qkv_weight,
        out_weight,
        owner_enc.reshape(1, -1),
        owner_slot.reshape(1, -1),
        llm_grads,
    )
    return pl.pallas_call(
        functools.partial(place_kernel, n_enc),
        out_shape=(
            jax.ShapeDtypeStruct((n_slot, 4 * D), BF16),
            jax.ShapeDtypeStruct((ROWS, D), BF16),
        ),
        in_specs=[vmem, vmem],
        out_specs=(vmem, vmem),
        scratch_shapes=[
            pltpu.VMEM((SLAB_W // 128, n_enc * SLAB, 128), F32),
            pltpu.VMEM((4 * D // 128, n_slot, 128), F32),
        ],
        compiler_params=pltpu.CompilerParams(vmem_limit_bytes=60 * 1024 * 1024),
        cost_estimate=pl.CostEstimate(
            flops=1_000_000, bytes_accessed=3_200_000, transcendentals=0
        ),
    )(slabs_in, grads_in)


def solution(mesh):
    n_enc, n_row = mesh.shape["enc"], mesh.shape["row"]
    n_x = 4
    in_specs = (
        P(("enc", "row"), None),
        P(),
        P(),
        P("row", None),
        P("row", None),
        P(),
        P(("enc", "row")),
        P(("enc", "row")),
        P(("enc", "row"), None),
    )
    out_specs = (P(("enc", "row"), None), P(("enc", "row"), None))
    return jax.shard_map(
        functools.partial(per_device, n_enc, n_x, n_row // n_x),
        mesh=mesh,
        in_specs=in_specs,
        out_specs=out_specs,
        check_vma=False,
    )
```

```python
import functools
import heapq

import jax
import jax.numpy as jnp
from jax import lax
from jax.experimental import pallas as pl
from jax.experimental.pallas import tpu as pltpu
from jax.sharding import PartitionSpec as P

HEADS = 8
HEAD_DIM = 80
WIN = 64
EPS = 1e-06

ROWS = 256
AL = ROWS + WIN
D = 1280
PROJ = HEADS * HEAD_DIM
CAP = 5
SHARD = 40
OUT_SHARD = 20
FLOWS = (512, 768)
SPLIT = 1024
SLAB = 16
SLAB_W = 1664
PIECES = ((0, 384), (384, 384), (768, 256), (1024, 256))
BLOCKS = ((0, 128, 0), (128, 128, 128), (256, 64, 192))
PART = 16
SLOT = 0.5

F32 = jnp.float32
BF16 = jnp.bfloat16
MESH = pl.DeviceIdType.MESH


def dot(a, b):
    return lax.dot_general(a, b, (((1,), (0,)), ((), ())), preferred_element_type=F32)


def dot_nt(a, b):
    return lax.dot_general(a, b, (((1,), (1,)), ((), ())), preferred_element_type=F32)


def dot_tn(a, b):
    return lax.dot_general(a, b, (((0,), (0,)), ((), ())), preferred_element_type=F32)


def iota(shape, dim):
    return lax.broadcasted_iota(jnp.int32, shape, dim)


def one_hot(cond):
    return jnp.where(cond, 1.0, 0.0).astype(BF16)


def ring_plan(n_x, n_z):
    dims = ((n_x, n_z), (n_z, n_x))
    tile_time = 0.16
    hop_time = 1.0

    def onward(port, da, db):
        size_a, size_b = dims[port]
        out = []
        if db == 0:
            for sign, reach in ((1, size_a // 2), (-1, size_a // 2 - 1)):
                gone = abs(da) if da * sign <= 0 else reach
                if gone < reach:
                    out.append((0, sign, reach - gone + size_b / 2))
        plus = size_b // 2 if da % 2 == 0 else size_b // 2 - 1
        for sign, reach in ((1, plus), (-1, size_b - 1 - plus)):
            gone = abs(db) if db * sign <= 0 else reach
            if gone < reach:
                out.append((1, sign, reach - gone))
        return out

    events = [[] for _ in FLOWS]
    free = {}
    waiting = {}
    count = 100
    agenda = [(0.0, f, f, (0, 0)) for f in range(len(FLOWS))]
    while agenda:
        now, _, flow, what = heapq.heappop(agenda)
        if len(what) == 2:
            port = flow
            if what != (0, 0):
                events[flow].append((now, count, "wait", what, None))
            for axis, sign, left in onward(port, *what):
                link = ("x" if axis == port else "z", sign)
                count += 2
                line = waiting.setdefault(link, [])
                heapq.heappush(line, (-left, count, flow, what, axis, sign, now))
                wake = max(now, free.get(link, 0.0))
                heapq.heappush(agenda, (wake, count + 10**6, flow, (link,)))
            continue
        link = what[0]
        if free.get(link, 0.0) > now + 1e-9 or not waiting[link]:
            continue
        _, _, flow, (da, db), axis, sign, ready = heapq.heappop(waiting[link])
        count += 2
        issue = max(ready, now - 1.0)
        hop = (sign, 0) if axis == 0 else (0, sign)
        events[flow].append((issue, count, "send", (da, db), hop))
        end = now + FLOWS[flow] / 64 * tile_time
        free[link] = end
        there = (da - sign, db) if axis == 0 else (da, db - sign)
        heapq.heappush(agenda, (end + hop_time, count, flow, there))
        heapq.heappush(agenda, (end, count + 10**6, flow, (link,)))
    return [sorted(flow_events) for flow_events in events]


def kernel(
    n_enc,
    n_x,
    n_z,
    phase_ref,
    patches_hbm,
    norm_gain_ref,
    merge_gain_ref,
    qkv_shard_ref,
    out_shard_ref,
    owner_enc_ref,
    owner_slot_ref,
    grads_hbm,
    recv2,
    pg_ref,
    patches_ref,
    grads_ref,
    wg0,
    wg1,
    w_ref,
    wo_ref,
    wo_wide,
    turn_ref,
    own_ref,
    rim_ref,
    pal_ref,
    hid_ref,
    qkv_ref,
    prob_ref,
    mask_ref,
    att_ref,
    resid_ref,
    normed_ref,
    ng_ref,
    ng_rim_ref,
    rg_ref,
    rgb_ref,
    ag_ref,
    dqkvb_ref,
    hg_ref,
    pal_grad_ref,
    grad_rim_ref,
    sel_ref,
    selt_ref,
    target_ref,
    slot_wide,
    slab_wide,
    send1,
    recv1,
    send2,
    relay1,
    relay2,
    w_send,
    w_recv,
    other_recv,
    slab_send,
    slab_recv,
    rim_send,
    rim_recv,
    relay_send,
    relay_recv,
    forward_send,
    own_sem,
    fetch_sem,
):
    n_row = n_x * n_z
    n_y = n_enc // 2
    n_slot = n_enc * CAP
    n_slab_rows = n_enc * SLAB
    enc = lax.axis_index("enc")
    row = lax.axis_index("row")
    core = lax.rem(enc, 2)
    y = enc // 2
    sibling = enc + 1 - 2 * core
    x = row // n_z
    z = lax.rem(row, n_z)
    left = lax.rem(row + n_row - 1, n_row)
    right = lax.rem(row + 1, n_row)
    phase = phase_ref[enc]
    edge = WIN - phase

    xs = [lax.rem(x + d, n_x) * n_z for d in range(n_x)]
    zs = [lax.rem(z + d, n_z) for d in range(n_z)]
    ys = [lax.rem(y + d, n_y) for d in range(n_y)]

    def xz(dx, dz):
        return xs[dx % n_x] + zs[dz % n_z]

    def chip(o):
        return ys[o % n_y]

    def cols(i, width):
        return pl.ds(pl.multiple_of(i * width, width), width)

    fetch_patches = pltpu.make_async_copy(patches_hbm, patches_ref, fetch_sem.at[0])
    fetch_grads = pltpu.make_async_copy(grads_hbm, grads_ref, fetch_sem.at[1])
    fetch_patches.start()
    fetch_grads.start()

    barrier = pltpu.get_barrier_semaphore()
    peers = [(enc, xz(1, 0)), (enc, xz(-1, 0)), (enc, xz(0, 1)), (enc, xz(0, -1))]
    peers += [(enc, left), (enc, right)]
    for peer in peers:
        pl.semaphore_signal(barrier, inc=1, device_id=peer, device_id_type=MESH)

    @pl.loop(1, n_enc)
    def _(d):
        pl.semaphore_signal(
            barrier, inc=1, device_id=(lax.rem(enc + d, n_enc), row), device_id_type=MESH
        )

    q_wide = qkv_shard_ref[...].astype(F32)
    odd_z = lax.rem(z, 2)
    odd = odd_z
    m = iota((SHARD, 1), 0)
    from_left = jnp.where(m < 16, m + 4 * odd, -1)
    from_left = jnp.where((m >= 32) & (m < 36), m - 16 - 64 * odd, from_left)
    from_left = jnp.where(m >= 36, m - 36 - 64 * (1 - odd), from_left)
    from_right = jnp.where((m >= 16) & (m < 32), m - 16 + 4 * odd, -1)
    from_right = jnp.where((m >= 32) & (m < 36), m - 32 - 64 * (1 - odd), from_right)
    from_right = jnp.where(m >= 36, m - 20 - 64 * odd, from_right)
    source = iota((SHARD, OUT_SHARD), 1)
    out40 = dot(one_hot(source == from_left), out_shard_ref[:, :PROJ]) + dot(
        one_hot(source == from_right), out_shard_ref[:, PROJ:]
    )

    def stacked(*parts):
        return jnp.concatenate(parts, 0).astype(BF16)

    wg0[row] = stacked(q_wide[:, :512], q_wide[:, 512:SPLIT])
    wg1[row] = stacked(q_wide[:, SPLIT:1792], jnp.concatenate([q_wide[:, 1792:], out40], 1))

    pl.semaphore_wait(barrier, len(peers) + n_enc - 1)

    plans = ring_plan(n_x, n_z)
    bufs = (wg0, wg1)

    def place(port, da, db):
        return xz(da, db) if port == 0 else xz(db, da)

    def block_wait(port, block):
        buf, r = bufs[port], place(port, *block)
        pltpu.make_async_copy(buf.at[r], buf.at[r], w_recv.at[r]).wait()

    def block_send(port, block, hop):
        buf, r = bufs[port], place(port, *block)
        pltpu.make_async_remote_copy(
            src_ref=buf.at[r],
            dst_ref=buf.at[r],
            send_sem=w_send.at[0],
            recv_sem=w_recv.at[r],
            device_id=(enc, place(port, *hop)),
            device_id_type=MESH,
        ).start()

    def hand_over(ref, send_sem, recv_sem):
        pltpu.make_async_remote_copy(
            src_ref=ref,
            dst_ref=ref,
            send_sem=send_sem,
            recv_sem=recv_sem,
            device_id=(sibling, row),
            device_id_type=MESH,
        ).start()

    def pack_pair(port, j):
        rows = pl.ds(pl.multiple_of(j * 2 * SHARD, 2 * SHARD), 2 * SHARD)
        out_rows = pl.ds(pl.multiple_of(j * 2 * OUT_SHARD, 8), 2 * OUT_SHARD)

        def halves(top):
            return [bufs[port][2 * j + k, top : top + SHARD, :].astype(F32) for k in range(2)]

        if port == 0:
            w_ref[rows, :512] = stacked(*halves(0))
            w_ref[rows, 512:SPLIT] = stacked(*halves(SHARD))
            hand_over(w_ref.at[rows, pl.ds(0, SPLIT)], w_send.at[1], other_recv.at[0])
            return
        w_ref[rows, SPLIT:1792] = stacked(*halves(0))
        even, odd = halves(SHARD)
        w_ref[rows, 1792:] = stacked(even[:, :128], odd[:, :128])
        hand_over(w_ref.at[rows, pl.ds(SPLIT, 3 * PROJ - SPLIT)], w_send.at[1], other_recv.at[0])
        even, odd = even[:, 128:], odd[:, 128:]
        upper = iota((8, 1), 0) < 4
        middle = jnp.where(upper, even[32:], odd[32:])
        wo_wide[out_rows, :PROJ] = jnp.concatenate([even[:16], middle, odd[:16]], 0)
        middle = pltpu.roll(jnp.where(upper, odd[32:], even[32:]), 4, 0)
        wo_wide[out_rows, PROJ:] = jnp.concatenate([even[16:32], middle, odd[16:32]], 0)
        hand_over(wo_wide.at[out_rows], w_send.at[2], other_recv.at[1])

    def rows_wait(ref, sem):
        pltpu.make_async_copy(ref, ref, sem).wait()

    def port_rows(port):
        return w_ref.at[:, pl.ds(0, SPLIT) if port == 0 else pl.ds(SPLIT, 3 * PROJ - SPLIT)]

    def slot_of(event):
        return int(event[0] / SLOT)

    n_slots = max(slot_of(plan[-1]) for plan in plans) + 1

    def pairs_after(port):
        arrival = {(0, 0): 0}
        for event in plans[port]:
            if event[2] == "wait":
                da, db = event[3]
                dx, dz = (da, db) if port == 0 else (db, da)
                arrival[dx % n_x, dz % n_z] = slot_of(event)
        found = []
        for m in range(1, n_z // 2 + 1):
            even, odd = (m - 1, -m) if m % 2 else (-m, m - 1)
            for dx in range(n_x):
                last = max(
                    arrival[dx, (start + k) % n_z] for start in (even, odd) for k in range(2)
                )
                found.append((last, dx, even, odd))
        return found

    def run_slot(port, slot):
        for event in plans[port]:
            if slot_of(event) == slot:
                _, _, kind, block, hop = event
                if kind == "wait":
                    block_wait(port, block)
                else:
                    block_send(port, block, hop)
        for last, dx, even, odd in pairs_after(port):
            if last == slot:
                first = xz(dx, even) + (xz(dx, odd) - xz(dx, even)) * odd_z
                pack_pair(port, first // 2)

    def weights_slot(slot):
        for port in range(2):
            if any(slot_of(event) == slot for event in plans[port]):

                @pl.when(core == port)
                def _():
                    run_slot(port, slot)

    def weights_drain():
        blocks = pl.ds(0, n_row - 1)
        for port in range(2):

            @pl.when(core == port)
            def _():
                rows_wait(bufs[port].at[blocks], w_send.at[0])
                rows_wait(port_rows(port), w_send.at[1])
                if port == 1:
                    rows_wait(wo_wide, w_send.at[2])

    def rim_copy(index, src, dst, target):
        return pltpu.make_async_remote_copy(
            src_ref=src,
            dst_ref=dst,
            send_sem=rim_send.at[index],
            recv_sem=rim_recv.at[index],
            device_id=(enc, target),
            device_id_type=MESH,
        )

    top = pl.ds(0, WIN)
    rims = (
        rim_copy(0, own_ref.at[top], rim_ref.at[0], right),
        rim_copy(1, own_ref.at[top], rim_ref.at[1], left),
    )
    ng_rim = rim_copy(2, ng_ref.at[top], ng_rim_ref, right)
    grad_rim = rim_copy(3, pal_grad_ref.at[top], grad_rim_ref, left)

    def slab(ref, e):
        return ref.at[pl.ds(pl.multiple_of(SLAB * e, SLAB), SLAB)]

    def exchange_copy(index, send, recv, peer):
        return pltpu.make_async_remote_copy(
            src_ref=slab(send, peer),
            dst_ref=slab(recv, enc),
            send_sem=slab_send.at[index],
            recv_sem=slab_recv.at[index],
            device_id=(peer, row),
            device_id_type=MESH,
        )

    def near_peers():
        for o in range(n_y // 2 - 1, 0, -1):
            ahead, behind = chip(o), chip(-o)
            for side in (0, 1):
                turned = ahead + (behind - ahead) * (core if side == 0 else 1 - core)
                for k in range(2):
                    yield 2 * turned + k
        yield sibling

    next_chip = chip(1) + (chip(-1) - chip(1)) * core
    last_chip = chip(-1) + (chip(1) - chip(-1)) * core
    far_chip = chip(n_y // 2 - 1) + (chip(n_y // 2 + 1) - chip(n_y // 2 - 1)) * core

    def relay_copy(index, send):
        pair = pl.ds(pl.multiple_of(2 * SLAB * chip(n_y // 2), 2 * SLAB), 2 * SLAB)
        return pltpu.make_async_remote_copy(
            src_ref=send.at[pair],
            dst_ref=(relay1, relay2)[index],
            send_sem=relay_send.at[index],
            recv_sem=relay_recv.at[index],
            device_id=(2 * next_chip + core, row),
            device_id_type=MESH,
        )

    def forward_copy(index, recv, k):
        origin = 2 * last_chip + core
        return pltpu.make_async_remote_copy(
            src_ref=(relay1, relay2)[index].at[pl.ds(SLAB * k, SLAB)],
            dst_ref=slab(recv, origin),
            send_sem=forward_send.at[index],
            recv_sem=slab_recv.at[index],
            device_id=(2 * far_chip + k, row),
            device_id_type=MESH,
        )

    def own_copy(index, send, recv):
        return pltpu.make_async_copy(slab(send, enc), slab(recv, enc), own_sem.at[index])

    def exchange_start(index, send, recv):
        relay_copy(index, send).start()
        for peer in near_peers():
            exchange_copy(index, send, recv, peer).start()
        own_copy(index, send, recv).start()

    def exchange_forward(index, recv):
        relay_copy(index, send1).wait_recv()
        for k in range(2):
            forward_copy(index, recv, k).start()

    def exchange_wait(index, send, recv):
        own_copy(index, send, recv).wait()
        rows_wait(recv.at[pl.ds(0, (n_enc - 1) * SLAB)], slab_recv.at[index])

    def exchange_drain(index, send):
        relay_copy(index, send).wait_send()
        rows_wait(send.at[pl.ds(0, (n_enc - 3) * SLAB)], slab_send.at[index])
        rows_wait((relay1, relay2)[index], forward_send.at[index])

    def rotate():
        fetch_patches.wait()
        turn = iota((ROWS, ROWS), 1) == ((iota((ROWS, ROWS), 0) - edge) & (ROWS - 1))
        turn_ref[...] = one_hot(turn)
        for c in range(0, D, 256):
            part = dot(turn_ref[...], patches_ref[:, c : c + 256])
            own_ref[:, c : c + 256] = part.astype(BF16)
        for copy in rims:
            copy.start()

    n_tile = D // 128

    def grads_wide(q0, q1):
        if q0 == 0:
            fetch_grads.wait()
        for t in range(q0 * n_tile, q1 * n_tile):
            slot_wide[t] = grads_ref[:, 128 * t : 128 * t + 128].astype(F32)

    def grads_move(q):
        for t in range(n_tile):
            at = q * n_tile + t
            for slot in range(4):
                part = slot_wide[at, pl.ds(slot, n_enc, stride=CAP), :]
                slab_wide[t, pl.ds(4 * slot + q, n_enc, stride=SLAB), :] = part
        for p, (off, width) in enumerate(PIECES):
            for t in range(3):
                if t < width // 128:
                    at = (q * D + off) // 128 + t
                    part = slot_wide[at, pl.ds(4, n_enc, stride=CAP), :]
                else:
                    part = jnp.zeros((n_enc, 128), F32)
                slab_wide[n_tile + t, pl.ds(4 * q + p, n_enc, stride=SLAB), :] = part

    def grads_pack(first, last):
        for t in range(first, last):
            send1[:, 128 * t : 128 * t + 128] = slab_wide[t].astype(BF16)
        if last == SLAB_W // 128:
            exchange_start(0, send1, recv1)

    n_tok = ROWS // 4

    def targets(code, patch):
        slot, base = code & 7, (code >> 3) * 16
        quarter = patch & 3
        target_a = jnp.where(slot < 4, base + slot * 4 + quarter, -1)
        target_b = jnp.where(slot == 4, base + quarter * 4, -8)
        return target_a, target_b

    def selector_targets():
        code_row = owner_enc_ref[...] * 8 + owner_slot_ref[...]
        square = iota((n_tok, n_tok), 0) == iota((n_tok, n_tok), 1)
        code_col = jnp.sum(jnp.where(square, code_row, 0), 1, keepdims=True)
        patch = (iota((1, ROWS), 1) - edge) & (ROWS - 1)
        tok = iota((n_tok, ROWS), 0) == (patch >> 2)
        code = jnp.sum(jnp.where(tok, code_col, 0), 0, keepdims=True)
        target_ref[0:1, :], target_ref[1:2, :] = targets(code, patch)

    def selector(p):
        bucket = iota((n_slab_rows, ROWS), 0)
        target = target_ref[0:1, :] if p == 0 else target_ref[1:2, :] + (p - 1)
        sel_ref[p] = one_hot(bucket == target)

    def selectors_back():
        code_row = owner_enc_ref[...] * 8 + owner_slot_ref[...]
        patch = (iota((ROWS, 1), 0) - edge) & (ROWS - 1)
        tok = iota((ROWS, n_tok), 1) == (patch >> 2)
        code = jnp.sum(jnp.where(tok, code_row, 0), 1, keepdims=True)
        target_a, target_b = targets(code, patch)
        bucket = iota((ROWS, n_slab_rows), 1)
        selt_ref[0] = one_hot(bucket == target_a)
        for p in range(4):
            selt_ref[1 + p] = one_hot(bucket == target_b + p)

    def piece(body, *args):
        return lambda: body(*args)

    def masks(r0, count, k0):
        i = iota((count, 128), 0) + r0
        j = iota((count, 128), 1) + k0
        first = jnp.where(row == 0, 0, -1)
        last = jnp.where(row == n_row - 1, ROWS // WIN, -1)
        ends = ((i >> 6) == first) | ((i >> 6) == last)
        i_low = jnp.where((i & (WIN - 1)) < edge, 1, 0)
        j_low = jnp.where((j & (WIN - 1)) < edge, 1, 0)
        apart = jnp.where(ends, i_low ^ j_low, 0)
        same = ((i >> 6) == (j >> 6)) & (apart == 0)
        mask_ref[r0 : r0 + count, :] = jnp.where(same, 1.0, 0.0)

    below = iota((WIN, 1), 0) < edge

    def rims_in():
        for copy in rims:
            copy.wait()
        pal_ref[:WIN, :] = jnp.where(below, rim_ref[0], own_ref[:WIN, :])
        pal_ref[WIN:ROWS, :] = own_ref[WIN:, :]
        pal_ref[ROWS:, :] = jnp.where(below, own_ref[:WIN, :], rim_ref[1])

    def in_parts(first, body):
        for k in range(WIN // PART):
            body(pl.ds(pl.multiple_of(first + PART * k, PART), PART))

    def rms_norm(src, dst, gain_ref, first):
        def body(rows):
            wide = src[rows, :].astype(F32)
            inv = lax.rsqrt(jnp.mean(wide * wide, -1, keepdims=True) + EPS)
            dst[rows, :] = (wide * inv * gain_ref[...].reshape(1, D)).astype(BF16)

        in_parts(first, body)

    def rms_back(wide, gain_ref, upstream_in):
        inv = lax.rsqrt(jnp.mean(wide * wide, -1, keepdims=True) + EPS)
        upstream = upstream_in * gain_ref[...].reshape(1, D)
        inner = jnp.mean(upstream * wide, -1, keepdims=True)
        return inv * upstream - wide * (inv * inv * inv) * inner

    def piece(body, *args):
        return lambda: body(*args)

    def project(c0, c1):
        for c in range(c0, c1, 256):
            w = min(256, c1 - c)
            part = dot(hid_ref[...], w_ref[:, c : c + w])
            qkv_ref[:, c : c + w] = part.astype(BF16)

    scale = HEAD_DIM ** (-0.5)
    pairs = range(HEADS // 2)

    def window(t, base=0):
        return slice(base + 128 * t, base + 128 * t + 256)

    def two_heads(t, value):
        lane = iota((1, 256), 1) - 32 * t
        zero = jnp.zeros_like(value)
        first = jnp.where((lane >= 0) & (lane < HEAD_DIM), value, zero)
        second = jnp.where((lane >= HEAD_DIM) & (lane < 2 * HEAD_DIM), value, zero)
        return jnp.concatenate([first, second], 0)

    def join(ref, rows, base, t, value, carry):
        low = value[:, :128] if carry is None else value[:, :128] + carry
        ref[rows, base + 128 * t : base + 128 * t + 128] = low.astype(BF16)
        high = value[:, 128:]
        if t == pairs[-1]:
            ref[rows, base + 128 * t + 128 : base + 128 * t + 256] = high.astype(BF16)
        return high

    carried = [None] * len(BLOCKS)

    def attend(t):
        for b, (r0, count, k0) in enumerate(BLOCKS):
            rows, keys = slice(r0, r0 + count), slice(k0, k0 + 128)
            scores = dot_nt(qkv_ref[rows, window(t)], two_heads(t, qkv_ref[keys, window(t, PROJ)]))
            seen = mask_ref[rows, :] > 0.5
            both = []
            for g in range(2):
                s = jnp.where(seen, scores[:, 128 * g : 128 * g + 128] * scale, -1e30)
                e = jnp.exp(s - jnp.max(s, -1, keepdims=True))
                p = e / jnp.sum(e, -1, keepdims=True)
                if r0 < ROWS:
                    prob_ref[2 * t + g, rows, :] = p
                both.append(p.astype(BF16))
            values = two_heads(t, qkv_ref[keys, window(t, 2 * PROJ)])
            mixed = dot(jnp.concatenate(both, 1), values)
            carried[b] = join(att_ref, rows, 0, t, mixed, carried[b])

    work = [piece(grads_wide, 0, 2), piece(grads_wide, 2, 4)]
    work += [piece(grads_move, q) for q in range(4)]
    work += [piece(grads_pack, 0, SLAB_W // 128)]
    work += [piece(masks, *block) for block in BLOCKS]
    work += [rims_in, selector_targets]
    for k in range(5):
        work += [piece(selector, k), piece(rms_norm, pal_ref, hid_ref, norm_gain_ref, k * WIN)]
    work += [selectors_back]
    for slot in range(n_slots):
        weights_slot(slot)
        if slot == 0:
            rotate()
        elif work:
            work.pop(0)()
        if slot == 20:
            exchange_forward(0, recv1)
    assert not work
    for port in range(2):

        @pl.when(core == port)
        def _():
            spans = ((0, SPLIT), (SPLIT, 3 * PROJ))
            project(*spans[port])
            rows_wait(port_rows(1 - port), other_recv.at[0])
            project(*spans[1 - port])
            if port == 0:
                rows_wait(wo_wide, other_recv.at[1])

    for t in pairs:
        attend(t)


    @pl.loop(0, D // 256)
    def _(i):
        c = cols(i, 256)
        wo_ref[:, c] = wo_wide[:, c].astype(BF16)
        branch = dot(att_ref[...], wo_ref[:, c])
        resid_ref[:, c] = (pal_ref[:, c].astype(F32) + branch).astype(BF16)

    @pl.loop(0, AL // WIN)
    def _(i):
        rms_norm(resid_ref, normed_ref, merge_gain_ref, i * WIN)

    normed_ref[:WIN, :] = jnp.where(below, normed_ref[ROWS:, :], normed_ref[:WIN, :])

    for c in range(0, D, 256):
        send2[:, c : c + 256] = dot(sel_ref[0], normed_ref[:ROWS, c : c + 256]).astype(BF16)
    head_part = jnp.zeros((n_slab_rows, 256), F32)
    tail_part = jnp.zeros((n_slab_rows, 128), F32)
    for p, (off, width) in enumerate(PIECES):
        head_part += dot(sel_ref[1 + p], normed_ref[:ROWS, off : off + 256])
        if width > 256:
            tail_part += dot(sel_ref[1 + p], normed_ref[:ROWS, off + 256 : off + width])
    send2[:, D : D + 256] = head_part.astype(BF16)
    send2[:, D + 256 :] = tail_part.astype(BF16)
    exchange_start(1, send2, recv2)

    exchange_wait(0, send1, recv1)

    def gradients(rows):
        for p, (off, width) in enumerate(PIECES):
            for c in range(0, width, 256):
                w = min(256, width - c)
                part = dot(selt_ref[0, rows], recv1[:, off + c : off + c + w])
                part += dot(selt_ref[1 + p, rows], recv1[:, D + c : D + c + w])
                ng_ref[rows, off + c : off + c + w] = part.astype(BF16)

    gradients(slice(0, WIN))
    ng_rim.start()
    gradients(slice(WIN, ROWS))

    def merge_back(rows):
        upstream = ng_ref[rows, :].astype(F32)
        grad = rms_back(resid_ref[rows, :].astype(F32), merge_gain_ref, upstream)
        rg_ref[rows, :] = grad
        rgb_ref[rows, :] = grad.astype(BF16)

    @pl.loop(1, ROWS // WIN)
    def _(i):
        in_parts(i * WIN, merge_back)

    ng_rim.wait()
    ng_ref[:WIN, :] = jnp.where(below, ng_rim_ref[...], ng_ref[:WIN, :])
    in_parts(0, merge_back)

    exchange_forward(1, recv2)

    for c0, c1 in ((0, 256), (256, 512), (512, 640)):
        ag_ref[:, c0:c1] = dot_nt(rgb_ref[...], wo_ref[c0:c1, :]).astype(BF16)

    carries = {}
    for t in pairs:
        for r0 in (0, 128):
            rows = slice(r0, r0 + 128)
            grad = ag_ref[rows, window(t)]
            values = two_heads(t, qkv_ref[rows, window(t, 2 * PROJ)])
            keys = two_heads(t, qkv_ref[rows, window(t, PROJ)])
            dp = dot_nt(grad, values)
            probs, score_grads = [], []
            for g in range(2):
                p = prob_ref[2 * t + g, rows, :]
                dp_g = dp[:, 128 * g : 128 * g + 128]
                centred = dp_g - jnp.sum(p * dp_g, -1, keepdims=True)
                score_grads.append((p * centred * scale).astype(BF16))
                probs.append(p.astype(BF16))
            dq = dot(jnp.concatenate(score_grads, 1), keys)
            queries = two_heads(t, qkv_ref[rows, window(t)])
            dk = dot_tn(jnp.concatenate(score_grads, 0), queries)
            dv = dot_tn(jnp.concatenate(probs, 0), two_heads(t, grad))
            for k, value in enumerate((dq, dk, dv)):
                key = (r0, k)
                carries[key] = join(dqkvb_ref, rows, k * PROJ, t, value, carries.get(key))

    @pl.loop(0, D // 256)
    def _(i):
        c = cols(i, 256)
        hg_ref[:, c] = dot_nt(dqkvb_ref[...], w_ref[c, :])

    def norm_back(rows):
        grad = rms_back(pal_ref[rows, :].astype(F32), norm_gain_ref, hg_ref[rows, :])
        pal_grad_ref[rows, :] = (rg_ref[rows, :] + grad).astype(BF16)

    in_parts(0, norm_back)
    grad_rim.start()

    @pl.loop(1, ROWS // WIN)
    def _(i):
        in_parts(i * WIN, norm_back)

    exchange_drain(0, send1)
    weights_drain()

    grad_rim.wait()
    own_ref[:WIN, :] = jnp.where(below, grad_rim_ref[...], pal_grad_ref[:WIN, :])
    own_ref[WIN:, :] = pal_grad_ref[WIN:, :]
    for c in range(0, D, 256):
        part = dot_tn(turn_ref[...], own_ref[:, c : c + 256])
        pg_ref[:, c : c + 256] = part.astype(BF16)

    exchange_drain(1, send2)
    exchange_wait(1, send2, recv2)


def place_kernel(n_enc, slabs_ref, grads_ref, llm_ref, pg_ref, wide_ref, llm_wide):
    for t in range(SLAB_W // 128):
        wide_ref[t] = slabs_ref[:, 128 * t : 128 * t + 128].astype(F32)
    for q in range(4):
        for t in range(D // 128):
            at = q * (D // 128) + t
            for slot in range(4):
                part = wide_ref[t, pl.ds(4 * slot + q, n_enc, stride=SLAB), :]
                llm_wide[at, pl.ds(slot, n_enc, stride=CAP), :] = part
        for p, (off, width) in enumerate(PIECES):
            for t in range(width // 128):
                at = (q * D + off) // 128 + t
                part = wide_ref[D // 128 + t, pl.ds(4 * q + p, n_enc, stride=SLAB), :]
                llm_wide[at, pl.ds(4, n_enc, stride=CAP), :] = part
    for t in range(4 * D // 128):
        llm_ref[:, 128 * t : 128 * t + 128] = llm_wide[t].astype(BF16)
    pg_ref[...] = grads_ref[...]


def per_device(
    n_enc,
    n_x,
    n_z,
    patches,
    norm_gain,
    merge_gain,
    qkv_weight,
    out_weight,
    window_phase,
    owner_enc,
    owner_slot,
    llm_grads,
):
    n_row = n_x * n_z
    n_slot = n_enc * CAP
    vmem = pl.BlockSpec(memory_space=pltpu.VMEM)
    smem = pl.BlockSpec(memory_space=pltpu.SMEM)
    anywhere = pl.BlockSpec(memory_space=pl.ANY)
    dma = pltpu.SemaphoreType.DMA
    slabs = pltpu.VMEM((n_enc * SLAB, SLAB_W), BF16)
    slabs_in, grads_in = pl.pallas_call(
        functools.partial(kernel, n_enc, n_x, n_z),
        out_shape=(
            jax.ShapeDtypeStruct((n_enc * SLAB, SLAB_W), BF16),
            jax.ShapeDtypeStruct((ROWS, D), BF16),
        ),
        in_specs=[smem, anywhere] + [vmem] * 6 + [anywhere],
        out_specs=(anywhere, vmem),
        scratch_shapes=[
            pltpu.VMEM((ROWS, D), BF16),
            pltpu.VMEM((n_slot, 4 * D), BF16),
            *(pltpu.VMEM((n_row, 2 * SHARD, width), BF16) for width in FLOWS),
            pltpu.VMEM((D, 3 * PROJ), BF16),
            pltpu.VMEM((PROJ, D), BF16),
            pltpu.VMEM((PROJ, D), F32),
            pltpu.VMEM((ROWS, ROWS), BF16),
            pltpu.VMEM((ROWS, D), BF16),
            pltpu.VMEM((2, WIN, D), BF16),
            pltpu.VMEM((AL, D), BF16),
            pltpu.VMEM((AL, D), BF16),
            pltpu.VMEM((AL, 3 * PROJ), BF16),
            pltpu.VMEM((HEADS, ROWS, 128), F32),
            pltpu.VMEM((AL, 128), F32),
            pltpu.VMEM((AL, PROJ), BF16),
            pltpu.VMEM((AL, D), BF16),
            pltpu.VMEM((AL, D), BF16),
            pltpu.VMEM((ROWS, D), BF16),
            pltpu.VMEM((WIN, D), BF16),
            pltpu.VMEM((ROWS, D), F32),
            pltpu.VMEM((ROWS, D), BF16),
            pltpu.VMEM((ROWS, PROJ), BF16),
            pltpu.VMEM((ROWS, 3 * PROJ), BF16),
            pltpu.VMEM((ROWS, D), F32),
            pltpu.VMEM((ROWS, D), BF16),
            pltpu.VMEM((WIN, D), BF16),
            pltpu.VMEM((5, n_enc * SLAB, ROWS), BF16),
            pltpu.VMEM((5, ROWS, n_enc * SLAB), BF16),
            pltpu.VMEM((8, ROWS), jnp.int32),
            pltpu.VMEM((4 * D // 128, n_slot, 128), F32),
            pltpu.VMEM((SLAB_W // 128, n_enc * SLAB, 128), F32),
            slabs,
            slabs,
            slabs,
            pltpu.VMEM((2 * SLAB, SLAB_W), BF16),
            pltpu.VMEM((2 * SLAB, SLAB_W), BF16),
            dma((3,)),
            dma((n_row,)),
            dma((2,)),
            dma((2,)),
            dma((2,)),
            dma((4,)),
            dma((4,)),
            dma((2,)),
            dma((2,)),
            dma((2,)),
            dma((2,)),
            dma((2,)),
        ],
        compiler_params=pltpu.CompilerParams(
            collective_id=0, has_side_effects=True, vmem_limit_bytes=56 * 1024 * 1024
        ),
        cost_estimate=pl.CostEstimate(flops=8_000_000_000, bytes_accessed=4_000_000, transcendentals=400000),
    )(
        window_phase,
        patches,
        norm_gain,
        merge_gain,
        qkv_weight,
        out_weight,
        owner_enc.reshape(1, -1),
        owner_slot.reshape(1, -1),
        llm_grads,
    )
    return pl.pallas_call(
        functools.partial(place_kernel, n_enc),
        out_shape=(
            jax.ShapeDtypeStruct((n_slot, 4 * D), BF16),
            jax.ShapeDtypeStruct((ROWS, D), BF16),
        ),
        in_specs=[vmem, vmem],
        out_specs=(vmem, vmem),
        scratch_shapes=[
            pltpu.VMEM((SLAB_W // 128, n_enc * SLAB, 128), F32),
            pltpu.VMEM((4 * D // 128, n_slot, 128), F32),
        ],
        compiler_params=pltpu.CompilerParams(vmem_limit_bytes=60 * 1024 * 1024),
        cost_estimate=pl.CostEstimate(
            flops=1_000_000, bytes_accessed=3_200_000, transcendentals=0
        ),
    )(slabs_in, grads_in)


def solution(mesh):
    n_enc, n_row = mesh.shape["enc"], mesh.shape["row"]
    n_x = 4
    in_specs = (
        P(("enc", "row"), None),
        P(),
        P(),
        P("row", None),
        P("row", None),
        P(),
        P(("enc", "row")),
        P(("enc", "row")),
        P(("enc", "row"), None),
    )
    out_specs = (P(("enc", "row"), None), P(("enc", "row"), None))
    return jax.shard_map(
        functools.partial(per_device, n_enc, n_x, n_row // n_x),
        mesh=mesh,
        in_specs=in_specs,
        out_specs=out_specs,
        check_vma=False,
    )
```

```python
import functools
import heapq

import jax
import jax.numpy as jnp
from jax import lax
from jax.experimental import pallas as pl
from jax.experimental.pallas import tpu as pltpu
from jax.sharding import PartitionSpec as P

HEADS = 8
HEAD_DIM = 80
WIN = 64
EPS = 1e-06

ROWS = 256
AL = ROWS + WIN
D = 1280
PROJ = HEADS * HEAD_DIM
CAP = 5
SHARD = 40
OUT_SHARD = 20
FLOWS = (512, 768)
SPLIT = 1024
SLAB = 16
SLAB_W = 1664
PIECES = ((0, 384), (384, 384), (768, 256), (1024, 256))
BLOCKS = ((0, 128, 0), (128, 128, 128), (256, 64, 192))
PART = 16
SLOT = 0.5

F32 = jnp.float32
BF16 = jnp.bfloat16
MESH = pl.DeviceIdType.MESH


def dot(a, b):
    return lax.dot_general(a, b, (((1,), (0,)), ((), ())), preferred_element_type=F32)


def dot_nt(a, b):
    return lax.dot_general(a, b, (((1,), (1,)), ((), ())), preferred_element_type=F32)


def dot_tn(a, b):
    return lax.dot_general(a, b, (((0,), (0,)), ((), ())), preferred_element_type=F32)


def iota(shape, dim):
    return lax.broadcasted_iota(jnp.int32, shape, dim)


def one_hot(cond):
    return jnp.where(cond, 1.0, 0.0).astype(BF16)


def ring_plan(n_x, n_z):
    dims = ((n_x, n_z), (n_z, n_x))
    tile_time = 0.16
    hop_time = 1.0

    def onward(port, da, db):
        size_a, size_b = dims[port]
        out = []
        if db == 0:
            for sign, reach in ((1, size_a // 2), (-1, size_a // 2 - 1)):
                gone = abs(da) if da * sign <= 0 else reach
                if gone < reach:
                    out.append((0, sign, reach - gone + size_b / 2))
        plus = size_b // 2 if da % 2 == 0 else size_b // 2 - 1
        for sign, reach in ((1, plus), (-1, size_b - 1 - plus)):
            gone = abs(db) if db * sign <= 0 else reach
            if gone < reach:
                out.append((1, sign, reach - gone))
        return out

    events = [[] for _ in FLOWS]
    free = {}
    waiting = {}
    count = 100
    agenda = [(0.0, f, f, (0, 0)) for f in range(len(FLOWS))]
    while agenda:
        now, _, flow, what = heapq.heappop(agenda)
        if len(what) == 2:
            port = flow
            if what != (0, 0):
                events[flow].append((now, count, "wait", what, None))
            for axis, sign, left in onward(port, *what):
                link = ("x" if axis == port else "z", sign)
                count += 2
                line = waiting.setdefault(link, [])
                heapq.heappush(line, (-left, count, flow, what, axis, sign, now))
                wake = max(now, free.get(link, 0.0))
                heapq.heappush(agenda, (wake, count + 10**6, flow, (link,)))
            continue
        link = what[0]
        if free.get(link, 0.0) > now + 1e-9 or not waiting[link]:
            continue
        _, _, flow, (da, db), axis, sign, ready = heapq.heappop(waiting[link])
        count += 2
        issue = max(ready, now - 1.0)
        hop = (sign, 0) if axis == 0 else (0, sign)
        events[flow].append((issue, count, "send", (da, db), hop))
        end = now + FLOWS[flow] / 64 * tile_time
        free[link] = end
        there = (da - sign, db) if axis == 0 else (da, db - sign)
        heapq.heappush(agenda, (end + hop_time, count, flow, there))
        heapq.heappush(agenda, (end, count + 10**6, flow, (link,)))
    return [sorted(flow_events) for flow_events in events]


def kernel(
    n_enc,
    n_x,
    n_z,
    phase_ref,
    patches_hbm,
    norm_gain_ref,
    merge_gain_ref,
    qkv_shard_ref,
    out_shard_ref,
    owner_enc_ref,
    owner_slot_ref,
    grads_hbm,
    recv2,
    pg_ref,
    patches_ref,
    grads_ref,
    wg0,
    wg1,
    w_ref,
    wo_ref,
    wo_wide,
    turn_ref,
    own_ref,
    rim_ref,
    pal_ref,
    hid_ref,
    qkv_ref,
    prob_ref,
    mask_ref,
    acc_ref,
    att_ref,
    resid_ref,
    normed_ref,
    ng_ref,
    ng_rim_ref,
    rg_ref,
    rgb_ref,
    ag_ref,
    dqkv_ref,
    dqkvb_ref,
    hg_ref,
    pal_grad_ref,
    grad_rim_ref,
    sel_ref,
    selt_ref,
    target_ref,
    slot_wide,
    slab_wide,
    send1,
    recv1,
    send2,
    relay1,
    relay2,
    w_send,
    w_recv,
    other_recv,
    slab_send,
    slab_recv,
    rim_send,
    rim_recv,
    relay_send,
    relay_recv,
    forward_send,
    own_sem,
    fetch_sem,
):
    n_row = n_x * n_z
    n_y = n_enc // 2
    n_slot = n_enc * CAP
    n_slab_rows = n_enc * SLAB
    enc = lax.axis_index("enc")
    row = lax.axis_index("row")
    core = lax.rem(enc, 2)
    y = enc // 2
    sibling = enc + 1 - 2 * core
    x = row // n_z
    z = lax.rem(row, n_z)
    left = lax.rem(row + n_row - 1, n_row)
    right = lax.rem(row + 1, n_row)
    phase = phase_ref[enc]
    edge = WIN - phase

    xs = [lax.rem(x + d, n_x) * n_z for d in range(n_x)]
    zs = [lax.rem(z + d, n_z) for d in range(n_z)]
    ys = [lax.rem(y + d, n_y) for d in range(n_y)]

    def xz(dx, dz):
        return xs[dx % n_x] + zs[dz % n_z]

    def chip(o):
        return ys[o % n_y]

    def cols(i, width):
        return pl.ds(pl.multiple_of(i * width, width), width)

    fetch_patches = pltpu.make_async_copy(patches_hbm, patches_ref, fetch_sem.at[0])
    fetch_grads = pltpu.make_async_copy(grads_hbm, grads_ref, fetch_sem.at[1])
    fetch_patches.start()
    fetch_grads.start()

    barrier = pltpu.get_barrier_semaphore()
    peers = [(enc, xz(1, 0)), (enc, xz(-1, 0)), (enc, xz(0, 1)), (enc, xz(0, -1))]
    peers += [(enc, left), (enc, right)]
    for peer in peers:
        pl.semaphore_signal(barrier, inc=1, device_id=peer, device_id_type=MESH)

    @pl.loop(1, n_enc)
    def _(d):
        pl.semaphore_signal(
            barrier, inc=1, device_id=(lax.rem(enc + d, n_enc), row), device_id_type=MESH
        )

    q_wide = qkv_shard_ref[...].astype(F32)
    odd_z = lax.rem(z, 2)
    odd = odd_z
    m = iota((SHARD, 1), 0)
    from_left = jnp.where(m < 16, m + 4 * odd, -1)
    from_left = jnp.where((m >= 32) & (m < 36), m - 16 - 64 * odd, from_left)
    from_left = jnp.where(m >= 36, m - 36 - 64 * (1 - odd), from_left)
    from_right = jnp.where((m >= 16) & (m < 32), m - 16 + 4 * odd, -1)
    from_right = jnp.where((m >= 32) & (m < 36), m - 32 - 64 * (1 - odd), from_right)
    from_right = jnp.where(m >= 36, m - 20 - 64 * odd, from_right)
    source = iota((SHARD, OUT_SHARD), 1)
    out40 = dot(one_hot(source == from_left), out_shard_ref[:, :PROJ]) + dot(
        one_hot(source == from_right), out_shard_ref[:, PROJ:]
    )

    def stacked(*parts):
        return jnp.concatenate(parts, 0).astype(BF16)

    wg0[row] = stacked(q_wide[:, :512], q_wide[:, 512:SPLIT])
    wg1[row] = stacked(q_wide[:, SPLIT:1792], jnp.concatenate([q_wide[:, 1792:], out40], 1))

    pl.semaphore_wait(barrier, len(peers) + n_enc - 1)

    plans = ring_plan(n_x, n_z)
    bufs = (wg0, wg1)

    def place(port, da, db):
        return xz(da, db) if port == 0 else xz(db, da)

    def block_wait(port, block):
        buf, r = bufs[port], place(port, *block)
        pltpu.make_async_copy(buf.at[r], buf.at[r], w_recv.at[r]).wait()

    def block_send(port, block, hop):
        buf, r = bufs[port], place(port, *block)
        pltpu.make_async_remote_copy(
            src_ref=buf.at[r],
            dst_ref=buf.at[r],
            send_sem=w_send.at[0],
            recv_sem=w_recv.at[r],
            device_id=(enc, place(port, *hop)),
            device_id_type=MESH,
        ).start()

    def hand_over(ref, send_sem, recv_sem):
        pltpu.make_async_remote_copy(
            src_ref=ref,
            dst_ref=ref,
            send_sem=send_sem,
            recv_sem=recv_sem,
            device_id=(sibling, row),
            device_id_type=MESH,
        ).start()

    def pack_pair(port, j):
        rows = pl.ds(pl.multiple_of(j * 2 * SHARD, 2 * SHARD), 2 * SHARD)
        out_rows = pl.ds(pl.multiple_of(j * 2 * OUT_SHARD, 8), 2 * OUT_SHARD)

        def halves(top):
            return [bufs[port][2 * j + k, top : top + SHARD, :].astype(F32) for k in range(2)]

        if port == 0:
            w_ref[rows, :512] = stacked(*halves(0))
            w_ref[rows, 512:SPLIT] = stacked(*halves(SHARD))
            hand_over(w_ref.at[rows, pl.ds(0, SPLIT)], w_send.at[1], other_recv.at[0])
            return
        w_ref[rows, SPLIT:1792] = stacked(*halves(0))
        even, odd = halves(SHARD)
        w_ref[rows, 1792:] = stacked(even[:, :128], odd[:, :128])
        hand_over(w_ref.at[rows, pl.ds(SPLIT, 3 * PROJ - SPLIT)], w_send.at[1], other_recv.at[0])
        even, odd = even[:, 128:], odd[:, 128:]
        upper = iota((8, 1), 0) < 4
        middle = jnp.where(upper, even[32:], odd[32:])
        wo_wide[out_rows, :PROJ] = jnp.concatenate([even[:16], middle, odd[:16]], 0)
        middle = pltpu.roll(jnp.where(upper, odd[32:], even[32:]), 4, 0)
        wo_wide[out_rows, PROJ:] = jnp.concatenate([even[16:32], middle, odd[16:32]], 0)
        hand_over(wo_wide.at[out_rows], w_send.at[2], other_recv.at[1])

    def rows_wait(ref, sem):
        pltpu.make_async_copy(ref, ref, sem).wait()

    def port_rows(port):
        return w_ref.at[:, pl.ds(0, SPLIT) if port == 0 else pl.ds(SPLIT, 3 * PROJ - SPLIT)]

    def slot_of(event):
        return int(event[0] / SLOT)

    n_slots = max(slot_of(plan[-1]) for plan in plans) + 1

    def pairs_after(port):
        arrival = {(0, 0): 0}
        for event in plans[port]:
            if event[2] == "wait":
                da, db = event[3]
                dx, dz = (da, db) if port == 0 else (db, da)
                arrival[dx % n_x, dz % n_z] = slot_of(event)
        found = []
        for m in range(1, n_z // 2 + 1):
            even, odd = (m - 1, -m) if m % 2 else (-m, m - 1)
            for dx in range(n_x):
                last = max(
                    arrival[dx, (start + k) % n_z] for start in (even, odd) for k in range(2)
                )
                found.append((last, dx, even, odd))
        return found

    def run_slot(port, slot):
        for event in plans[port]:
            if slot_of(event) == slot:
                _, _, kind, block, hop = event
                if kind == "wait":
                    block_wait(port, block)
                else:
                    block_send(port, block, hop)
        for last, dx, even, odd in pairs_after(port):
            if last == slot:
                first = xz(dx, even) + (xz(dx, odd) - xz(dx, even)) * odd_z
                pack_pair(port, first // 2)

    def weights_slot(slot):
        for port in range(2):
            if any(slot_of(event) == slot for event in plans[port]):

                @pl.when(core == port)
                def _():
                    run_slot(port, slot)

    def weights_wait():
        for port in range(2):

            @pl.when(core != port)
            def _():
                rows_wait(port_rows(port), other_recv.at[0])
                if port == 1:
                    rows_wait(wo_wide, other_recv.at[1])

    def weights_drain():
        blocks = pl.ds(0, n_row - 1)
        for port in range(2):

            @pl.when(core == port)
            def _():
                rows_wait(bufs[port].at[blocks], w_send.at[0])
                rows_wait(port_rows(port), w_send.at[1])
                if port == 1:
                    rows_wait(wo_wide, w_send.at[2])

    def rim_copy(index, src, dst, target):
        return pltpu.make_async_remote_copy(
            src_ref=src,
            dst_ref=dst,
            send_sem=rim_send.at[index],
            recv_sem=rim_recv.at[index],
            device_id=(enc, target),
            device_id_type=MESH,
        )

    top = pl.ds(0, WIN)
    rims = (
        rim_copy(0, own_ref.at[top], rim_ref.at[0], right),
        rim_copy(1, own_ref.at[top], rim_ref.at[1], left),
    )
    ng_rim = rim_copy(2, ng_ref.at[top], ng_rim_ref, right)
    grad_rim = rim_copy(3, pal_grad_ref.at[top], grad_rim_ref, left)

    def slab(ref, e):
        return ref.at[pl.ds(pl.multiple_of(SLAB * e, SLAB), SLAB)]

    def exchange_copy(index, send, recv, peer):
        return pltpu.make_async_remote_copy(
            src_ref=slab(send, peer),
            dst_ref=slab(recv, enc),
            send_sem=slab_send.at[index],
            recv_sem=slab_recv.at[index],
            device_id=(peer, row),
            device_id_type=MESH,
        )

    def near_peers():
        for o in range(n_y // 2 - 1, 0, -1):
            ahead, behind = chip(o), chip(-o)
            for side in (0, 1):
                turned = ahead + (behind - ahead) * (core if side == 0 else 1 - core)
                for k in range(2):
                    yield 2 * turned + k
        yield sibling

    next_chip = chip(1) + (chip(-1) - chip(1)) * core
    last_chip = chip(-1) + (chip(1) - chip(-1)) * core
    far_chip = chip(n_y // 2 - 1) + (chip(n_y // 2 + 1) - chip(n_y // 2 - 1)) * core

    def relay_copy(index, send):
        pair = pl.ds(pl.multiple_of(2 * SLAB * chip(n_y // 2), 2 * SLAB), 2 * SLAB)
        return pltpu.make_async_remote_copy(
            src_ref=send.at[pair],
            dst_ref=(relay1, relay2)[index],
            send_sem=relay_send.at[index],
            recv_sem=relay_recv.at[index],
            device_id=(2 * next_chip + core, row),
            device_id_type=MESH,
        )

    def forward_copy(index, recv, k):
        origin = 2 * last_chip + core
        return pltpu.make_async_remote_copy(
            src_ref=(relay1, relay2)[index].at[pl.ds(SLAB * k, SLAB)],
            dst_ref=slab(recv, origin),
            send_sem=forward_send.at[index],
            recv_sem=slab_recv.at[index],
            device_id=(2 * far_chip + k, row),
            device_id_type=MESH,
        )

    def own_copy(index, send, recv):
        return pltpu.make_async_copy(slab(send, enc), slab(recv, enc), own_sem.at[index])

    def exchange_start(index, send, recv):
        relay_copy(index, send).start()
        for peer in near_peers():
            exchange_copy(index, send, recv, peer).start()
        own_copy(index, send, recv).start()

    def exchange_forward(index, recv):
        relay_copy(index, send1).wait_recv()
        for k in range(2):
            forward_copy(index, recv, k).start()

    def exchange_wait(index, send, recv):
        own_copy(index, send, recv).wait()
        rows_wait(recv.at[pl.ds(0, (n_enc - 1) * SLAB)], slab_recv.at[index])

    def exchange_drain(index, send):
        relay_copy(index, send).wait_send()
        rows_wait(send.at[pl.ds(0, (n_enc - 3) * SLAB)], slab_send.at[index])
        rows_wait((relay1, relay2)[index], forward_send.at[index])

    def rotate():
        fetch_patches.wait()
        turn = iota((ROWS, ROWS), 1) == ((iota((ROWS, ROWS), 0) - edge) & (ROWS - 1))
        turn_ref[...] = one_hot(turn)
        for c in range(0, D, 256):
            part = dot(turn_ref[...], patches_ref[:, c : c + 256])
            own_ref[:, c : c + 256] = part.astype(BF16)
        for copy in rims:
            copy.start()

    n_tile = D // 128

    def grads_wide(q0, q1):
        if q0 == 0:
            fetch_grads.wait()
        for t in range(q0 * n_tile, q1 * n_tile):
            slot_wide[t] = grads_ref[:, 128 * t : 128 * t + 128].astype(F32)

    def grads_move(q):
        for t in range(n_tile):
            at = q * n_tile + t
            for slot in range(4):
                part = slot_wide[at, pl.ds(slot, n_enc, stride=CAP), :]
                slab_wide[t, pl.ds(4 * slot + q, n_enc, stride=SLAB), :] = part
        for p, (off, width) in enumerate(PIECES):
            for t in range(3):
                if t < width // 128:
                    at = (q * D + off) // 128 + t
                    part = slot_wide[at, pl.ds(4, n_enc, stride=CAP), :]
                else:
                    part = jnp.zeros((n_enc, 128), F32)
                slab_wide[n_tile + t, pl.ds(4 * q + p, n_enc, stride=SLAB), :] = part

    def grads_pack(first, last):
        for t in range(first, last):
            send1[:, 128 * t : 128 * t + 128] = slab_wide[t].astype(BF16)
        if last == SLAB_W // 128:
            exchange_start(0, send1, recv1)

    n_tok = ROWS // 4

    def targets(code, patch):
        slot, base = code & 7, (code >> 3) * 16
        quarter = patch & 3
        target_a = jnp.where(slot < 4, base + slot * 4 + quarter, -1)
        target_b = jnp.where(slot == 4, base + quarter * 4, -8)
        return target_a, target_b

    def selector_targets():
        code_row = owner_enc_ref[...] * 8 + owner_slot_ref[...]
        square = iota((n_tok, n_tok), 0) == iota((n_tok, n_tok), 1)
        code_col = jnp.sum(jnp.where(square, code_row, 0), 1, keepdims=True)
        patch = (iota((1, ROWS), 1) - edge) & (ROWS - 1)
        tok = iota((n_tok, ROWS), 0) == (patch >> 2)
        code = jnp.sum(jnp.where(tok, code_col, 0), 0, keepdims=True)
        target_ref[0:1, :], target_ref[1:2, :] = targets(code, patch)

    def selector(p):
        bucket = iota((n_slab_rows, ROWS), 0)
        target = target_ref[0:1, :] if p == 0 else target_ref[1:2, :] + (p - 1)
        sel_ref[p] = one_hot(bucket == target)

    def selectors_back():
        code_row = owner_enc_ref[...] * 8 + owner_slot_ref[...]
        patch = (iota((ROWS, 1), 0) - edge) & (ROWS - 1)
        tok = iota((ROWS, n_tok), 1) == (patch >> 2)
        code = jnp.sum(jnp.where(tok, code_row, 0), 1, keepdims=True)
        target_a, target_b = targets(code, patch)
        bucket = iota((ROWS, n_slab_rows), 1)
        selt_ref[0] = one_hot(bucket == target_a)
        for p in range(4):
            selt_ref[1 + p] = one_hot(bucket == target_b + p)

    def piece(body, *args):
        return lambda: body(*args)

    def masks(r0, count, k0):
        i = iota((count, 128), 0) + r0
        j = iota((count, 128), 1) + k0
        first = jnp.where(row == 0, 0, -1)
        last = jnp.where(row == n_row - 1, ROWS // WIN, -1)
        ends = ((i >> 6) == first) | ((i >> 6) == last)
        i_low = jnp.where((i & (WIN - 1)) < edge, 1, 0)
        j_low = jnp.where((j & (WIN - 1)) < edge, 1, 0)
        apart = jnp.where(ends, i_low ^ j_low, 0)
        same = ((i >> 6) == (j >> 6)) & (apart == 0)
        mask_ref[r0 : r0 + count, :] = jnp.where(same, 1.0, 0.0)

    def zeros():
        acc_ref[...] = jnp.zeros_like(acc_ref)
        dqkv_ref[...] = jnp.zeros_like(dqkv_ref)

    below = iota((WIN, 1), 0) < edge

    def rims_in():
        for copy in rims:
            copy.wait()
        pal_ref[:WIN, :] = jnp.where(below, rim_ref[0], own_ref[:WIN, :])
        pal_ref[WIN:ROWS, :] = own_ref[WIN:, :]
        pal_ref[ROWS:, :] = jnp.where(below, own_ref[:WIN, :], rim_ref[1])

    def in_parts(first, body):
        for k in range(WIN // PART):
            body(pl.ds(pl.multiple_of(first + PART * k, PART), PART))

    def rms_norm(src, dst, gain_ref, first):
        def body(rows):
            wide = src[rows, :].astype(F32)
            inv = lax.rsqrt(jnp.mean(wide * wide, -1, keepdims=True) + EPS)
            dst[rows, :] = (wide * inv * gain_ref[...].reshape(1, D)).astype(BF16)

        in_parts(first, body)

    def rms_back(wide, gain_ref, upstream_in):
        inv = lax.rsqrt(jnp.mean(wide * wide, -1, keepdims=True) + EPS)
        upstream = upstream_in * gain_ref[...].reshape(1, D)
        inner = jnp.mean(upstream * wide, -1, keepdims=True)
        return inv * upstream - wide * (inv * inv * inv) * inner

    def piece(body, *args):
        return lambda: body(*args)

    def project(c0, c1):
        for c in range(c0, c1, 256):
            w = min(256, c1 - c)
            part = dot(hid_ref[...], w_ref[:, c : c + w])
            qkv_ref[:, c : c + w] = part.astype(BF16)

    scale = HEAD_DIM ** (-0.5)
    pairs = range(HEADS // 2)

    def window(t, base=0):
        return slice(base + 128 * t, base + 128 * t + 256)

    def two_heads(t, value):
        lane = iota((1, 256), 1) - 32 * t
        zero = jnp.zeros_like(value)
        first = jnp.where((lane >= 0) & (lane < HEAD_DIM), value, zero)
        second = jnp.where((lane >= HEAD_DIM) & (lane < 2 * HEAD_DIM), value, zero)
        return jnp.concatenate([first, second], 0)

    def attend(t):
        for r0, count, k0 in BLOCKS:
            rows, keys = slice(r0, r0 + count), slice(k0, k0 + 128)
            scores = dot_nt(qkv_ref[rows, window(t)], two_heads(t, qkv_ref[keys, window(t, PROJ)]))
            seen = mask_ref[rows, :] > 0.5
            both = []
            for g in range(2):
                s = jnp.where(seen, scores[:, 128 * g : 128 * g + 128] * scale, -1e30)
                e = jnp.exp(s - jnp.max(s, -1, keepdims=True))
                p = e / jnp.sum(e, -1, keepdims=True)
                if r0 < ROWS:
                    prob_ref[2 * t + g, rows, :] = p
                both.append(p.astype(BF16))
            values = two_heads(t, qkv_ref[keys, window(t, 2 * PROJ)])
            acc_ref[rows, window(t)] += dot(jnp.concatenate(both, 1), values)

    work = [piece(grads_wide, 0, 2), piece(grads_wide, 2, 4)]
    work += [piece(grads_move, q) for q in range(4)]
    work += [piece(grads_pack, 0, SLAB_W // 128)]
    work += [piece(masks, *block) for block in BLOCKS]
    work += [rims_in, selector_targets]
    for k in range(5):
        work += [piece(selector, k), piece(rms_norm, pal_ref, hid_ref, norm_gain_ref, k * WIN)]
    work += [zeros, selectors_back]
    for slot in range(n_slots):
        weights_slot(slot)
        if slot == 0:
            rotate()
        elif work:
            work.pop(0)()
        if slot == 20:
            exchange_forward(0, recv1)
    assert not work
    weights_wait()
    project(0, 3 * PROJ)
    for t in pairs:
        attend(t)

    att_ref[...] = acc_ref[...].astype(BF16)

    @pl.loop(0, D // 256)
    def _(i):
        c = cols(i, 256)
        wo_ref[:, c] = wo_wide[:, c].astype(BF16)
        branch = dot(att_ref[...], wo_ref[:, c])
        resid_ref[:, c] = (pal_ref[:, c].astype(F32) + branch).astype(BF16)

    @pl.loop(0, AL // WIN)
    def _(i):
        rms_norm(resid_ref, normed_ref, merge_gain_ref, i * WIN)

    normed_ref[:WIN, :] = jnp.where(below, normed_ref[ROWS:, :], normed_ref[:WIN, :])

    for c in range(0, D, 256):
        send2[:, c : c + 256] = dot(sel_ref[0], normed_ref[:ROWS, c : c + 256]).astype(BF16)
    head_part = jnp.zeros((n_slab_rows, 256), F32)
    tail_part = jnp.zeros((n_slab_rows, 128), F32)
    for p, (off, width) in enumerate(PIECES):
        head_part += dot(sel_ref[1 + p], normed_ref[:ROWS, off : off + 256])
        if width > 256:
            tail_part += dot(sel_ref[1 + p], normed_ref[:ROWS, off + 256 : off + width])
    send2[:, D : D + 256] = head_part.astype(BF16)
    send2[:, D + 256 :] = tail_part.astype(BF16)
    exchange_start(1, send2, recv2)

    exchange_wait(0, send1, recv1)

    def gradients(rows):
        for p, (off, width) in enumerate(PIECES):
            for c in range(0, width, 256):
                w = min(256, width - c)
                part = dot(selt_ref[0, rows], recv1[:, off + c : off + c + w])
                part += dot(selt_ref[1 + p, rows], recv1[:, D + c : D + c + w])
                ng_ref[rows, off + c : off + c + w] = part.astype(BF16)

    gradients(slice(0, WIN))
    ng_rim.start()
    exchange_forward(1, recv2)
    gradients(slice(WIN, ROWS))

    def merge_back(rows):
        upstream = ng_ref[rows, :].astype(F32)
        grad = rms_back(resid_ref[rows, :].astype(F32), merge_gain_ref, upstream)
        rg_ref[rows, :] = grad
        rgb_ref[rows, :] = grad.astype(BF16)

    @pl.loop(1, ROWS // WIN)
    def _(i):
        in_parts(i * WIN, merge_back)

    ng_rim.wait()
    ng_ref[:WIN, :] = jnp.where(below, ng_rim_ref[...], ng_ref[:WIN, :])
    in_parts(0, merge_back)


    for c0, c1 in ((0, 256), (256, 512), (512, 640)):
        ag_ref[:, c0:c1] = dot_nt(rgb_ref[...], wo_ref[c0:c1, :]).astype(BF16)

    for t in pairs:
        for r0 in (0, 128):
            rows = slice(r0, r0 + 128)
            grad = ag_ref[rows, window(t)]
            values = two_heads(t, qkv_ref[rows, window(t, 2 * PROJ)])
            keys = two_heads(t, qkv_ref[rows, window(t, PROJ)])
            dp = dot_nt(grad, values)
            probs, score_grads = [], []
            for g in range(2):
                p = prob_ref[2 * t + g, rows, :]
                dp_g = dp[:, 128 * g : 128 * g + 128]
                centred = dp_g - jnp.sum(p * dp_g, -1, keepdims=True)
                score_grads.append((p * centred * scale).astype(BF16))
                probs.append(p.astype(BF16))
            dq = dot(jnp.concatenate(score_grads, 1), keys)
            queries = two_heads(t, qkv_ref[rows, window(t)])
            dk = dot_tn(jnp.concatenate(score_grads, 0), queries)
            dv = dot_tn(jnp.concatenate(probs, 0), two_heads(t, grad))
            dqkv_ref[rows, window(t)] += dq
            dqkv_ref[rows, window(t, PROJ)] += dk
            dqkv_ref[rows, window(t, 2 * PROJ)] += dv

    dqkvb_ref[...] = dqkv_ref[...].astype(BF16)

    @pl.loop(0, D // 256)
    def _(i):
        c = cols(i, 256)
        hg_ref[:, c] = dot_nt(dqkvb_ref[...], w_ref[c, :])

    def norm_back(rows):
        grad = rms_back(pal_ref[rows, :].astype(F32), norm_gain_ref, hg_ref[rows, :])
        pal_grad_ref[rows, :] = (rg_ref[rows, :] + grad).astype(BF16)

    in_parts(0, norm_back)
    grad_rim.start()

    @pl.loop(1, ROWS // WIN)
    def _(i):
        in_parts(i * WIN, norm_back)

    exchange_drain(0, send1)
    weights_drain()

    grad_rim.wait()
    own_ref[:WIN, :] = jnp.where(below, grad_rim_ref[...], pal_grad_ref[:WIN, :])
    own_ref[WIN:, :] = pal_grad_ref[WIN:, :]
    for c in range(0, D, 256):
        part = dot_tn(turn_ref[...], own_ref[:, c : c + 256])
        pg_ref[:, c : c + 256] = part.astype(BF16)

    exchange_drain(1, send2)
    exchange_wait(1, send2, recv2)


def place_kernel(n_enc, slabs_ref, grads_ref, llm_ref, pg_ref, wide_ref, llm_wide):
    for t in range(SLAB_W // 128):
        wide_ref[t] = slabs_ref[:, 128 * t : 128 * t + 128].astype(F32)
    for q in range(4):
        for t in range(D // 128):
            at = q * (D // 128) + t
            for slot in range(4):
                part = wide_ref[t, pl.ds(4 * slot + q, n_enc, stride=SLAB), :]
                llm_wide[at, pl.ds(slot, n_enc, stride=CAP), :] = part
        for p, (off, width) in enumerate(PIECES):
            for t in range(width // 128):
                at = (q * D + off) // 128 + t
                part = wide_ref[D // 128 + t, pl.ds(4 * q + p, n_enc, stride=SLAB), :]
                llm_wide[at, pl.ds(4, n_enc, stride=CAP), :] = part
    for t in range(4 * D // 128):
        llm_ref[:, 128 * t : 128 * t + 128] = llm_wide[t].astype(BF16)
    pg_ref[...] = grads_ref[...]


def per_device(
    n_enc,
    n_x,
    n_z,
    patches,
    norm_gain,
    merge_gain,
    qkv_weight,
    out_weight,
    window_phase,
    owner_enc,
    owner_slot,
    llm_grads,
):
    n_row = n_x * n_z
    n_slot = n_enc * CAP
    vmem = pl.BlockSpec(memory_space=pltpu.VMEM)
    smem = pl.BlockSpec(memory_space=pltpu.SMEM)
    anywhere = pl.BlockSpec(memory_space=pl.ANY)
    dma = pltpu.SemaphoreType.DMA
    slabs = pltpu.VMEM((n_enc * SLAB, SLAB_W), BF16)
    slabs_in, grads_in = pl.pallas_call(
        functools.partial(kernel, n_enc, n_x, n_z),
        out_shape=(
            jax.ShapeDtypeStruct((n_enc * SLAB, SLAB_W), BF16),
            jax.ShapeDtypeStruct((ROWS, D), BF16),
        ),
        in_specs=[smem, anywhere] + [vmem] * 6 + [anywhere],
        out_specs=(anywhere, vmem),
        scratch_shapes=[
            pltpu.VMEM((ROWS, D), BF16),
            pltpu.VMEM((n_slot, 4 * D), BF16),
            *(pltpu.VMEM((n_row, 2 * SHARD, width), BF16) for width in FLOWS),
            pltpu.VMEM((D, 3 * PROJ), BF16),
            pltpu.VMEM((PROJ, D), BF16),
            pltpu.VMEM((PROJ, D), F32),
            pltpu.VMEM((ROWS, ROWS), BF16),
            pltpu.VMEM((ROWS, D), BF16),
            pltpu.VMEM((2, WIN, D), BF16),
            pltpu.VMEM((AL, D), BF16),
            pltpu.VMEM((AL, D), BF16),
            pltpu.VMEM((AL, 3 * PROJ), BF16),
            pltpu.VMEM((HEADS, ROWS, 128), F32),
            pltpu.VMEM((AL, 128), F32),
            pltpu.VMEM((AL, PROJ), F32),
            pltpu.VMEM((AL, PROJ), BF16),
            pltpu.VMEM((AL, D), BF16),
            pltpu.VMEM((AL, D), BF16),
            pltpu.VMEM((ROWS, D), BF16),
            pltpu.VMEM((WIN, D), BF16),
            pltpu.VMEM((ROWS, D), F32),
            pltpu.VMEM((ROWS, D), BF16),
            pltpu.VMEM((ROWS, PROJ), BF16),
            pltpu.VMEM((ROWS, 3 * PROJ), F32),
            pltpu.VMEM((ROWS, 3 * PROJ), BF16),
            pltpu.VMEM((ROWS, D), F32),
            pltpu.VMEM((ROWS, D), BF16),
            pltpu.VMEM((WIN, D), BF16),
            pltpu.VMEM((5, n_enc * SLAB, ROWS), BF16),
            pltpu.VMEM((5, ROWS, n_enc * SLAB), BF16),
            pltpu.VMEM((8, ROWS), jnp.int32),
            pltpu.VMEM((4 * D // 128, n_slot, 128), F32),
            pltpu.VMEM((SLAB_W // 128, n_enc * SLAB, 128), F32),
            slabs,
            slabs,
            slabs,
            pltpu.VMEM((2 * SLAB, SLAB_W), BF16),
            pltpu.VMEM((2 * SLAB, SLAB_W), BF16),
            dma((3,)),
            dma((n_row,)),
            dma((2,)),
            dma((2,)),
            dma((2,)),
            dma((4,)),
            dma((4,)),
            dma((2,)),
            dma((2,)),
            dma((2,)),
            dma((2,)),
            dma((2,)),
        ],
        compiler_params=pltpu.CompilerParams(
            collective_id=0, has_side_effects=True, vmem_limit_bytes=56 * 1024 * 1024
        ),
        cost_estimate=pl.CostEstimate(flops=8_000_000_000, bytes_accessed=4_000_000, transcendentals=400000),
    )(
        window_phase,
        patches,
        norm_gain,
        merge_gain,
        qkv_weight,
        out_weight,
        owner_enc.reshape(1, -1),
        owner_slot.reshape(1, -1),
        llm_grads,
    )
    return pl.pallas_call(
        functools.partial(place_kernel, n_enc),
        out_shape=(
            jax.ShapeDtypeStruct((n_slot, 4 * D), BF16),
            jax.ShapeDtypeStruct((ROWS, D), BF16),
        ),
        in_specs=[vmem, vmem],
        out_specs=(vmem, vmem),
        scratch_shapes=[
            pltpu.VMEM((SLAB_W // 128, n_enc * SLAB, 128), F32),
            pltpu.VMEM((4 * D // 128, n_slot, 128), F32),
        ],
        compiler_params=pltpu.CompilerParams(vmem_limit_bytes=60 * 1024 * 1024),
        cost_estimate=pl.CostEstimate(
            flops=1_000_000, bytes_accessed=3_200_000, transcendentals=0
        ),
    )(slabs_in, grads_in)


def solution(mesh):
    n_enc, n_row = mesh.shape["enc"], mesh.shape["row"]
    n_x = 4
    in_specs = (
        P(("enc", "row"), None),
        P(),
        P(),
        P("row", None),
        P("row", None),
        P(),
        P(("enc", "row")),
        P(("enc", "row")),
        P(("enc", "row"), None),
    )
    out_specs = (P(("enc", "row"), None), P(("enc", "row"), None))
    return jax.shard_map(
        functools.partial(per_device, n_enc, n_x, n_row // n_x),
        mesh=mesh,
        in_specs=in_specs,
        out_specs=out_specs,
        check_vma=False,
    )
```
